128 devices in a mesh: seq: 32 (over y, z, core), section: 4 (over x).
Axes of the slice: x: 4, y: 4, z: 4, core: 2. Of those that a mesh axis runs over, the one named last changes fastest.
Arguments:
- tokens: bfloat16 [16384, 1280], P('seq'), may hold values from -6 to 6
- norm_gain: bfloat16 [1280], replicated, may hold values from 0.25 to 1.75
- w_qkv: bfloat16 [3, 1280, 1280], P(None, None, 'section')
- w_out: bfloat16 [1280, 1280], P('section'), may hold values from -0.15625 to 0.15625
- merge_gain: bfloat16 [1280], replicated, may hold values from 0.25 to 1.75
- seg_blocks: int32 [32], replicated, may hold values from 1 to 16, 256 in all
- mb_sizes: int32 [32], replicated, may hold values from 1 to 256, 4096 in all
- mb_receiver: int32 [32], replicated, may hold values from 0 to 31, each once
- merged_grad: bfloat16 [4096, 5120], P('seq'), may hold values from -6 to 6
Outputs:
- delivered: bfloat16 [8192, 5120], P('seq', 'section')
- grad_x: bfloat16 [16384, 1280], P('seq')
- grad_w_qkv: float32 [3, 1280, 1280], P(None, 'seq', 'section')
- grad_w_out: float32 [1280, 1280], P('section', 'seq')
The draws below stay inside these ranges and needn't reach their ends.
Inputs may be any that keep to these rules, and one draw needn't show every extreme that they name: `seg_blocks`: images lie whole in the pack and sum to 16384 patches; the longest has exactly 1024 patches. `mb_sizes`: Micro-batches cover the 4096 merged rows in order; the largest has exactly 256 rows. `mb_receiver`: each receiver gets exactly one micro-batch.
All inputs are finite; a program needn't handle non-finite values.
Results may differ from the reference program's by a relative error of at most 0.022.
Values may be sent and summed in bfloat16 or wider, within the bound.
A program may use at most 192 MiB of HBM per device.

```python
import math
import jax
import jax.numpy as jnp
import numpy as np
from jax import lax

D = 1280
HEADS = 16
TOK_DEV = 512
TOKENS = 16384
MERGED = 4096
CAP = 256
NSEG = 32
N_BATCH = 32
N_SEQ = 32


def draw_w_qkv(key, part):
    key = jax.random.fold_in(key, 11)
    spread = 1.0 / math.sqrt(D)
    weights = jax.random.normal(key, (3, D, D), jnp.float32) * spread
    return weights.astype(jnp.bfloat16)


def levels(stream_key, shape, pieces, low, high):
    loudness, own = 1.0, jax.random.fold_in(stream_key, 6)
    for position, shards_of in pieces:
        steps = jnp.exp(jax.random.uniform(jax.random.fold_in(own, position), (shards_of,), jnp.float32, low / len(pieces), high / len(pieces)))
        loudness = loudness * jnp.repeat(steps, shape[position] // shards_of).reshape([-1 if axis == position else 1 for axis in range(len(shape))])
    return loudness


def profile(amount, total, reach, lean):
    portions = [(1 << 20) // math.isqrt(standing ** lean) + 1 for standing in range(2, amount + 1)]
    spare, counts = total - reach - (amount - 1), [1] * (amount - 1)
    while spare > 0:
        candidates = [i for i in range(amount - 1) if counts[i] < reach]
        mass, budget = sum([portions[i] for i in candidates]), spare
        for i in candidates:
            addition = min(reach - counts[i], max(1, budget * portions[i] // mass), spare)
            counts[i] = counts[i] + addition
            spare = spare - addition
    return np.array([reach] + counts)


def uneven_parts(key, amount, total, limit, slope):
    if amount == 2:
        one = jax.random.randint(key, (), max(1, total - limit), min(limit, total - 1) + 1)
        return jnp.stack([one, total - one])
    sizes = jnp.asarray(profile(amount, total, limit, slope), jnp.int32)
    couples = (amount - 1) // 2
    donor, receiver = sizes[1:1 + 2 * couples:2], sizes[2:2 + 2 * couples:2]
    slack = jnp.minimum(donor - 1, limit - receiver)
    shifted = jax.random.randint(jax.random.fold_in(key, 1), (couples,), 0, 1 << 20) % (slack + 1)
    sizes = sizes.at[1:1 + 2 * couples:2].set(donor - shifted).at[2:2 + 2 * couples:2].set(receiver + shifted)
    return sizes[jax.random.permutation(jax.random.fold_in(key, 2), amount)]


def gaussian(own_key, extent, deviation, limit, split=(), held_as=jnp.bfloat16):
    level = levels(own_key, extent, split, -0.22, 0.18) if split else 1.0
    values = jax.random.normal(own_key, extent, jnp.float32) * deviation * level
    return jnp.minimum(jnp.maximum(values, -limit), limit).astype(held_as)


def setup_inputs(seed: int = 0) -> dict:
    key_list = jax.random.split(jax.random.key(seed), 10)
    tokens = gaussian(key_list[0], (TOKENS, D), 1.0, 6.0, ((0, 32),))
    norm_gain = jnp.clip(1.0 + 0.15 * jax.random.normal(key_list[1], (D,), jnp.float32), 0.25, 1.75).astype(jnp.bfloat16)
    w_qkv = draw_w_qkv(jax.random.fold_in(key_list[9], 71), 0)
    w_out = gaussian(key_list[3], (D, D), D ** -0.5, 0.15625, ((0, 4),))
    merge_gain = jnp.clip(1.0 + 0.15 * jax.random.normal(key_list[4], (D,), jnp.float32), 0.25, 1.75).astype(jnp.bfloat16)
    seg_blocks = uneven_parts(key_list[5], NSEG, TOKENS // 64, TOK_DEV // 32, 1).astype(jnp.int32)
    mb_sizes = uneven_parts(key_list[6], N_BATCH, MERGED, CAP, 1).astype(jnp.int32)
    mb_receiver = jax.random.permutation(key_list[7], N_SEQ).astype(jnp.int32)
    merged_grad = gaussian(key_list[8], (MERGED, 4 * D), 1.0, 6.0, ((0, 32),))
    return {"tokens": tokens, "norm_gain": norm_gain, "w_qkv": w_qkv, "w_out": w_out, "merge_gain": merge_gain, "seg_blocks": seg_blocks, "mb_sizes": mb_sizes, "mb_receiver": mb_receiver, "merged_grad": merged_grad}


EPS = 1e-06

def norm_forward(values, scale_gain):
    average = lax.optimization_barrier(jnp.mean(values, axis=-1, keepdims=True))
    centered = values - average
    inv_scale = lax.rsqrt(lax.optimization_barrier(jnp.mean(centered * centered, axis=-1, keepdims=True)) + EPS)
    unit_rows = centered * inv_scale
    return (unit_rows * scale_gain.astype(jnp.float32), unit_rows, inv_scale)

def norm_backward(incoming, scale_gain, unit_rows, inv_scale):
    scaled = incoming * scale_gain.astype(jnp.float32)
    return inv_scale * (scaled - lax.optimization_barrier(jnp.mean(scaled, axis=-1, keepdims=True)) - unit_rows * lax.optimization_barrier(jnp.mean(scaled * unit_rows, axis=-1, keepdims=True)))

def reference(tokens, norm_gain, w_qkv, w_out, merge_gain, seg_blocks, mb_sizes, mb_receiver, merged_grad):
    head_dim = D // HEADS
    factor = head_dim ** (-0.5)
    inputs32 = tokens.astype(jnp.float32)
    normed_f, unit_one, inv_one = norm_forward(inputs32, norm_gain)
    normed = normed_f.astype(jnp.bfloat16)
    query = jnp.dot(normed, w_qkv[0], preferred_element_type=jnp.float32).astype(jnp.bfloat16)
    key_all = jnp.dot(normed, w_qkv[1], preferred_element_type=jnp.float32).astype(jnp.bfloat16)
    value_all = jnp.dot(normed, w_qkv[2], preferred_element_type=jnp.float32).astype(jnp.bfloat16)
    image_ends = (64 * jnp.cumsum(seg_blocks)).astype(jnp.int32)
    positions = jnp.arange(TOKENS, dtype=jnp.int32)
    segment = lax.optimization_barrier(jnp.sum((positions[:, None] >= image_ends[None, :]).astype(jnp.int32), axis=1)).astype(jnp.int32)
    margin = 2 * TOK_DEV
    span_len = 5 * TOK_DEV
    key_pad = jnp.pad(key_all, ((margin, margin), (0, 0)))
    value_pad = jnp.pad(value_all, ((margin, margin), (0, 0)))
    seg_pad = jnp.pad(segment, (margin, margin), constant_values=-1)
    query_blocks = query.reshape(N_SEQ, TOK_DEV, HEADS, head_dim)
    query_segments = segment.reshape(N_SEQ, TOK_DEV)
    block_ids = jnp.arange(N_SEQ, dtype=jnp.int32)

    def key_window(block_id):
        first_row = (block_id * TOK_DEV).astype(jnp.int32)
        key_win = lax.dynamic_slice_in_dim(key_pad, first_row, span_len, 0).reshape(span_len, HEADS, head_dim).astype(jnp.float32)
        value_win = lax.dynamic_slice_in_dim(value_pad, first_row, span_len, 0).reshape(span_len, HEADS, head_dim).astype(jnp.float32)
        seg_win = lax.dynamic_slice_in_dim(seg_pad, first_row, span_len, 0)
        return (key_win, value_win, seg_win)

    def forward_block(inputs):
        query_b, seg_b, block_id = inputs
        key_win, value_win, seg_win = key_window(block_id)
        scores = jnp.einsum('qhd,khd->hqk', query_b.astype(jnp.float32), key_win) * factor
        allowed = (seg_b[:, None] == seg_win[None, :])[None]
        highest = lax.optimization_barrier(jnp.max(jnp.where(allowed, scores, -jnp.inf), axis=2))
        totals = lax.optimization_barrier(jnp.sum(jnp.where(allowed, jnp.exp(scores - highest[:, :, None]), 0.0), axis=2))
        log_total = highest + jnp.log(totals)
        weights = jnp.where(allowed, jnp.exp(scores - log_total[:, :, None]), 0.0).astype(jnp.bfloat16)
        attended_b = jnp.einsum('hqk,khd->qhd', weights.astype(jnp.float32), value_win).astype(jnp.bfloat16)
        return (attended_b, log_total)
    attended_h, log_totals = lax.map(forward_block, (query_blocks, query_segments, block_ids))
    attended = attended_h.reshape(TOKENS, D)
    layer_out = inputs32 + jnp.dot(attended, w_out, preferred_element_type=jnp.float32)
    normed_two, unit_two, inv_two = norm_forward(layer_out, merge_gain)
    merged = normed_two.astype(jnp.bfloat16).reshape(MERGED, 4 * D)
    starts = (jnp.cumsum(mb_sizes) - mb_sizes).astype(jnp.int32)
    receivers = jnp.arange(N_SEQ, dtype=jnp.int32)
    batch_ids = jnp.arange(N_BATCH, dtype=jnp.int32)
    picked = lax.optimization_barrier(jnp.sum(jnp.where(mb_receiver[None, :] == receivers[:, None], batch_ids[None, :], 0), axis=1)).astype(jnp.int32)
    first_rows = starts[picked]
    live_rows = mb_sizes[picked]
    slot_ids = jnp.arange(CAP, dtype=jnp.int32)
    row_index = jnp.minimum(first_rows[:, None] + slot_ids[None, :], MERGED - 1).astype(jnp.int32)
    taken = jnp.take(merged, row_index.reshape(-1), axis=0).reshape(N_SEQ, CAP, 4 * D)
    delivered = jnp.where((slot_ids[None, :] < live_rows[:, None])[:, :, None], taken, jnp.zeros_like(taken)).reshape(N_SEQ * CAP, 4 * D)
    grad_incoming = merged_grad.reshape(TOKENS, D).astype(jnp.float32)
    grad_layer = norm_backward(grad_incoming, merge_gain, unit_two, inv_two).astype(jnp.bfloat16)
    grad_att = jnp.dot(grad_layer, w_out.T, preferred_element_type=jnp.float32).astype(jnp.bfloat16)
    grad_w_out = jnp.dot(attended.T, grad_layer, preferred_element_type=jnp.float32)
    row_delta = lax.optimization_barrier(jnp.sum(grad_att.astype(jnp.float32).reshape(TOKENS, HEADS, head_dim) * attended.astype(jnp.float32).reshape(TOKENS, HEADS, head_dim), axis=2))
    delta_blocks = row_delta.reshape(N_SEQ, TOK_DEV, HEADS).transpose(0, 2, 1)
    grad_blocks = grad_att.reshape(N_SEQ, TOK_DEV, HEADS, head_dim)

    def backward_block(carry, inputs):
        key_acc, value_acc = carry
        query_b, seg_b, block_id, log_total, delta_b, grad_b = inputs
        key_win, value_win, seg_win = key_window(block_id)
        query_f = query_b.astype(jnp.float32)
        grad_f = grad_b.astype(jnp.float32)
        scores = jnp.einsum('qhd,khd->hqk', query_f, key_win) * factor
        allowed = (seg_b[:, None] == seg_win[None, :])[None]
        probs = jnp.where(allowed, jnp.exp(scores - log_total[:, :, None]), 0.0)
        weights = probs.astype(jnp.bfloat16)
        grad_probs = jnp.einsum('qhd,khd->hqk', grad_f, value_win)
        grad_scores = (probs * (grad_probs - delta_b[:, :, None])).astype(jnp.bfloat16).astype(jnp.float32)
        grad_query_b = (jnp.einsum('hqk,khd->qhd', grad_scores, key_win) * factor).astype(jnp.bfloat16)
        key_part = jnp.einsum('hqk,qhd->khd', grad_scores, query_f)
        value_part = jnp.einsum('hqk,qhd->khd', weights.astype(jnp.float32), grad_f)
        first_row = (block_id * TOK_DEV).astype(jnp.int32)
        key_acc = lax.dynamic_update_slice_in_dim(key_acc, lax.dynamic_slice_in_dim(key_acc, first_row, span_len, 0) + key_part, first_row, 0)
        value_acc = lax.dynamic_update_slice_in_dim(value_acc, lax.dynamic_slice_in_dim(value_acc, first_row, span_len, 0) + value_part, first_row, 0)
        return ((key_acc, value_acc), grad_query_b)
    empty_acc = jnp.zeros((TOKENS + 4 * TOK_DEV, HEADS, head_dim), jnp.float32)
    (key_acc, value_acc), grad_query_h = lax.scan(backward_block, (empty_acc, empty_acc), (query_blocks, query_segments, block_ids, log_totals, delta_blocks, grad_blocks))
    grad_query = grad_query_h.reshape(TOKENS, D)
    grad_key = (key_acc[margin:margin + TOKENS] * factor).reshape(TOKENS, D).astype(jnp.bfloat16)
    grad_value = value_acc[margin:margin + TOKENS].reshape(TOKENS, D).astype(jnp.bfloat16)
    grad_w_qkv = jnp.stack([jnp.dot(normed.T, grad_query, preferred_element_type=jnp.float32), jnp.dot(normed.T, grad_key, preferred_element_type=jnp.float32), jnp.dot(normed.T, grad_value, preferred_element_type=jnp.float32)])
    grad_normed = jnp.dot(grad_query, w_qkv[0].T, preferred_element_type=jnp.float32) + jnp.dot(grad_key, w_qkv[1].T, preferred_element_type=jnp.float32) + jnp.dot(grad_value, w_qkv[2].T, preferred_element_type=jnp.float32)
    grad_x = (grad_layer.astype(jnp.float32) + norm_backward(grad_normed, norm_gain, unit_one, inv_one)).astype(jnp.bfloat16)
    return (delivered, grad_x, grad_w_qkv, grad_w_out)
```

```python
import math

import jax
import jax.numpy as jnp
from jax import lax
from jax.experimental import pallas as pl
from jax.experimental.pallas import tpu as pltpu
from jax.sharding import PartitionSpec as P

HEADS = 16
EPS = 1e-06
HEAD_DIM = 80
PAIR = 160
BIG = -1e30
CHUNK = 256
BF16 = jnp.bfloat16
F32 = jnp.float32
MESH = pl.DeviceIdType.MESH
FACTOR = HEAD_DIM ** -0.5
LOG2E = 1.0 / math.log(2.0)
LN2 = math.log(2.0)


def dot_nn(left, right):
    return lax.dot_general(left, right, (((1,), (0,)), ((), ())), preferred_element_type=F32)


def dot_nt(left, right):
    return lax.dot_general(left, right, (((1,), (1,)), ((), ())), preferred_element_type=F32)


def place():
    section = lax.axis_index("section")
    seq = lax.axis_index("seq")
    return section, seq // 2, seq % 2


def shape(dims, dtype=BF16):
    return jax.ShapeDtypeStruct(dims, dtype)


def local_call(body, outs, ins, scratch=(), smem=0, limit=48):
    vmem = pl.BlockSpec(memory_space=pltpu.VMEM)
    scalar = pl.BlockSpec(memory_space=pltpu.SMEM)
    return pl.pallas_call(
        body,
        out_shape=outs,
        in_specs=[scalar] * smem + [vmem] * (len(ins) - smem),
        out_specs=[vmem] * len(outs),
        scratch_shapes=list(scratch),
        compiler_params=pltpu.CompilerParams(vmem_limit_bytes=limit << 20),
    )(*ins)


def exchange(number, outs, ins, peers, plan):
    with_peers = peers(*(0, 0, 0))
    count = len(with_peers)

    def body(*refs):
        in_refs, out_refs = refs[: len(ins)], refs[len(ins) : len(ins) + len(outs)]
        send_sems, recv_sems = refs[len(ins) + len(outs) :]
        spot = place()
        barrier = pltpu.get_barrier_semaphore()
        for peer in peers(*spot):
            pl.semaphore_signal(barrier, inc=1, device_id=peer, device_id_type=MESH)
        pl.semaphore_wait(barrier, count)
        copies = []
        for index, (source, target, device) in enumerate(plan(*spot, in_refs, out_refs)):
            if device is None:
                copy = pltpu.make_async_copy(source, target, recv_sems.at[index])
            else:
                copy = pltpu.make_async_remote_copy(
                    src_ref=source,
                    dst_ref=target,
                    send_sem=send_sems.at[index],
                    recv_sem=recv_sems.at[index],
                    device_id=device,
                    device_id_type=MESH,
                )
            copy.start()
            copies.append(copy)
        for copy in copies:
            copy.wait()

    return pl.pallas_call(
        body,
        out_shape=outs,
        in_specs=[pl.BlockSpec(memory_space=pl.ANY)] * len(ins),
        out_specs=[pl.BlockSpec(memory_space=pl.ANY)] * len(outs),
        scratch_shapes=[pltpu.SemaphoreType.DMA((20,)), pltpu.SemaphoreType.DMA((20,))],
        compiler_params=pltpu.CompilerParams(collective_id=number, has_side_effects=True),
    )(*ins)


def dev(chip, core, section):
    return (chip * 2 + core, section)


def around(chip, step):
    return (chip + step + 16) % 16


def project_body(tokens_ref, gain_ref, w_ref, qkv_ref, normed_t_ref, normed_ref):
    gain = gain_ref[...].astype(F32)
    for tile in range(4):
        rows = pl.ds(tile * 128, 128)
        values = tokens_ref[rows, :].astype(F32)
        centered = values - jnp.mean(values, axis=1, keepdims=True)
        inv = lax.rsqrt(jnp.mean(centered * centered, axis=1, keepdims=True) + EPS)
        normed = (centered * inv * gain).astype(BF16)
        normed_ref[rows, :] = normed
        normed_t_ref[:, rows] = normed.T
    for which in range(3):
        out = dot_nn(normed_ref[...], w_ref[which])
        if which == 0:
            out = out * (FACTOR * LOG2E)
        qkv_ref[which] = out.T.astype(BF16)


def membership(ends_ref, first, count):
    spots = first + lax.broadcasted_iota(jnp.int32, (32, count), 1)
    return (spots >= ends_ref[:, 0:1]) & (spots < ends_ref[:, 1:2])


def three_parts(row):
    high = row.astype(BF16)
    rest = row - high.astype(F32)
    middle = rest.astype(BF16)
    low = (rest - middle.astype(F32)).astype(BF16)
    return jnp.concatenate([high, middle, low, jnp.zeros((13, row.shape[1]), BF16)], axis=0)


def permutation(transposed):
    natural = lax.broadcasted_iota(jnp.int32, (512, 512), 1 if transposed else 0)
    moved = lax.broadcasted_iota(jnp.int32, (512, 512), 0 if transposed else 1)
    return jnp.where(natural == 4 * (moved % 128) + moved // 128, 1.0, 0.0).astype(BF16)


def forward_body(bounds_ref, ends_ref, q_ref, kv_ref, o_ref, op_ref, log_ref, qrow, kx, scores):
    chip = lax.axis_index("seq") // 2
    first = chip * 1024
    for head in range(2):
        feats = pl.ds(head * HEAD_DIM, HEAD_DIM)
        for block in range(4):
            lanes = pl.ds(block * 256, 256)
            inside = membership(ends_ref, first + block * 256, 256)
            joined = jnp.concatenate(
                [
                    q_ref[feats, lanes],
                    jnp.where(inside, 0.0, BIG).astype(BF16),
                    jnp.zeros((16, 256), BF16),
                ],
                axis=0,
            )
            qrow[head, lanes, :] = joined.T

    def build(chunk, carry):
        lanes = pl.ds(pl.multiple_of(chunk * CHUNK, CHUNK), CHUNK)
        inside = membership(ends_ref, first - 1024 + chunk * CHUNK, CHUNK)
        hot = jnp.where(inside, 1.0, 0.0).astype(BF16)
        for head in range(2):
            kx[head, 0:80, lanes] = kv_ref[0, pl.ds(head * HEAD_DIM, HEAD_DIM), lanes]
            kx[head, 80:112, lanes] = hot
            kx[head, 112:128, lanes] = jnp.zeros((16, CHUNK), BF16)
        return carry

    lax.fori_loop(bounds_ref[0, 0], bounds_ref[3, 1], build, 0)

    def tile_step(tile, carry):
        low, high = bounds_ref[tile, 0], bounds_ref[tile, 1]
        rows = pl.ds(pl.multiple_of(tile * 256, 256), 256)
        for head in range(2):
            feats = pl.ds(head * HEAD_DIM, HEAD_DIM)
            queries = qrow[head, rows, :]

            def score_step(chunk, top):
                lanes = pl.ds(pl.multiple_of(chunk * CHUNK, CHUNK), CHUNK)
                part = dot_nn(queries, kx[head, :, lanes])
                scores[:, lanes] = part
                return jnp.maximum(top, jnp.maximum(part[:, :128], part[:, 128:]))

            top = lax.fori_loop(low, high, score_step, jnp.full((256, 128), BIG, F32))
            top_col = jnp.max(top, axis=1, keepdims=True)
            top_row = jnp.max(top.T, axis=0, keepdims=True)

            def sum_step(chunk, carry):
                total, out = carry
                lanes = pl.ds(pl.multiple_of(chunk * CHUNK, CHUNK), CHUNK)
                probs = jnp.exp2(scores[:, lanes] - top_col)
                out = out + dot_nt(kv_ref[1, feats, lanes], probs.astype(BF16))
                return total + (probs[:, :128] + probs[:, 128:]), out

            total, out = lax.fori_loop(
                low,
                high,
                sum_step,
                (jnp.zeros((256, 128), F32), jnp.zeros((HEAD_DIM, 256), F32)),
            )
            total_row = jnp.sum(total.T, axis=0, keepdims=True)
            o_ref[feats, rows] = (out * (1.0 / total_row)).astype(BF16)
            log_ref[head : head + 1, rows] = top_row + jnp.log(total_row) * LOG2E
        return carry

    lax.fori_loop(0, 4, tile_step, 0)
    perm = permutation(False)
    for half in range(2):
        moved = dot_nn(o_ref[:, half * 512 : half * 512 + 512], perm).astype(BF16)
        for part in range(4):
            op_ref[half, part] = moved[:, part * 128 : part * 128 + 128]


def backward_body(
    bounds_ref, ends_ref, q_ref, kv_ref, o_ref, log_ref, gp_ref, dq_ref, dkv_ref,
    qrow, kx, vx, grow, gnat, acc,
):
    chip = lax.axis_index("seq") // 2
    first = chip * 1024
    back = permutation(True)
    for half in range(2):
        joined = jnp.concatenate([gp_ref[half, part] for part in range(4)], axis=1)
        gnat[:, half * 512 : half * 512 + 512] = dot_nn(joined, back).astype(BF16)
    for head in range(2):
        feats = pl.ds(head * HEAD_DIM, HEAD_DIM)
        for block in range(4):
            lanes = pl.ds(block * 256, 256)
            inside = membership(ends_ref, first + block * 256, 256)
            joined = jnp.concatenate(
                [
                    q_ref[feats, lanes],
                    jnp.where(inside, 0.0, BIG).astype(BF16),
                    three_parts(-log_ref[head : head + 1, lanes]),
                ],
                axis=0,
            )
            qrow[head, lanes, :] = joined.T
            grads = gnat[feats, lanes]
            delta = jnp.sum(
                grads.astype(F32) * o_ref[feats, lanes].astype(F32), axis=0, keepdims=True
            )
            joined = jnp.concatenate(
                [grads, three_parts(-delta), jnp.zeros((32, 256), BF16)], axis=0
            )
            grow[head, lanes, :] = joined.T

    ones = jnp.where(lax.broadcasted_iota(jnp.int32, (16, CHUNK), 0) < 3, 1.0, 0.0).astype(BF16)

    def build(chunk, carry):
        lanes = pl.ds(pl.multiple_of(chunk * CHUNK, CHUNK), CHUNK)
        inside = membership(ends_ref, first - 1024 + chunk * CHUNK, CHUNK)
        hot = jnp.where(inside, 1.0, 0.0).astype(BF16)
        for head in range(2):
            feats = pl.ds(head * HEAD_DIM, HEAD_DIM)
            kx[head, 0:80, lanes] = kv_ref[0, feats, lanes]
            kx[head, 80:112, lanes] = hot
            kx[head, 112:128, lanes] = ones
            vx[head, 0:80, lanes] = kv_ref[1, feats, lanes]
            vx[head, 80:96, lanes] = ones
            vx[head, 96:128, lanes] = jnp.zeros((32, CHUNK), BF16)
        return carry

    lax.fori_loop(bounds_ref[0, 0], bounds_ref[3, 1], build, 0)
    acc[...] = jnp.zeros_like(acc)

    def tile_step(tile, carry):
        low, high = bounds_ref[tile, 0], bounds_ref[tile, 1]
        rows = pl.ds(pl.multiple_of(tile * 256, 256), 256)
        for head in range(2):
            feats = pl.ds(head * HEAD_DIM, HEAD_DIM)
            queries, grads = qrow[head, rows, :], grow[head, rows, :]
            queries_t, grads_t = q_ref[feats, rows], gnat[feats, rows]

            def step(chunk, dq):
                lanes = pl.ds(pl.multiple_of(chunk * CHUNK, CHUNK), CHUNK)
                probs = jnp.exp2(dot_nn(queries, kx[head, :, lanes]))
                shifted = dot_nn(grads, vx[head, :, lanes])
                dscores = (probs * shifted).astype(BF16)
                acc[0, feats, lanes] += dot_nn(queries_t, dscores)
                acc[1, feats, lanes] += dot_nn(grads_t, probs.astype(BF16))
                return dq + dot_nt(kv_ref[0, feats, lanes], dscores)

            dq = lax.fori_loop(low, high, step, jnp.zeros((HEAD_DIM, 256), F32))
            dq_ref[feats, rows] = (dq * FACTOR).astype(BF16)
        return carry

    lax.fori_loop(0, 4, tile_step, 0)
    dkv_ref[0] = (acc[0] * LN2).astype(BF16)
    dkv_ref[1] = acc[1].astype(BF16)


def middle_body(
    att_ref, w_ref, tokens_ref, mgrad_ref, gain_ref, merged_ref, gl_ref, glt_ref, gat_ref
):
    section = lax.axis_index("section")
    row = lax.broadcasted_iota(jnp.int32, (128, 512), 0)
    column = lax.broadcasted_iota(jnp.int32, (128, 512), 1)
    chosen = jnp.where(column == 4 * row + section, 1.0, 0.0).astype(BF16)
    attended = att_ref[...].T
    layer = dot_nn(chosen, tokens_ref[...]) + dot_nn(attended, w_ref[...])
    gain = gain_ref[...].astype(F32)
    centered = layer - jnp.mean(layer, axis=1, keepdims=True)
    inv = lax.rsqrt(jnp.mean(centered * centered, axis=1, keepdims=True) + EPS)
    unit = centered * inv
    merged = (unit * gain).astype(BF16)
    row = lax.broadcasted_iota(jnp.int32, (128, 128), 0)
    column = lax.broadcasted_iota(jnp.int32, (128, 128), 1)
    order = jnp.where(column == 32 * (row % 4) + row // 4, 1.0, 0.0).astype(BF16)
    merged_ref[...] = dot_nn(order, merged).astype(BF16)
    scaled = mgrad_ref[...].astype(F32) * gain
    grad_layer = inv * (
        scaled
        - jnp.mean(scaled, axis=1, keepdims=True)
        - unit * jnp.mean(scaled * unit, axis=1, keepdims=True)
    )
    grad_layer = grad_layer.astype(BF16)
    gl_ref[...] = grad_layer
    glt_ref[...] = grad_layer.T
    gat_ref[...] = dot_nt(w_ref[...], grad_layer).astype(BF16)


def gradients_body(dq_ref, dkv_ref, w_ref, normed_t_ref, glt_ref, att_ref, gn_ref, p_ref, dj, djp, att, glt):
    for head in range(2):
        rows = pl.ds(head * PAIR, PAIR)
        dj[rows, :] = dq_ref[head]
        for which in range(2):
            total = dkv_ref[0, head, which].astype(F32) + dkv_ref[1, head, which].astype(F32)
            total = total + dkv_ref[2, head, which].astype(F32)
            dj[pl.ds(320 * (which + 1) + head * PAIR, PAIR), :] = total.astype(BF16)
        for part in range(4):
            att[rows, part * 128 : part * 128 + 128] = att_ref[head, part]
    for part in range(4):
        glt[:, part * 128 : part * 128 + 128] = glt_ref[part]
    djp[...] = dot_nn(dj[...], permutation(False)).astype(BF16)

    def step(index, carry):
        rows = pl.ds(pl.multiple_of(index * 256, 256), 256)
        total = dot_nn(w_ref[0, rows, :], djp[0:320, :])
        total = total + dot_nn(w_ref[1, rows, :], djp[320:640, :])
        total = total + dot_nn(w_ref[2, rows, :], djp[640:960, :])
        total = total.astype(BF16)
        for part in range(4):
            gn_ref[part, rows, :] = total[:, part * 128 : part * 128 + 128]
        normed = normed_t_ref[rows, :]
        p_ref[0, rows, :] = dot_nt(normed, dj[0:640, :]).astype(BF16)
        right = jnp.concatenate(
            [dot_nt(normed, dj[640:960, :]), dot_nt(glt[rows, :], att[...])], axis=1
        )
        p_ref[1, rows, :] = right.astype(BF16)
        return carry

    lax.fori_loop(0, 5, step, 0)


def first_norm_body(gn_ref, got_ref, tokens_ref, gain_ref, gl_ref, own_ref, other_ref, gx_ref, sum_ref):
    section = lax.axis_index("section")
    core = lax.axis_index("seq") % 2
    row = lax.broadcasted_iota(jnp.int32, (128, 512), 0)
    column = lax.broadcasted_iota(jnp.int32, (128, 512), 1)
    chosen = jnp.where(column == 4 * row + section, 1.0, 0.0).astype(BF16)
    values = dot_nn(chosen, tokens_ref[...])
    centered = values - jnp.mean(values, axis=1, keepdims=True)
    inv = lax.rsqrt(jnp.mean(centered * centered, axis=1, keepdims=True) + EPS)
    unit = centered * inv
    total = gn_ref[section].astype(F32) + got_ref[0].astype(F32)
    total = total + (got_ref[1].astype(F32) + got_ref[2].astype(F32))
    scaled = total.T * gain_ref[...].astype(F32)
    grad = inv * (
        scaled
        - jnp.mean(scaled, axis=1, keepdims=True)
        - unit * jnp.mean(scaled * unit, axis=1, keepdims=True)
    )
    gx_ref[...] = (gl_ref[...].astype(F32) + grad).astype(BF16)
    sum_ref[...] = (own_ref[core].astype(F32) + other_ref[...].astype(F32)).astype(BF16)


def sum_z_body(own_ref, got_ref, out_ref):
    z = (lax.axis_index("seq") // 2) % 4
    for y in range(4):
        total = own_ref[y, z].astype(F32) + got_ref[0, y].astype(F32)
        total = total + (got_ref[1, y].astype(F32) + got_ref[2, y].astype(F32))
        out_ref[y] = total.astype(BF16)


def sum_y_body(own_ref, got_ref, out_ref):
    y = lax.axis_index("seq") // 8
    total = own_ref[y].astype(F32) + got_ref[0].astype(F32)
    out_ref[...] = total + (got_ref[1].astype(F32) + got_ref[2].astype(F32))


def halo_peers(section, chip, core):
    found = [dev(chip, 1 - core, section)]
    for step in (1, -1):
        for other in (core, 1 - core):
            found.append(dev(around(chip, step), other, section))
    return found


def row_peers(section, chip, core):
    found = []
    for step in range(4):
        for turn in range(2):
            if step or turn:
                found.append(dev(chip, (core + turn) % 2, (section + step) % 4))
    return found


def section_peers(section, chip, core):
    return [dev(chip, core, (section + step) % 4) for step in range(1, 4)]


def partner(section, chip, core):
    return [dev(chip, 1 - core, section)]


def z_peers(section, chip, core):
    return [dev(chip // 4 * 4 + (chip + step) % 4, core, section) for step in range(1, 4)]


def y_peers(section, chip, core):
    return [dev((chip + 4 * step) % 16, core, section) for step in range(1, 4)]


def halo_plan(section, chip, core, ins, outs):
    (qkv,), (q, kv) = ins, outs
    own, other = pl.ds(core * PAIR, PAIR), pl.ds((1 - core) * PAIR, PAIR)
    mine = pl.ds(pl.multiple_of(core * 512, 512), 512)
    moves = []
    for step, base in ((1, 0), (-1, 2048)):
        lanes = pl.ds(pl.multiple_of(base + core * 512, 512), 512)
        for rows, target in ((own, core), (other, 1 - core)):
            moves.append(
                (qkv.at[1:3, rows, :], kv.at[:, :, lanes], dev(around(chip, step), target, section))
            )
    lanes = pl.ds(pl.multiple_of(1024 + core * 512, 512), 512)
    mate = dev(chip, 1 - core, section)
    moves.append((qkv.at[1:3, other, :], kv.at[:, :, lanes], mate))
    moves.append((qkv.at[0, other, :], q.at[:, mine], mate))
    moves.append((qkv.at[1:3, own, :], kv.at[:, :, lanes], None))
    moves.append((qkv.at[0, own, :], q.at[:, mine], None))
    return moves


def attended_plan(section, chip, core, ins, outs):
    (op,), (att, own) = ins, outs
    rows = pl.ds((section * 2 + core) * PAIR, PAIR)
    moves = []
    for step in (2, 1, 3, 0):
        for turn in range(2):
            to_section, to_core = (section + step) % 4, (core + turn) % 2
            device = dev(chip, to_core, to_section) if step or turn else None
            moves.append((op.at[to_core, to_section], att.at[rows, :], device))
    moves.append((op.at[1 - core], own.at[core], dev(chip, 1 - core, section)))
    moves.append((op.at[core], own.at[core], None))
    return moves


def grad_attended_plan(section, chip, core, ins, outs):
    (gat,), (gp,) = ins, outs
    moves = []
    for step in (2, 1, 3, 0):
        for turn in range(2):
            to_section, to_core = (section + step) % 4, (core + turn) % 2
            device = dev(chip, to_core, to_section) if step or turn else None
            rows = pl.ds((to_section * 2 + to_core) * PAIR, PAIR)
            moves.append((gat.at[rows, :], gp.at[core, section], device))
    return moves


def back_plan(section, chip, core, ins, outs):
    (dq, dkv, glt), (dq_all, dkv_all, glt_all) = ins, outs
    moves = []
    for step, base, slot in ((-1, 0, 0), (1, 2048, 1)):
        for target in (core, 1 - core):
            lanes = pl.ds(pl.multiple_of(base + target * 512, 512), 512)
            moves.append(
                (
                    dkv.at[:, :, lanes],
                    dkv_all.at[slot, core],
                    dev(around(chip, step), target, section),
                )
            )
    for target, device in ((1 - core, dev(chip, 1 - core, section)), (core, None)):
        lanes = pl.ds(pl.multiple_of(1024 + target * 512, 512), 512)
        moves.append((dkv.at[:, :, lanes], dkv_all.at[2, core], device))
        lanes = pl.ds(pl.multiple_of(target * 512, 512), 512)
        moves.append((dq.at[:, lanes], dq_all.at[core], device))
    for step in (2, 1, 3, 0):
        device = dev(chip, core, (section + step) % 4) if step else None
        moves.append((glt, glt_all.at[section], device))
    return moves


def sums_plan(section, chip, core, ins, outs):
    (gn, p), (got, other) = ins, outs
    moves = []
    for step in (2, 1, 3):
        to_section = (section + step) % 4
        moves.append((gn.at[to_section], got.at[step - 1], dev(chip, core, to_section)))
    moves.append((p.at[1 - core], other, dev(chip, 1 - core, section)))
    return moves


def rows_z_plan(section, chip, core, ins, outs):
    (gx, psum), (gx_all, got) = ins, outs
    moves = []
    for step in (2, 1, 3):
        z = (chip + step) % 4
        moves.append(
            (psum.at[:, z], got.at[step - 1], dev(chip // 4 * 4 + z, core, section))
        )
        moves.append((gx, gx_all.at[section], dev(chip, core, (section + step) % 4)))
    moves.append((gx, gx_all.at[section], None))
    return moves


def y_plan(section, chip, core, ins, outs):
    (psum,), (got,) = ins, outs
    moves = []
    for step in (2, 1, 3):
        to_chip = (chip + 4 * step) % 16
        moves.append((psum.at[to_chip // 4], got.at[step - 1], dev(to_chip, core, section)))
    return moves


def final_plan(section, chip, core, ins, outs):
    (total,), (both,) = ins, outs
    moves = []
    for target, device in ((1 - core, dev(chip, 1 - core, section)), (core, None)):
        moves.append((total.at[pl.ds(pl.multiple_of(target * 40, 8), 40), :], both.at[core], device))
    return moves


def local(
    tokens, norm_gain, w_qkv, w_out, merge_gain, seg_blocks, mb_sizes, mb_receiver, merged_grad
):
    section = lax.axis_index("section")
    seq = lax.axis_index("seq")
    chip = seq // 2
    w_full = lax.all_gather(w_out, "section", axis=0, tiled=True)
    ends = 64 * jnp.cumsum(seg_blocks)
    spans = jnp.stack([ends - 64 * seg_blocks, ends], axis=1)
    tile_first = chip * 1024 + 256 * jnp.arange(4, dtype=jnp.int32)[:, None]
    starts_in = jnp.max(jnp.where(spans[None, :, 0] <= tile_first, spans[None, :, 0], 0), axis=1)
    ends_in = jnp.min(jnp.where(ends[None, :] >= tile_first + 256, ends[None, :], 16384), axis=1)
    base = (chip - 1) * 1024
    bounds = jnp.stack(
        [(starts_in - base) // CHUNK, (ends_in - base + CHUNK - 1) // CHUNK], axis=1
    ).astype(jnp.int32)
    gain_one, gain_two = norm_gain.reshape(1, -1), merge_gain.reshape(1, -1)

    qkv, normed_t = local_call(
        project_body,
        [shape((3, 320, 512)), shape((1280, 512))],
        [tokens, gain_one, w_qkv],
        [pltpu.VMEM((512, 1280), BF16)],
    )
    q, kv = exchange(
        1, [shape((PAIR, 1024)), shape((2, PAIR, 3072))], [qkv], halo_peers, halo_plan
    )
    o, op, log_total = local_call(
        forward_body,
        [shape((PAIR, 1024)), shape((2, 4, PAIR, 128)), shape((2, 1024), F32)],
        [bounds, spans, q, kv],
        [
            pltpu.VMEM((2, 1024, 128), BF16),
            pltpu.VMEM((2, 128, 3072), BF16),
            pltpu.VMEM((256, 3072), F32),
        ],
        smem=1,
    )
    att, att_own = exchange(
        2, [shape((1280, 128)), shape((2, 4, PAIR, 128))], [op], row_peers, attended_plan
    )
    mgrad = lax.dynamic_slice_in_dim(merged_grad, section * 1280, 1280, 1)
    merged, grad_layer, glt, gat = local_call(
        middle_body,
        [shape((128, 1280)), shape((128, 1280)), shape((1280, 128)), shape((1280, 128))],
        [att, w_full, tokens, mgrad, gain_two],
    )
    (gp,) = exchange(3, [shape((2, 4, PAIR, 128))], [gat], row_peers, grad_attended_plan)
    dq, dkv = local_call(
        backward_body,
        [shape((PAIR, 1024)), shape((2, PAIR, 3072))],
        [bounds, spans, q, kv, o, log_total, gp],
        [
            pltpu.VMEM((2, 1024, 128), BF16),
            pltpu.VMEM((2, 128, 3072), BF16),
            pltpu.VMEM((2, 128, 3072), BF16),
            pltpu.VMEM((2, 1024, 128), BF16),
            pltpu.VMEM((PAIR, 1024), BF16),
            pltpu.VMEM((2, PAIR, 3072), F32),
        ],
        smem=1,
    )
    dq_all, dkv_all, glt_all = exchange(
        4,
        [shape((2, PAIR, 512)), shape((3, 2, 2, PAIR, 512)), shape((4, 1280, 128))],
        [dq, dkv, glt],
        lambda *spot: halo_peers(*spot) + section_peers(*spot),
        back_plan,
    )
    gn, p = local_call(
        gradients_body,
        [shape((4, 1280, 128)), shape((2, 1280, 640))],
        [dq_all, dkv_all, w_qkv, normed_t, glt_all, att_own],
        [
            pltpu.VMEM((960, 512), BF16),
            pltpu.VMEM((960, 512), BF16),
            pltpu.VMEM((320, 512), BF16),
            pltpu.VMEM((1280, 512), BF16),
        ],
    )
    gn_got, p_other = exchange(
        5,
        [shape((3, 1280, 128)), shape((1280, 640))],
        [gn, p],
        lambda *spot: section_peers(*spot) + partner(*spot),
        sums_plan,
    )
    gx, psum = local_call(
        first_norm_body,
        [shape((128, 1280)), shape((1280, 640))],
        [gn, gn_got, tokens, gain_one, grad_layer, p, p_other],
    )
    psum = psum.reshape(4, 4, 80, 640)
    gx_all, got_z = exchange(
        6,
        [shape((4, 128, 1280)), shape((3, 4, 80, 640))],
        [gx, psum],
        lambda *spot: section_peers(*spot) + z_peers(*spot),
        rows_z_plan,
    )
    (psum_z,) = local_call(sum_z_body, [shape((4, 80, 640))], [psum, got_z])
    (got_y,) = exchange(7, [shape((3, 80, 640))], [psum_z], y_peers, y_plan)
    (total,) = local_call(sum_y_body, [shape((80, 640), F32)], [psum_z, got_y])
    (both,) = exchange(8, [shape((2, 40, 640), F32)], [total], partner, final_plan)
    weights = both.transpose(1, 0, 2).reshape(40, 4, 320)
    grad_w_qkv = weights[:, :3].transpose(1, 0, 2)
    grad_w_out = weights[:, 3].T
    grad_x = gx_all.transpose(1, 0, 2).reshape(512, 1280)

    spread = lax.all_to_all(merged, "seq", 0, 0, tiled=True)
    receivers = jnp.arange(32, dtype=jnp.int32)
    mine = mb_receiver[None, :] == receivers[:, None]
    starts = jnp.cumsum(mb_sizes) - mb_sizes
    starts = jnp.sum(jnp.where(mine, starts[None, :], 0), axis=1)
    lives = jnp.sum(jnp.where(mine, mb_sizes[None, :], 0), axis=1)
    wanted = ((starts - seq + 31) // 32)[:, None] + jnp.arange(8, dtype=jnp.int32)[None, :]
    hot = wanted.reshape(256, 1) == jnp.arange(128, dtype=jnp.int32)[None, :]
    parcels = dot_nn(hot.astype(BF16), spread).astype(BF16)
    arrived = lax.all_to_all(parcels, "seq", 0, 0, tiled=True)
    my_start, my_live = starts[seq], lives[seq]
    slots = (receivers[:, None] - my_start) % 32 + 32 * jnp.arange(8, dtype=jnp.int32)[None, :]
    out_rows = jnp.arange(256, dtype=jnp.int32)[:, None]
    hot = (slots.reshape(1, 256) == out_rows) & (out_rows < my_live)
    delivered = dot_nn(hot.astype(BF16), arrived).astype(BF16)
    return (delivered, grad_x, grad_w_qkv, grad_w_out)


def solution(mesh):
    placed = (
        P("seq", None),
        P(),
        P(None, None, "section"),
        P("section", None),
        P(),
        P(),
        P(),
        P(),
        P("seq", None),
    )
    return jax.shard_map(
        local,
        mesh=mesh,
        in_specs=placed,
        out_specs=(
            P("seq", "section"),
            P("seq", None),
            P(None, "seq", "section"),
            P("section", "seq"),
        ),
        check_vma=False,
    )
```

```python
import math

import jax
import jax.numpy as jnp
from jax import lax
from jax.experimental import pallas as pl
from jax.experimental.pallas import tpu as pltpu
from jax.sharding import PartitionSpec as P

HEADS = 16
EPS = 1e-06
HEAD_DIM = 80
PAIR = 160
BIG = -1e30
CHUNK = 256
BF16 = jnp.bfloat16
F32 = jnp.float32
MESH = pl.DeviceIdType.MESH
FACTOR = HEAD_DIM ** -0.5
LOG2E = 1.0 / math.log(2.0)
LN2 = math.log(2.0)


def dot_nn(left, right):
    return lax.dot_general(left, right, (((1,), (0,)), ((), ())), preferred_element_type=F32)


def dot_nt(left, right):
    return lax.dot_general(left, right, (((1,), (1,)), ((), ())), preferred_element_type=F32)


def place():
    section = lax.axis_index("section")
    seq = lax.axis_index("seq")
    return section, seq // 2, seq % 2


def shape(dims, dtype=BF16):
    return jax.ShapeDtypeStruct(dims, dtype)


class Copies:
    def __init__(self, send_sems, recv_sems):
        self.send_sems, self.recv_sems, self.used = send_sems, recv_sems, 0

    def start(self, source, target, device):
        index = self.used
        self.used = index + 1
        if device is None:
            copy = pltpu.make_async_copy(source, target, self.recv_sems.at[index])
        else:
            copy = pltpu.make_async_remote_copy(
                src_ref=source,
                dst_ref=target,
                send_sem=self.send_sems.at[index],
                recv_sem=self.recv_sems.at[index],
                device_id=device,
                device_id_type=MESH,
            )
        copy.start()
        return copy


def wait_all(copies):
    for copy in copies:
        copy.wait()


def greet(peers):
    barrier = pltpu.get_barrier_semaphore()
    for peer in peers:
        pl.semaphore_signal(barrier, inc=1, device_id=peer, device_id_type=MESH)
    pl.semaphore_wait(barrier, len(peers))


def linked_call(number, body, outs, ins, scratch, copies, limit=48):
    vmem = pl.BlockSpec(memory_space=pltpu.VMEM)
    return pl.pallas_call(
        body,
        out_shape=outs,
        in_specs=[vmem] * len(ins),
        out_specs=[vmem] * len(outs),
        scratch_shapes=list(scratch)
        + [pltpu.SemaphoreType.DMA((copies,)), pltpu.SemaphoreType.DMA((copies,))],
        compiler_params=pltpu.CompilerParams(
            collective_id=number, has_side_effects=True, vmem_limit_bytes=limit << 20
        ),
    )(*ins)


def local_call(body, outs, ins, scratch=(), smem=0, limit=48):
    vmem = pl.BlockSpec(memory_space=pltpu.VMEM)
    scalar = pl.BlockSpec(memory_space=pltpu.SMEM)
    return pl.pallas_call(
        body,
        out_shape=outs,
        in_specs=[scalar] * smem + [vmem] * (len(ins) - smem),
        out_specs=[vmem] * len(outs),
        scratch_shapes=list(scratch),
        compiler_params=pltpu.CompilerParams(vmem_limit_bytes=limit << 20),
    )(*ins)


def dev(chip, core, section):
    return (chip * 2 + core, section)


def around(chip, step):
    return (chip + step + 16) % 16


def project_body(
    tokens_ref, gain_ref, w_ref, q_ref, kv_ref, normed_t_ref, normed_ref, out_ref, send, recv
):
    section, chip, core = place()
    copies = Copies(send, recv)
    gain = gain_ref[...].astype(F32)
    for tile in range(4):
        rows = pl.ds(tile * 128, 128)
        values = tokens_ref[rows, :].astype(F32)
        centered = values - jnp.mean(values, axis=1, keepdims=True)
        inv = lax.rsqrt(jnp.mean(centered * centered, axis=1, keepdims=True) + EPS)
        normed_ref[rows, :] = (centered * inv * gain).astype(BF16)
    own = pl.ds(pl.multiple_of(core * PAIR, 16), PAIR)
    other = pl.ds(pl.multiple_of((1 - core) * PAIR, 16), PAIR)
    mate = dev(chip, 1 - core, section)
    waits = []
    for which in (1, 2, 0):
        out = dot_nt(w_ref[which], normed_ref[...])
        if which == 0:
            out = out * (FACTOR * LOG2E)
        out_ref[which] = out.astype(BF16)
        if which == 1:
            greet(halo_peers(section, chip, core))
        if which:
            for step, base in ((1, 0), (-1, 2048)):
                lanes = pl.ds(pl.multiple_of(base + core * 512, 512), 512)
                for rows, target in ((own, core), (other, 1 - core)):
                    device = dev(around(chip, step), target, section)
                    waits.append(
                        copies.start(out_ref.at[which, rows, :], kv_ref.at[which - 1, :, lanes], device)
                    )
            lanes = pl.ds(pl.multiple_of(1024 + core * 512, 512), 512)
            target = kv_ref.at[which - 1, :, lanes]
        else:
            target = q_ref.at[:, pl.ds(pl.multiple_of(core * 512, 512), 512)]
        waits.append(copies.start(out_ref.at[which, other, :], target, mate))
        waits.append(copies.start(out_ref.at[which, own, :], target, None))
    for tile in range(4):
        rows = pl.ds(tile * 128, 128)
        normed_t_ref[:, rows] = normed_ref[rows, :].T
    wait_all(waits)


def membership(ends_ref, first, count):
    spots = first + lax.broadcasted_iota(jnp.int32, (32, count), 1)
    return (spots >= ends_ref[:, 0:1]) & (spots < ends_ref[:, 1:2])


def three_parts(row):
    high = row.astype(BF16)
    rest = row - high.astype(F32)
    middle = rest.astype(BF16)
    low = (rest - middle.astype(F32)).astype(BF16)
    return jnp.concatenate([high, middle, low, jnp.zeros((13, row.shape[1]), BF16)], axis=0)


def permutation(transposed):
    natural = lax.broadcasted_iota(jnp.int32, (512, 512), 1 if transposed else 0)
    moved = lax.broadcasted_iota(jnp.int32, (512, 512), 0 if transposed else 1)
    return jnp.where(natural == 4 * (moved % 128) + moved // 128, 1.0, 0.0).astype(BF16)


def forward_body(bounds_ref, ends_ref, q_ref, kv_ref, o_ref, op_ref, log_ref, qrow, kx, scores):
    chip = lax.axis_index("seq") // 2
    first = chip * 1024
    for head in range(2):
        feats = pl.ds(head * HEAD_DIM, HEAD_DIM)
        for block in range(4):
            lanes = pl.ds(block * 256, 256)
            inside = membership(ends_ref, first + block * 256, 256)
            joined = jnp.concatenate(
                [
                    q_ref[feats, lanes],
                    jnp.where(inside, 0.0, BIG).astype(BF16),
                    jnp.zeros((16, 256), BF16),
                ],
                axis=0,
            )
            qrow[head, lanes, :] = joined.T

    def build(chunk, carry):
        lanes = pl.ds(pl.multiple_of(chunk * CHUNK, CHUNK), CHUNK)
        inside = membership(ends_ref, first - 1024 + chunk * CHUNK, CHUNK)
        hot = jnp.where(inside, 1.0, 0.0).astype(BF16)
        for head in range(2):
            kx[head, 0:80, lanes] = kv_ref[0, pl.ds(head * HEAD_DIM, HEAD_DIM), lanes]
            kx[head, 80:112, lanes] = hot
            kx[head, 112:128, lanes] = jnp.zeros((16, CHUNK), BF16)
        return carry

    lax.fori_loop(bounds_ref[0, 0], bounds_ref[3, 1], build, 0)

    def tile_step(tile, carry):
        low, high = bounds_ref[tile, 0], bounds_ref[tile, 1]
        rows = pl.ds(pl.multiple_of(tile * 256, 256), 256)
        queries = [qrow[head, rows, :] for head in range(2)]

        def score_step(chunk, tops):
            lanes = pl.ds(pl.multiple_of(chunk * CHUNK, CHUNK), CHUNK)
            found = []
            for head in range(2):
                part = dot_nn(queries[head], kx[head, :, lanes])
                scores[head, :, lanes] = part
                found.append(jnp.maximum(tops[head], jnp.maximum(part[:, :128], part[:, 128:])))
            return tuple(found)

        start = jnp.full((256, 128), BIG, F32)
        tops = lax.fori_loop(low, high, score_step, (start, start))
        columns = [jnp.max(top, axis=1, keepdims=True) for top in tops]

        def sum_step(chunk, carry):
            lanes = pl.ds(pl.multiple_of(chunk * CHUNK, CHUNK), CHUNK)
            found = []
            for head in range(2):
                total, out = carry[head]
                feats = pl.ds(head * HEAD_DIM, HEAD_DIM)
                probs = jnp.exp2(scores[head, :, lanes] - columns[head])
                out = out + dot_nt(kv_ref[1, feats, lanes], probs.astype(BF16))
                found.append((total + (probs[:, :128] + probs[:, 128:]), out))
            return tuple(found)

        start = (jnp.zeros((256, 128), F32), jnp.zeros((HEAD_DIM, 256), F32))
        sums = lax.fori_loop(low, high, sum_step, (start, start))
        for head in range(2):
            total, out = sums[head]
            top_row = jnp.max(tops[head].T, axis=0, keepdims=True)
            total_row = jnp.sum(total.T, axis=0, keepdims=True)
            o_ref[pl.ds(head * HEAD_DIM, HEAD_DIM), rows] = (out * (1.0 / total_row)).astype(BF16)
            log_ref[head : head + 1, rows] = top_row + jnp.log(total_row) * LOG2E
        return carry

    lax.fori_loop(0, 4, tile_step, 0)
    perm = permutation(False)
    for half in range(2):
        moved = dot_nn(o_ref[:, half * 512 : half * 512 + 512], perm).astype(BF16)
        for part in range(4):
            op_ref[half, part] = moved[:, part * 128 : part * 128 + 128]


def backward_body(
    bounds_ref, ends_ref, q_ref, kv_ref, o_ref, log_ref, gp_ref, dq_ref, dkv_ref,
    qrow, kx, vx, grow, gnat, acc,
):
    chip = lax.axis_index("seq") // 2
    first = chip * 1024
    back = permutation(True)
    for half in range(2):
        joined = jnp.concatenate([gp_ref[half, part] for part in range(4)], axis=1)
        gnat[:, half * 512 : half * 512 + 512] = dot_nn(joined, back).astype(BF16)
    for head in range(2):
        feats = pl.ds(head * HEAD_DIM, HEAD_DIM)
        for block in range(4):
            lanes = pl.ds(block * 256, 256)
            inside = membership(ends_ref, first + block * 256, 256)
            joined = jnp.concatenate(
                [
                    q_ref[feats, lanes],
                    jnp.where(inside, 0.0, BIG).astype(BF16),
                    three_parts(-log_ref[head : head + 1, lanes]),
                ],
                axis=0,
            )
            qrow[head, lanes, :] = joined.T
            grads = gnat[feats, lanes]
            delta = jnp.sum(
                grads.astype(F32) * o_ref[feats, lanes].astype(F32), axis=0, keepdims=True
            )
            joined = jnp.concatenate(
                [grads, three_parts(-delta), jnp.zeros((32, 256), BF16)], axis=0
            )
            grow[head, lanes, :] = joined.T

    ones = jnp.where(lax.broadcasted_iota(jnp.int32, (16, CHUNK), 0) < 3, 1.0, 0.0).astype(BF16)

    def build(chunk, carry):
        lanes = pl.ds(pl.multiple_of(chunk * CHUNK, CHUNK), CHUNK)
        inside = membership(ends_ref, first - 1024 + chunk * CHUNK, CHUNK)
        hot = jnp.where(inside, 1.0, 0.0).astype(BF16)
        for head in range(2):
            feats = pl.ds(head * HEAD_DIM, HEAD_DIM)
            kx[head, 0:80, lanes] = kv_ref[0, feats, lanes]
            kx[head, 80:112, lanes] = hot
            kx[head, 112:128, lanes] = ones
            vx[head, 0:80, lanes] = kv_ref[1, feats, lanes]
            vx[head, 80:96, lanes] = ones
            vx[head, 96:128, lanes] = jnp.zeros((32, CHUNK), BF16)
        return carry

    lax.fori_loop(bounds_ref[0, 0], bounds_ref[3, 1], build, 0)
    acc[...] = jnp.zeros_like(acc)

    def tile_step(tile, carry):
        low, high = bounds_ref[tile, 0], bounds_ref[tile, 1]
        rows = pl.ds(pl.multiple_of(tile * 256, 256), 256)
        features = [pl.ds(head * HEAD_DIM, HEAD_DIM) for head in range(2)]

        def step(chunk, sums):
            lanes = pl.ds(pl.multiple_of(chunk * CHUNK, CHUNK), CHUNK)
            found = []
            for head in range(2):
                feats = features[head]
                probs = jnp.exp2(dot_nn(qrow[head, rows, :], kx[head, :, lanes]))
                shifted = dot_nn(grow[head, rows, :], vx[head, :, lanes])
                dscores = (probs * shifted).astype(BF16)
                acc[0, feats, lanes] += dot_nn(q_ref[feats, rows], dscores)
                acc[1, feats, lanes] += dot_nn(gnat[feats, rows], probs.astype(BF16))
                found.append(sums[head] + dot_nt(kv_ref[0, feats, lanes], dscores))
            return tuple(found)

        start = jnp.zeros((HEAD_DIM, 256), F32)
        sums = lax.fori_loop(low, high, step, (start, start))
        for head in range(2):
            dq_ref[features[head], rows] = (sums[head] * FACTOR).astype(BF16)
        return carry

    lax.fori_loop(0, 4, tile_step, 0)
    dkv_ref[0] = (acc[0] * LN2).astype(BF16)
    dkv_ref[1] = acc[1].astype(BF16)


def middle_body(
    op_ref, w_ref, tokens_ref, mgrad_ref, gain_ref,
    gl_ref, glt_ref, gp_ref, own_ref, table_ref,
    att, gat, packed, send, recv,
):
    section, chip, core = place()
    copies = Copies(send, recv)
    greet(row_peers(section, chip, core) + core_peers(section, chip, core))
    rows = pl.ds(pl.multiple_of((section * 2 + core) * PAIR, 16), PAIR)
    waits = []
    for step in (2, 1, 3, 0):
        for turn in range(2):
            to_section, to_core = (section + step) % 4, (core + turn) % 2
            device = dev(chip, to_core, to_section) if step or turn else None
            waits.append(copies.start(op_ref.at[to_core, to_section], att.at[rows, :], device))
    late = [
        copies.start(op_ref.at[1 - core], own_ref.at[core], dev(chip, 1 - core, section)),
        copies.start(op_ref.at[core], own_ref.at[core], None),
    ]
    row = lax.broadcasted_iota(jnp.int32, (128, 512), 0)
    column = lax.broadcasted_iota(jnp.int32, (128, 512), 1)
    chosen = jnp.where(column == 4 * row + section, 1.0, 0.0).astype(BF16)
    values = dot_nn(chosen, tokens_ref[...])
    gain = gain_ref[...].astype(F32)
    scaled = mgrad_ref[...].astype(F32) * gain
    scaled_mean = jnp.mean(scaled, axis=1, keepdims=True)
    row = lax.broadcasted_iota(jnp.int32, (128, 128), 0)
    column = lax.broadcasted_iota(jnp.int32, (128, 128), 1)
    order = jnp.where(column == 16 * (row % 8) + row // 8, 1.0, 0.0).astype(BF16)
    wait_all(waits)
    layer = values + dot_nn(att[...].T, w_ref[...])
    centered = layer - jnp.mean(layer, axis=1, keepdims=True)
    inv = lax.rsqrt(jnp.mean(centered * centered, axis=1, keepdims=True) + EPS)
    unit = centered * inv
    grad_layer = inv * (
        scaled - scaled_mean - unit * jnp.mean(scaled * unit, axis=1, keepdims=True)
    )
    grad_layer = grad_layer.astype(BF16)
    gat[...] = dot_nt(w_ref[...], grad_layer).astype(BF16)
    for step in (2, 1, 3, 0):
        for turn in range(2):
            to_section, to_core = (section + step) % 4, (core + turn) % 2
            device = dev(chip, to_core, to_section) if step or turn else None
            rows = pl.ds(pl.multiple_of((to_section * 2 + to_core) * PAIR, 16), PAIR)
            late.append(copies.start(gat.at[rows, :], gp_ref.at[core, section], device))
    moved = dot_nn(order, (unit * gain).astype(BF16))
    for chip_to in range(16):
        eight = moved[chip_to * 8 : chip_to * 8 + 8]
        packed[chip_to] = jnp.concatenate([eight[:, :640], eight[:, 640:]], axis=0).astype(BF16)
    for step in range(16):
        to_chip = (chip + step) % 16
        device = dev(to_chip, core, section) if step else None
        late.append(copies.start(packed.at[to_chip], table_ref.at[chip], device))
    gl_ref[...] = grad_layer
    glt_ref[...] = grad_layer.T
    wait_all(late)


def tail_body(
    dq_ref, dkv_ref, glt_ref, own_ref, table_ref, starts_ref, live_ref, gl_ref, tokens_ref,
    gain_ref, w_ref, normed_t_ref,
    delivered_ref, gx_ref, weights_ref,
    dq_in, dkv_in, dj, rows_ref, gn, gn_in, gx_own, gx_all, att, glt,
    parcels, arrived, p_mine, p_away, p_in,
    sum_a, sum_b, in_a, in_b, sub_a, sub_b, late_a, late_b, total, send, recv,
):
    section, chip, core = place()
    y, z = chip // 4, chip % 4
    copies = Copies(send, recv)
    mate = dev(chip, 1 - core, section)
    greet(plane_peers(section, chip, core) + section_peers(section, chip, core))
    back = []
    for half in range(2):
        waits = []
        for step, base, slot in ((-1, 0, 0), (1, 2048, 1)):
            for target in (core, 1 - core):
                lanes = pl.ds(pl.multiple_of(base + target * 512 + half * 256, 256), 256)
                device = dev(around(chip, step), target, section)
                waits.append(
                    copies.start(dkv_ref.at[:, :, lanes], dkv_in.at[half, slot, core], device)
                )
        for target, device in ((1 - core, mate), (core, None)):
            lanes = pl.ds(pl.multiple_of(1024 + target * 512 + half * 256, 256), 256)
            waits.append(copies.start(dkv_ref.at[:, :, lanes], dkv_in.at[half, 2, core], device))
            lanes = pl.ds(pl.multiple_of(target * 512 + half * 256, 256), 256)
            waits.append(copies.start(dq_ref.at[:, lanes], dq_in.at[half, core], device))
        back.append(waits)

    begin = starts_ref[...]
    block, offset = begin // 128, begin % 128
    first = 8 * ((block + 1 - core) // 2)
    first = first + jnp.where(block % 2 == core, (offset - chip + 15) // 16, 0)
    out_row = lax.broadcasted_iota(jnp.int32, (512, 256), 0)
    in_row = lax.broadcasted_iota(jnp.int32, (512, 256), 1)
    wanted = first + out_row % 8
    wanted = (wanted // 8) * 16 + wanted % 8 + 8 * ((out_row // 8) % 2)
    hot = jnp.where(in_row == wanted, 1.0, 0.0).astype(BF16)
    table = table_ref[...].reshape(256, 640)
    parcels[...] = dot_nn(hot, table).astype(BF16).reshape(32, 16, 640)

    for head in range(2):
        for part in range(4):
            att[head * PAIR : head * PAIR + PAIR, part * 128 : part * 128 + 128] = own_ref[head, part]
    for part in range(4):
        glt[:, part * 128 : part * 128 + 128] = glt_ref[part]

    row = lax.broadcasted_iota(jnp.int32, (256, 256), 0)
    column = lax.broadcasted_iota(jnp.int32, (256, 256), 1)
    by_part = jnp.where(column == 4 * (row % 64) + row // 64, 1.0, 0.0).astype(BF16)
    natural = jnp.where(row == 4 * (column % 64) + column // 64, 1.0, 0.0).astype(BF16)
    w_all = w_ref[...]
    sums = []
    for half in range(2):
        wait_all(back[half])
        lanes = pl.ds(half * 256, 256)
        for head in range(2):
            dj[head * PAIR : head * PAIR + PAIR, lanes] = dq_in[half, head]
            for which in range(2):
                grad = dkv_in[half, 0, head, which].astype(F32)
                grad = grad + dkv_in[half, 1, head, which].astype(F32)
                grad = grad + dkv_in[half, 2, head, which].astype(F32)
                start = 320 * (which + 1) + head * PAIR
                dj[start : start + PAIR, lanes] = grad.astype(BF16)
        rows_ref[...] = dot_nt(by_part, dj[:, lanes]).astype(BF16)
        gn[half] = dot_nn(rows_ref[...], w_all).astype(BF16).reshape(4, 64, 1280)
        waits = []
        for step in (2, 1, 3):
            to_section = (section + step) % 4
            device = dev(chip, core, to_section)
            waits.append(copies.start(gn.at[half, to_section], gn_in.at[half, step - 1], device))
        sums.append(waits)

    deliveries = []
    for step in range(16):
        for turn in range(2):
            to_chip, to_core = (chip + step) % 16, (core + turn) % 2
            device = dev(to_chip, to_core, section) if step or turn else None
            deliveries.append(
                copies.start(parcels.at[to_chip * 2 + to_core], arrived.at[chip * 2 + core], device)
            )

    def products(index, core_of):
        rows = pl.ds(index * 320, 320)
        normed = normed_t_ref[rows, :]
        if core_of == 0:
            return dot_nt(normed, dj[0:640, :])
        return jnp.concatenate(
            [dot_nt(normed, dj[640:960, :]), dot_nt(glt[rows, :], att[...])], axis=1
        )

    pairs = []
    for index in range(4):
        for core_of in range(2):
            @pl.when(core != core_of)
            def _():
                p_away[index] = products(index, core_of).astype(BF16).reshape(4, 80, 640)

        pairs.append(copies.start(p_away.at[index], p_in.at[index], mate))
    for index in range(4):
        for core_of in range(2):
            @pl.when(core == core_of)
            def _():
                p_mine[index] = products(index, core_of).reshape(4, 80, 640)

    gathers = []

    def finish_norm(half):
        row = lax.broadcasted_iota(jnp.int32, (64, 256), 0)
        column = lax.broadcasted_iota(jnp.int32, (64, 256), 1)
        chosen = jnp.where(column == 4 * row + section, 1.0, 0.0).astype(BF16)
        values = dot_nn(chosen, tokens_ref[half * 256 : half * 256 + 256, :])
        centered = values - jnp.mean(values, axis=1, keepdims=True)
        inv = lax.rsqrt(jnp.mean(centered * centered, axis=1, keepdims=True) + EPS)
        unit = centered * inv
        wait_all(sums[half])
        grad = gn[half, section].astype(F32) + gn_in[half, 0].astype(F32)
        grad = grad + (gn_in[half, 1].astype(F32) + gn_in[half, 2].astype(F32))
        scaled = grad * gain_ref[...].astype(F32)
        grad = inv * (
            scaled
            - jnp.mean(scaled, axis=1, keepdims=True)
            - unit * jnp.mean(scaled * unit, axis=1, keepdims=True)
        )
        grad = grad + gl_ref[half * 64 : half * 64 + 64, :].astype(F32)
        gx_own[half] = grad.astype(BF16)
        waits = []
        for step in (2, 1, 3, 0):
            device = dev(chip, core, (section + step) % 4) if step else None
            waits.append(copies.start(gx_own.at[half], gx_all.at[half, section], device))
        gathers.append(waits)

    finish_norm(0)
    firsts = [[], []]
    for index in range(4):
        pairs[index].wait()
        summed = (p_mine[index] + p_in[index].astype(F32)).astype(BF16)
        sum_a[index] = summed[:, :, :384]
        sum_b[index] = summed[:, :, 384:]
    for step in (2, 1, 3):
        to_z, to_y = (z + step) % 4, (y + step) % 4
        device = dev(y * 4 + to_z, core, section)
        firsts[0].append(copies.start(sum_a.at[:, to_z], in_a.at[step - 1], device))
        device = dev(to_y * 4 + z, core, section)
        firsts[1].append(copies.start(sum_b.at[to_y], in_b.at[step - 1], device))
    finish_norm(1)
    seconds = []
    wait_all(firsts[1])
    grad = sum_b[y].astype(F32) + in_b[0].astype(F32)
    sub_b[...] = (grad + (in_b[1].astype(F32) + in_b[2].astype(F32))).astype(BF16)
    for step in (2, 1, 3):
        to_z = (z + step) % 4
        device = dev(y * 4 + to_z, core, section)
        seconds.append(copies.start(sub_b.at[to_z], late_b.at[step - 1], device))
    wait_all(firsts[0])
    for index in range(4):
        grad = sum_a[index, z].astype(F32) + in_a[0, index].astype(F32)
        grad = grad + (in_a[1, index].astype(F32) + in_a[2, index].astype(F32))
        sub_a[index] = grad.astype(BF16)
    for step in (2, 1, 3):
        to_y = (y + step) % 4
        device = dev(to_y * 4 + z, core, section)
        seconds.append(copies.start(sub_a.at[to_y], late_a.at[step - 1], device))

    lane = lax.broadcasted_iota(jnp.int32, (1, 512), 1)
    from_chip, from_core, side, number = lane // 32, (lane // 16) % 2, (lane // 8) % 2, lane % 8
    begin, live = live_ref[0:1, :], live_ref[1:2, :]
    block, offset = begin // 128, begin % 128
    spot = 8 * ((block + 1 - from_core) // 2) + number
    spot = spot + jnp.where(block % 2 == from_core, (offset - from_chip + 15) // 16, 0)
    slot = (2 * (spot // 8) + from_core) * 128 + 16 * (spot % 8) + from_chip - begin
    out_row = lax.broadcasted_iota(jnp.int32, (256, 512), 0)
    taken = (out_row == slot) & (out_row < live)
    wait_all(deliveries)
    rows = arrived[...].reshape(512, 640)
    for which in range(2):
        hot = jnp.where(taken & (side == which), 1.0, 0.0).astype(BF16)
        delivered_ref[:, which * 640 : which * 640 + 640] = dot_nn(hot, rows).astype(BF16)

    wait_all(seconds)
    grad = sub_a[y].astype(F32) + late_a[0].astype(F32)
    total[:, :384] = grad + (late_a[1].astype(F32) + late_a[2].astype(F32))
    grad = sub_b[z].astype(F32) + late_b[0].astype(F32)
    total[:, 384:] = grad + (late_b[1].astype(F32) + late_b[2].astype(F32))
    lasts = []
    for target, device in ((1 - core, mate), (core, None)):
        rows = pl.ds(pl.multiple_of(target * 40, 8), 40)
        lasts.append(copies.start(total.at[rows, :], weights_ref.at[core], device))
    for half in range(2):
        wait_all(gathers[half])
        rows = gx_all[half].reshape(256, 1280)
        gx_ref[half * 256 : half * 256 + 256, :] = dot_nn(natural, rows).astype(BF16)
    wait_all(lasts)


def halo_peers(section, chip, core):
    found = [dev(chip, 1 - core, section)]
    for step in (1, -1):
        for other in (core, 1 - core):
            found.append(dev(around(chip, step), other, section))
    return found


def row_peers(section, chip, core):
    found = []
    for step in range(4):
        for turn in range(2):
            if step or turn:
                found.append(dev(chip, (core + turn) % 2, (section + step) % 4))
    return found


def section_peers(section, chip, core):
    return [dev(chip, core, (section + step) % 4) for step in range(1, 4)]


def core_peers(section, chip, core):
    return [dev((chip + step) % 16, core, section) for step in range(1, 16)]


def plane_peers(section, chip, core):
    found = [dev(chip, 1 - core, section)]
    for step in range(1, 16):
        for turn in range(2):
            found.append(dev((chip + step) % 16, (core + turn) % 2, section))
    return found


def local(
    tokens, norm_gain, w_qkv, w_out, merge_gain, seg_blocks, mb_sizes, mb_receiver, merged_grad
):
    section = lax.axis_index("section")
    seq = lax.axis_index("seq")
    chip = seq // 2
    w_full = lax.all_gather(w_out, "section", axis=0, tiled=True)
    w_rows = w_qkv.transpose(0, 2, 1)
    ends = 64 * jnp.cumsum(seg_blocks)
    spans = jnp.stack([ends - 64 * seg_blocks, ends], axis=1)
    tile_first = chip * 1024 + 256 * jnp.arange(4, dtype=jnp.int32)[:, None]
    starts_in = jnp.max(jnp.where(spans[None, :, 0] <= tile_first, spans[None, :, 0], 0), axis=1)
    ends_in = jnp.min(jnp.where(ends[None, :] >= tile_first + 256, ends[None, :], 16384), axis=1)
    base = (chip - 1) * 1024
    bounds = jnp.stack(
        [(starts_in - base) // CHUNK, (ends_in - base + CHUNK - 1) // CHUNK], axis=1
    ).astype(jnp.int32)
    mine = mb_receiver[None, :] == jnp.arange(32, dtype=jnp.int32)[:, None]
    starts = jnp.cumsum(mb_sizes) - mb_sizes
    starts = jnp.sum(jnp.where(mine, starts[None, :], 0), axis=1)
    lives = jnp.sum(jnp.where(mine, mb_sizes[None, :], 0), axis=1)
    start_rows = jnp.repeat(starts, 16).reshape(512, 1)
    here = jnp.broadcast_to(jnp.stack([starts[seq], lives[seq]])[:, None], (2, 512))
    gain_one, gain_two = norm_gain.reshape(1, -1), merge_gain.reshape(1, -1)
    mgrad = lax.dynamic_slice_in_dim(merged_grad, section * 1280, 1280, 1)

    q, kv, normed_t = linked_call(
        1,
        project_body,
        [shape((PAIR, 1024)), shape((2, PAIR, 3072)), shape((1280, 512))],
        [tokens, gain_one, w_rows],
        [pltpu.VMEM((512, 1280), BF16), pltpu.VMEM((3, 320, 512), BF16)],
        16,
    )
    o, op, log_total = local_call(
        forward_body,
        [shape((PAIR, 1024)), shape((2, 4, PAIR, 128)), shape((2, 1024), F32)],
        [bounds, spans, q, kv],
        [
            pltpu.VMEM((2, 1024, 128), BF16),
            pltpu.VMEM((2, 128, 3072), BF16),
            pltpu.VMEM((2, 256, 3072), F32),
        ],
        smem=1,
    )
    grad_layer, glt, gp, att_own, table = linked_call(
        2,
        middle_body,
        [
            shape((128, 1280)),
            shape((1280, 128)),
            shape((2, 4, PAIR, 128)),
            shape((2, 4, PAIR, 128)),
            shape((16, 16, 640)),
        ],
        [op, w_full, tokens, mgrad, gain_two],
        [
            pltpu.VMEM((1280, 128), BF16),
            pltpu.VMEM((1280, 128), BF16),
            pltpu.VMEM((16, 16, 640), BF16),
        ],
        34,
    )
    glt_all = lax.all_gather(glt, "section")
    dq, dkv = local_call(
        backward_body,
        [shape((PAIR, 1024)), shape((2, PAIR, 3072))],
        [bounds, spans, q, kv, o, log_total, gp],
        [
            pltpu.VMEM((2, 1024, 128), BF16),
            pltpu.VMEM((2, 128, 3072), BF16),
            pltpu.VMEM((2, 128, 3072), BF16),
            pltpu.VMEM((2, 1024, 128), BF16),
            pltpu.VMEM((PAIR, 1024), BF16),
            pltpu.VMEM((2, PAIR, 3072), F32),
        ],
        smem=1,
    )
    delivered, grad_x, weights = linked_call(
        3,
        tail_body,
        [shape((256, 1280)), shape((512, 1280)), shape((2, 40, 640), F32)],
        [
            dq, dkv, glt_all, att_own, table, start_rows, here, grad_layer, tokens,
            gain_one, w_rows.reshape(960, 1280), normed_t,
        ],
        [
            pltpu.VMEM((2, 2, PAIR, 256), BF16),
            pltpu.VMEM((2, 3, 2, 2, PAIR, 256), BF16),
            pltpu.VMEM((960, 512), BF16),
            pltpu.VMEM((256, 960), BF16),
            pltpu.VMEM((2, 4, 64, 1280), BF16),
            pltpu.VMEM((2, 3, 64, 1280), BF16),
            pltpu.VMEM((2, 64, 1280), BF16),
            pltpu.VMEM((2, 4, 64, 1280), BF16),
            pltpu.VMEM((320, 512), BF16),
            pltpu.VMEM((1280, 512), BF16),
            pltpu.VMEM((32, 16, 640), BF16),
            pltpu.VMEM((32, 16, 640), BF16),
            pltpu.VMEM((4, 4, 80, 640), F32),
            pltpu.VMEM((4, 4, 80, 640), BF16),
            pltpu.VMEM((4, 4, 80, 640), BF16),
            pltpu.VMEM((4, 4, 80, 384), BF16),
            pltpu.VMEM((4, 4, 80, 256), BF16),
            pltpu.VMEM((3, 4, 80, 384), BF16),
            pltpu.VMEM((3, 4, 80, 256), BF16),
            pltpu.VMEM((4, 80, 384), BF16),
            pltpu.VMEM((4, 80, 256), BF16),
            pltpu.VMEM((3, 80, 384), BF16),
            pltpu.VMEM((3, 80, 256), BF16),
            pltpu.VMEM((80, 640), F32),
        ],
        90,
    )
    sums = weights.transpose(1, 0, 2).reshape(40, 4, 320)
    grad_w_qkv = sums[:, :3].transpose(1, 0, 2)
    grad_w_out = sums[:, 3].T
    return (delivered, grad_x, grad_w_qkv, grad_w_out)


def solution(mesh):
    placed = (
        P("seq", None),
        P(),
        P(None, None, "section"),
        P("section", None),
        P(),
        P(),
        P(),
        P(),
        P("seq", None),
    )
    return jax.shard_map(
        local,
        mesh=mesh,
        in_specs=placed,
        out_specs=(
            P("seq", "section"),
            P("seq", None),
            P(None, "seq", "section"),
            P("section", "seq"),
        ),
        check_vma=False,
    )
```

```python
import math

import jax
import jax.numpy as jnp
from jax import lax
from jax.experimental import pallas as pl
from jax.experimental.pallas import tpu as pltpu
from jax.sharding import PartitionSpec as P

HEADS = 16
EPS = 1e-06
HEAD_DIM = 80
PAIR = 160
BIG = -1e30
CHUNK = 256
SAFE = 60.0
BF16 = jnp.bfloat16
F32 = jnp.float32
MESH = pl.DeviceIdType.MESH
FACTOR = HEAD_DIM ** -0.5
LOG2E = 1.0 / math.log(2.0)
LN2 = math.log(2.0)


def dot_nn(left, right):
    return lax.dot_general(left, right, (((1,), (0,)), ((), ())), preferred_element_type=F32)


def dot_nt(left, right):
    return lax.dot_general(left, right, (((1,), (1,)), ((), ())), preferred_element_type=F32)


def place():
    section = lax.axis_index("section")
    seq = lax.axis_index("seq")
    return section, seq // 2, seq % 2


def shape(dims, dtype=BF16):
    return jax.ShapeDtypeStruct(dims, dtype)


class Copies:
    def __init__(self, send_sems, recv_sems):
        self.send_sems, self.recv_sems, self.used = send_sems, recv_sems, 0

    def start(self, source, target, device):
        index = self.used
        self.used = index + 1
        if device is None:
            copy = pltpu.make_async_copy(source, target, self.recv_sems.at[index])
        else:
            copy = pltpu.make_async_remote_copy(
                src_ref=source,
                dst_ref=target,
                send_sem=self.send_sems.at[index],
                recv_sem=self.recv_sems.at[index],
                device_id=device,
                device_id_type=MESH,
            )
        copy.start()
        return copy


def wait_all(copies):
    for copy in copies:
        copy.wait()


def greet(peers):
    barrier = pltpu.get_barrier_semaphore()
    for peer in peers:
        pl.semaphore_signal(barrier, inc=1, device_id=peer, device_id_type=MESH)
    pl.semaphore_wait(barrier, len(peers))


VMEM = pl.BlockSpec(memory_space=pltpu.VMEM)
SMEM = pl.BlockSpec(memory_space=pltpu.SMEM)
HBM = pl.BlockSpec(memory_space=pltpu.HBM)


def call(body, outs, ins, scratch=(), copies=0, number=None, limit=14):
    more = {} if number is None else {"collective_id": number, "has_side_effects": True}
    semaphores = [pltpu.SemaphoreType.DMA((copies,))] * (0 if not copies else 1 if number is None else 2)
    return pl.pallas_call(
        body,
        out_shape=[array for _, array in outs],
        in_specs=[place for place, _ in ins],
        out_specs=[place for place, _ in outs],
        scratch_shapes=list(scratch) + semaphores,
        compiler_params=pltpu.CompilerParams(vmem_limit_bytes=limit << 20, **more),
    )(*[array for _, array in ins])


def dev(chip, core, section):
    return (chip * 2 + core, section)


def around(chip, step):
    return (chip + step + 16) % 16


def project_body(
    tokens_hbm, gain_ref, w_hbm, w_out_hbm, q_ref, kv_ref, normed_t_hbm, w_full,
    tokens_ref, w_ref, normed_ref, normed_t_ref, out_ref, send, recv,
):
    section, chip, core = place()
    copies = Copies(send, recv)
    load_tokens = copies.start(tokens_hbm, tokens_ref, None)
    load_w = copies.start(w_hbm, w_ref, None)
    greet(halo_peers(section, chip, core) + section_peers(section, chip, core)[::2])
    mate = dev(chip, 1 - core, section)
    ahead, behind = (section + 1) % 4, (section + 3) % 4
    ahead_dev, behind_dev = dev(chip, core, ahead), dev(chip, core, behind)

    def w_rows(owner, start, count):
        return w_full.at[pl.ds(pl.multiple_of(owner * 320 + core * PAIR + start, 16), count), :]

    mine = w_out_hbm.at[pl.ds(pl.multiple_of(core * PAIR, 16), PAIR), :]
    to_ahead = copies.start(mine, w_rows(section, 0, PAIR), ahead_dev)
    to_behind = copies.start(mine, w_rows(section, 0, PAIR), behind_dev)
    keep = w_full.at[pl.ds(pl.multiple_of(section * 320, 16), 320), :]
    waits = [copies.start(w_out_hbm, keep, None)]
    load_tokens.wait()
    gain = gain_ref[...].reshape(1, 1280).astype(F32)
    for tile in range(4):
        rows = pl.ds(tile * 128, 128)
        values = tokens_ref[rows, :].astype(F32)
        centered = values - jnp.mean(values, axis=1, keepdims=True)
        inv = lax.rsqrt(jnp.mean(centered * centered, axis=1, keepdims=True) + EPS)
        normed_ref[rows, :] = (centered * inv * gain).astype(BF16)
    own = pl.ds(pl.multiple_of(core * PAIR, 16), PAIR)
    other = pl.ds(pl.multiple_of((1 - core) * PAIR, 16), PAIR)
    load_w.wait()
    for which in (1, 2, 0):
        out = dot_nt(w_ref[which], normed_ref[...])
        if which == 0:
            out = out * (FACTOR * LOG2E)
        out_ref[which] = out.astype(BF16)
        if which:
            for step, base in ((1, 0), (-1, 2048)):
                lanes = pl.ds(pl.multiple_of(base + core * 512, 512), 512)
                for rows, target in ((own, core), (other, 1 - core)):
                    device = dev(around(chip, step), target, section)
                    waits.append(
                        copies.start(out_ref.at[which, rows, :], kv_ref.at[which - 1, :, lanes], device)
                    )
            lanes = pl.ds(pl.multiple_of(1024 + core * 512, 512), 512)
            target = kv_ref.at[which - 1, :, lanes]
        else:
            target = q_ref.at[:, pl.ds(pl.multiple_of(core * 512, 512), 512)]
        waits.append(copies.start(out_ref.at[which, other, :], target, mate))
        waits.append(copies.start(out_ref.at[which, own, :], target, None))
    for tile in range(4):
        rows = pl.ds(tile * 128, 128)
        normed_t_ref[:, rows] = normed_ref[rows, :].T
    waits.append(copies.start(normed_t_ref, normed_t_hbm, None))

    to_ahead.wait()
    relay = [copies.start(w_rows(behind, 0, 80), w_rows(behind, 0, 80), ahead_dev)]
    to_behind.wait()
    relay.append(copies.start(w_rows(ahead, 80, 80), w_rows(ahead, 80, 80), behind_dev))
    waits.append(copies.start(w_rows(behind, 0, PAIR), w_rows(behind, 0, PAIR), mate))
    waits.append(copies.start(w_rows(ahead, 0, PAIR), w_rows(ahead, 0, PAIR), mate))
    far = (section + 2) % 4
    for copy, start in zip(relay, (0, 80)):
        copy.wait()
        waits.append(copies.start(w_rows(far, start, 80), w_rows(far, start, 80), mate))
    wait_all(waits)


def spans_and_bounds(seg_ref, first, spans_ref, bounds_ref):
    row = lax.broadcasted_iota(jnp.int32, (32, 128), 0)
    begins, ends = jnp.zeros((32, 128), jnp.int32), jnp.zeros((32, 128), jnp.int32)
    end = jnp.int32(0)
    low = [jnp.int32(0)] * 4
    high = [jnp.int32(16384)] * 4
    for image in range(32):
        begin = end
        end = begin + 64 * seg_ref[image]
        begins = jnp.where(row == image, begin, begins)
        ends = jnp.where(row == image, end, ends)
        for tile in range(4):
            start = first + 256 * tile
            low[tile] = jnp.where(begin <= start, begin, low[tile])
            high[tile] = jnp.where((begin < start + 256) & (end >= start + 256), end, high[tile])
    spans_ref[0] = begins
    spans_ref[1] = ends
    for tile in range(4):
        bounds_ref[tile, 0] = (low[tile] - (first - 1024)) // CHUNK
        bounds_ref[tile, 1] = (high[tile] - (first - 1024) + CHUNK - 1) // CHUNK


def membership(spans_ref, first, count):
    spots = first + lax.broadcasted_iota(jnp.int32, (32, count), 1)
    return (spots >= spans_ref[0, :, 0:1]) & (spots < spans_ref[1, :, 0:1])


def three_parts(row):
    high = row.astype(BF16)
    rest = row - high.astype(F32)
    middle = rest.astype(BF16)
    low = (rest - middle.astype(F32)).astype(BF16)
    return jnp.concatenate([high, middle, low, jnp.zeros((13, row.shape[1]), BF16)], axis=0)


def permutation(transposed):
    moved = lax.broadcasted_iota(jnp.int32, (512, 1) if transposed else (1, 512), 0 if transposed else 1)
    natural = lax.broadcasted_iota(jnp.int32, (512, 512), 1 if transposed else 0)
    return jnp.where(natural == 4 * (moved % 128) + moved // 128, 1.0, 0.0).astype(BF16)


def forward_body(
    seg_ref, q_ref, kv_ref, o_hbm, kv_hbm, op_ref, log_ref,
    spans_ref, bounds_ref, o_ref, qrow, kx, vrow, sems,
):
    first = (lax.axis_index("seq") // 2) * 1024
    keep = pltpu.make_async_copy(kv_ref, kv_hbm, sems.at[0])
    keep.start()
    spans_and_bounds(seg_ref, first, spans_ref, bounds_ref)
    longest = []
    for head in range(2):
        feats = pl.ds(head * HEAD_DIM, HEAD_DIM)
        for block in range(4):
            lanes = pl.ds(block * 256, 256)
            inside = membership(spans_ref, first + block * 256, 256)
            joined = jnp.concatenate(
                [
                    q_ref[feats, lanes],
                    jnp.where(inside, 0.0, BIG).astype(BF16),
                    jnp.zeros((16, 256), BF16),
                ],
                axis=0,
            )
            qrow[head, lanes, :] = joined.T
        values = q_ref[feats, :].astype(F32)
        longest.append(jnp.max(jnp.sum(values * values, axis=0, keepdims=True)))

    ones = jnp.where(lax.broadcasted_iota(jnp.int32, (16, CHUNK), 0) < 3, 1.0, 0.0).astype(BF16)

    def build(chunk, tops):
        found = []
        lanes = pl.ds(pl.multiple_of(chunk * CHUNK, CHUNK), CHUNK)
        inside = membership(spans_ref, first - 1024 + chunk * CHUNK, CHUNK)
        hot = jnp.where(inside, 1.0, 0.0).astype(BF16)
        for head in range(2):
            feats = pl.ds(head * HEAD_DIM, HEAD_DIM)
            kx[head, 0:80, lanes] = kv_ref[0, feats, lanes]
            kx[head, 80:112, lanes] = hot
            kx[head, 112:128, lanes] = ones
            joined = jnp.concatenate(
                [kv_ref[1, feats, lanes], ones, jnp.zeros((32, CHUNK), BF16)], axis=0
            )
            vrow[head, lanes, :] = joined.T
            values = kv_ref[0, feats, lanes].astype(F32)
            found.append(jnp.maximum(tops[head], jnp.sum(values * values, axis=0, keepdims=True)))
        return tuple(found)

    start = jnp.zeros((1, CHUNK), F32)
    tops = lax.fori_loop(bounds_ref[0, 0], bounds_ref[3, 1], build, (start, start))
    small = longest[0] * jnp.max(tops[0]) <= SAFE * SAFE
    small = small & (longest[1] * jnp.max(tops[1]) <= SAFE * SAFE)
    lane = lax.broadcasted_iota(jnp.int32, (256, 128), 1)

    def sum_tile(tile, rows):
        def sum_step(chunk, sums):
            lanes = pl.ds(pl.multiple_of(chunk * CHUNK, CHUNK), CHUNK)
            probs = [
                jnp.exp2(dot_nn(qrow[head, rows, :], kx[head, :, lanes])).astype(BF16)
                for head in range(2)
            ]
            return tuple(sums[head] + dot_nn(probs[head], vrow[head, lanes, :]) for head in range(2))

        start = jnp.zeros((256, 128), F32)
        return lax.fori_loop(bounds_ref[tile, 0], bounds_ref[tile, 1], sum_step, (start, start))

    def write(head, rows, sums, top_row):
        out = sums.T
        total_row = out[80:81, :]
        o_ref[pl.ds(head * HEAD_DIM, HEAD_DIM), rows] = (out[:80] * (1.0 / total_row)).astype(BF16)
        log_ref[head : head + 1, rows] = top_row + jnp.log(total_row) * LOG2E

    def plain_step(tile, carry):
        rows = pl.ds(pl.multiple_of(tile * 256, 256), 256)
        sums = sum_tile(tile, rows)
        for head in range(2):
            write(head, rows, sums[head], 0.0)
        return carry

    def shifted_step(tile, carry):
        low, high = bounds_ref[tile, 0], bounds_ref[tile, 1]
        rows = pl.ds(pl.multiple_of(tile * 256, 256), 256)

        def score_step(chunk, tops):
            lanes = pl.ds(pl.multiple_of(chunk * CHUNK, CHUNK), CHUNK)
            found = []
            for head in range(2):
                part = dot_nn(qrow[head, rows, :], kx[head, :, lanes])
                found.append(jnp.maximum(tops[head], jnp.maximum(part[:, :128], part[:, 128:])))
            return tuple(found)

        start = jnp.full((256, 128), BIG, F32)
        tops = lax.fori_loop(low, high, score_step, (start, start))
        for head in range(2):
            shift = -jnp.max(tops[head], axis=1, keepdims=True)
            part_one = shift.astype(BF16).astype(F32)
            part_two = (shift - part_one).astype(BF16).astype(F32)
            part_three = shift - part_one - part_two
            moved = jnp.where(lane == 112, part_one, qrow[head, rows, :].astype(F32))
            moved = jnp.where(lane == 113, part_two, moved)
            qrow[head, rows, :] = jnp.where(lane == 114, part_three, moved).astype(BF16)

        sums = sum_tile(tile, rows)
        for head in range(2):
            write(head, rows, sums[head], jnp.max(tops[head].T, axis=0, keepdims=True))
        return carry

    @pl.when(small)
    def _():
        lax.fori_loop(0, 4, plain_step, 0)

    @pl.when(jnp.logical_not(small))
    def _():
        lax.fori_loop(0, 4, shifted_step, 0)

    keep_o = pltpu.make_async_copy(o_ref, o_hbm, sems.at[1])
    keep_o.start()
    perm = permutation(False)
    for half in range(2):
        moved = dot_nn(o_ref[:, half * 512 : half * 512 + 512], perm).astype(BF16)
        for part in range(4):
            op_ref[half, part] = moved[:, part * 128 : part * 128 + 128]
    keep.wait()
    keep_o.wait()


def backward_body(
    seg_ref, sizes_ref, receiver_ref, q_ref, kv_hbm, o_hbm, log_ref, gp_ref,
    dq_ref, dkv_ref, starts_ref, here_ref,
    spans_ref, bounds_ref, kv_ref, o_ref, qrow, kx, vx, krow, grow, gnat, acc, sems,
):
    seq = lax.axis_index("seq")
    first = (seq // 2) * 1024
    load_kv = pltpu.make_async_copy(kv_hbm, kv_ref, sems.at[0])
    load_o = pltpu.make_async_copy(o_hbm, o_ref, sems.at[1])
    load_kv.start()
    load_o.start()
    spans_and_bounds(seg_ref, first, spans_ref, bounds_ref)
    start = jnp.int32(0)
    my_start, my_size = jnp.int32(0), jnp.int32(0)
    for batch in range(32):
        size, receiver = sizes_ref[batch], receiver_ref[batch]
        starts_ref[pl.ds(pl.multiple_of(receiver * 16, 16), 16), :] = jnp.full((16, 128), start)
        my_start = jnp.where(receiver == seq, start, my_start)
        my_size = jnp.where(receiver == seq, size, my_size)
        start = start + size
    here_ref[0:8, :] = jnp.full((8, 512), my_start)
    here_ref[8:16, :] = jnp.full((8, 512), my_size)
    back = permutation(True)
    for half in range(2):
        joined = jnp.concatenate([gp_ref[half, part] for part in range(4)], axis=1)
        gnat[:, half * 512 : half * 512 + 512] = dot_nn(joined, back).astype(BF16)
    load_kv.wait()
    load_o.wait()
    for head in range(2):
        feats = pl.ds(head * HEAD_DIM, HEAD_DIM)
        for block in range(4):
            lanes = pl.ds(block * 256, 256)
            inside = membership(spans_ref, first + block * 256, 256)
            joined = jnp.concatenate(
                [
                    q_ref[feats, lanes],
                    jnp.where(inside, 0.0, BIG).astype(BF16),
                    three_parts(-log_ref[head : head + 1, lanes]),
                ],
                axis=0,
            )
            qrow[head, lanes, :] = joined.T
            grads = gnat[feats, lanes]
            delta = jnp.sum(
                grads.astype(F32) * o_ref[feats, lanes].astype(F32), axis=0, keepdims=True
            )
            joined = jnp.concatenate(
                [grads, three_parts(-delta), jnp.zeros((32, 256), BF16)], axis=0
            )
            grow[head, lanes, :] = joined.T

    ones = jnp.where(lax.broadcasted_iota(jnp.int32, (16, CHUNK), 0) < 3, 1.0, 0.0).astype(BF16)

    def build(chunk, carry):
        lanes = pl.ds(pl.multiple_of(chunk * CHUNK, CHUNK), CHUNK)
        inside = membership(spans_ref, first - 1024 + chunk * CHUNK, CHUNK)
        hot = jnp.where(inside, 1.0, 0.0).astype(BF16)
        for head in range(2):
            feats = pl.ds(head * HEAD_DIM, HEAD_DIM)
            kx[head, 0:80, lanes] = kv_ref[0, feats, lanes]
            kx[head, 80:112, lanes] = hot
            kx[head, 112:128, lanes] = ones
            krow[head, lanes, :] = kx[head, :, lanes].T
            vx[head, 0:80, lanes] = kv_ref[1, feats, lanes]
            vx[head, 80:96, lanes] = ones
            vx[head, 96:128, lanes] = jnp.zeros((32, CHUNK), BF16)
        return carry

    lax.fori_loop(bounds_ref[0, 0], bounds_ref[3, 1], build, 0)
    acc[...] = jnp.zeros_like(acc)

    def tile_step(tile, carry):
        low, high = bounds_ref[tile, 0], bounds_ref[tile, 1]
        rows = pl.ds(pl.multiple_of(tile * 256, 256), 256)
        features = [pl.ds(head * HEAD_DIM, HEAD_DIM) for head in range(2)]

        def step(chunk, sums):
            lanes = pl.ds(pl.multiple_of(chunk * CHUNK, CHUNK), CHUNK)
            found = []
            for head in range(2):
                feats = features[head]
                probs = jnp.exp2(dot_nn(qrow[head, rows, :], kx[head, :, lanes]))
                shifted = dot_nn(grow[head, rows, :], vx[head, :, lanes])
                dscores = (probs * shifted).astype(BF16)
                acc[0, feats, lanes] += dot_nn(q_ref[feats, rows], dscores)
                acc[1, feats, lanes] += dot_nn(gnat[feats, rows], probs.astype(BF16))
                found.append(sums[head] + dot_nn(dscores, krow[head, lanes, :]))
            return tuple(found)

        start = jnp.zeros((256, 128), F32)
        sums = lax.fori_loop(low, high, step, (start, start))
        for head in range(2):
            dq_ref[features[head], rows] = (sums[head].T[:80] * FACTOR).astype(BF16)
        return carry

    lax.fori_loop(0, 4, tile_step, 0)
    dkv_ref[0] = (acc[0] * LN2).astype(BF16)
    dkv_ref[1] = acc[1].astype(BF16)


def middle_body(
    op_ref, w_hbm, tokens_hbm, mgrad_hbm, gain_ref,
    gp_ref, gl_hbm, glt_hbm, own_ref, table_ref,
    w_ref, tokens_ref, mgrad_ref, gl_ref, glt_ref, att, gat, packed, send, recv,
):
    section, chip, core = place()
    copies = Copies(send, recv)
    columns = pl.ds(pl.multiple_of(section * 1280, 128), 1280)
    load_mgrad = copies.start(mgrad_hbm.at[:, columns], mgrad_ref, None)
    load_tokens = copies.start(tokens_hbm, tokens_ref, None)
    load_w = copies.start(w_hbm, w_ref, None)
    greet(row_peers(section, chip, core) + core_peers(section, chip, core))
    rows = pl.ds(pl.multiple_of((section * 2 + core) * PAIR, 16), PAIR)
    waits = []
    for step in (2, 1, 3, 0):
        for turn in range(2):
            to_section, to_core = (section + step) % 4, (core + turn) % 2
            device = dev(chip, to_core, to_section) if step or turn else None
            waits.append(copies.start(op_ref.at[to_core, to_section], att.at[rows, :], device))
    late = [
        copies.start(op_ref.at[1 - core], own_ref.at[core], dev(chip, 1 - core, section)),
        copies.start(op_ref.at[core], own_ref.at[core], None),
    ]
    row = lax.broadcasted_iota(jnp.int32, (128, 512), 0)
    column = lax.broadcasted_iota(jnp.int32, (128, 512), 1)
    chosen = jnp.where(column == 4 * row + section, 1.0, 0.0).astype(BF16)
    load_tokens.wait()
    load_mgrad.wait()
    values = dot_nn(chosen, tokens_ref[...])
    gain = gain_ref[...].reshape(1, 1280).astype(F32)
    scaled = mgrad_ref[...].astype(F32) * gain
    scaled_mean = jnp.mean(scaled, axis=1, keepdims=True)
    row = lax.broadcasted_iota(jnp.int32, (128, 128), 0)
    column = lax.broadcasted_iota(jnp.int32, (128, 128), 1)
    order = jnp.where(column == 16 * (row % 8) + row // 8, 1.0, 0.0).astype(BF16)
    load_w.wait()
    wait_all(waits)
    layer = values + dot_nn(att[...].T, w_ref[...])
    centered = layer - jnp.mean(layer, axis=1, keepdims=True)
    inv = lax.rsqrt(jnp.mean(centered * centered, axis=1, keepdims=True) + EPS)
    unit = centered * inv
    grad_layer = inv * (
        scaled - scaled_mean - unit * jnp.mean(scaled * unit, axis=1, keepdims=True)
    )
    grad_layer = grad_layer.astype(BF16)
    gat[...] = dot_nt(w_ref[...], grad_layer).astype(BF16)
    for step in (2, 1, 3, 0):
        for turn in range(2):
            to_section, to_core = (section + step) % 4, (core + turn) % 2
            device = dev(chip, to_core, to_section) if step or turn else None
            rows = pl.ds(pl.multiple_of((to_section * 2 + to_core) * PAIR, 16), PAIR)
            late.append(copies.start(gat.at[rows, :], gp_ref.at[core, section], device))
    moved = dot_nn(order, (unit * gain).astype(BF16))
    for chip_to in range(16):
        eight = moved[chip_to * 8 : chip_to * 8 + 8]
        packed[chip_to] = jnp.concatenate([eight[:, :640], eight[:, 640:]], axis=0).astype(BF16)
    for step in range(16):
        to_chip = (chip + step) % 16
        device = dev(to_chip, core, section) if step else None
        late.append(copies.start(packed.at[to_chip], table_ref.at[chip], device))
    gl_ref[...] = grad_layer
    glt_ref[...] = grad_layer.T
    late.append(copies.start(gl_ref, gl_hbm, None))
    late.append(copies.start(glt_ref, glt_hbm, None))
    wait_all(late)


def tail_body(
    dq_ref, dkv_ref, starts_ref, live_ref, glt_hbm, own_hbm, table_hbm, gl_hbm, tokens_hbm,
    gain_ref, w_hbm, normed_t_hbm,
    delivered_ref, gx_all, weights_ref,
    table_ref, gl_ref, tokens_ref, w_ref, normed_t_ref,
    dkv_in, dj, rows_ref, gn, gn_in, gx_own, att, glt,
    parcels, arrived, p_mine, p_away, p_in,
    sum_a, sum_b, in_a, in_b, sub_a, sub_b, late_a, late_b, total, send, recv,
):
    section, chip, core = place()
    y, z = chip // 4, chip % 4
    copies = Copies(send, recv)
    mate = dev(chip, 1 - core, section)
    greet(plane_peers(section, chip, core) + section_peers(section, chip, core))
    back = []
    for half in range(2):
        waits = []
        for step, base, slot in ((-1, 0, 0), (1, 2048, 1)):
            for target in (core, 1 - core):
                lanes = pl.ds(pl.multiple_of(base + target * 512 + half * 256, 256), 256)
                device = dev(around(chip, step), target, section)
                waits.append(
                    copies.start(dkv_ref.at[:, :, lanes], dkv_in.at[half, slot, core], device)
                )
        for target, device in ((1 - core, mate), (core, None)):
            lanes = pl.ds(pl.multiple_of(1024 + target * 512 + half * 256, 256), 256)
            waits.append(copies.start(dkv_ref.at[:, :, lanes], dkv_in.at[half, 2, core], device))
            lanes = pl.ds(pl.multiple_of(target * 512 + half * 256, 256), 256)
            into = dj.at[pl.ds(pl.multiple_of(core * PAIR, 16), PAIR), half * 256 : half * 256 + 256]
            waits.append(copies.start(dq_ref.at[:, lanes], into, device))
        back.append(waits)
    gathered = []
    lanes = pl.ds(pl.multiple_of(section * 128, 128), 128)
    for step in (2, 1, 3, 0):
        device = dev(chip, core, (section + step) % 4) if step else None
        gathered.append(copies.start(glt_hbm, glt.at[:, lanes], device))
    load_table = copies.start(table_hbm, table_ref, None)
    load_w = copies.start(w_hbm, w_ref, None)
    loads = [
        copies.start(source, target, None)
        for source, target in (
            (normed_t_hbm, normed_t_ref), (tokens_hbm, tokens_ref), (gl_hbm, gl_ref)
        )
    ]
    for head in range(2):
        for part in range(4):
            target = att.at[head * PAIR : head * PAIR + PAIR, part * 128 : part * 128 + 128]
            loads.append(copies.start(own_hbm.at[head, part], target, None))

    begin = starts_ref[:, 0:1]
    block, offset = begin // 128, begin % 128
    first = 8 * ((block + 1 - core) // 2)
    first = first + jnp.where(block % 2 == core, (offset - chip + 15) // 16, 0)
    out_row = lax.broadcasted_iota(jnp.int32, (512, 256), 0)
    in_row = lax.broadcasted_iota(jnp.int32, (512, 256), 1)
    wanted = first + out_row % 8
    wanted = (wanted // 8) * 16 + wanted % 8 + 8 * ((out_row // 8) % 2)
    hot = jnp.where(in_row == wanted, 1.0, 0.0).astype(BF16)
    load_table.wait()
    table = table_ref[...].reshape(256, 640)
    parcels[...] = dot_nn(hot, table).astype(BF16).reshape(32, 16, 640)

    row = lax.broadcasted_iota(jnp.int32, (256, 256), 0)
    column = lax.broadcasted_iota(jnp.int32, (256, 256), 1)
    by_part = jnp.where(column == 4 * (row % 64) + row // 64, 1.0, 0.0).astype(BF16)
    load_w.wait()
    w_all = w_ref[...].reshape(960, 1280)
    sums = []
    for half in range(2):
        wait_all(back[half])
        lanes = pl.ds(half * 256, 256)
        for head in range(2):
            for which in range(2):
                grad = dkv_in[half, 0, head, which].astype(F32)
                grad = grad + dkv_in[half, 1, head, which].astype(F32)
                grad = grad + dkv_in[half, 2, head, which].astype(F32)
                start = 320 * (which + 1) + head * PAIR
                dj[start : start + PAIR, lanes] = grad.astype(BF16)
        rows_ref[...] = dot_nt(by_part, dj[:, lanes]).astype(BF16)
        gn[half] = dot_nn(rows_ref[...], w_all).astype(BF16).reshape(4, 64, 1280)
        waits = []
        for step in (2, 1, 3):
            to_section = (section + step) % 4
            device = dev(chip, core, to_section)
            waits.append(copies.start(gn.at[half, to_section], gn_in.at[half, step - 1], device))
        sums.append(waits)

    deliveries = []
    for step in range(16):
        for turn in range(2):
            to_chip, to_core = (chip + step) % 16, (core + turn) % 2
            device = dev(to_chip, to_core, section) if step or turn else None
            deliveries.append(
                copies.start(parcels.at[to_chip * 2 + to_core], arrived.at[chip * 2 + core], device)
            )

    def products(index, core_of):
        rows = pl.ds(index * 320, 320)
        normed = normed_t_ref[rows, :]
        if core_of == 0:
            return dot_nt(normed, dj[0:640, :])
        return jnp.concatenate(
            [dot_nt(normed, dj[640:960, :]), dot_nt(glt[rows, :], att[...])], axis=1
        )

    wait_all(gathered)
    wait_all(loads)
    pairs = []
    for index in range(4):
        for core_of in range(2):
            @pl.when(core != core_of)
            def _():
                p_away[index] = products(index, core_of).astype(BF16).reshape(4, 80, 640)

        pairs.append(copies.start(p_away.at[index], p_in.at[index], mate))
    for index in range(4):
        for core_of in range(2):
            @pl.when(core == core_of)
            def _():
                p_mine[index] = products(index, core_of).reshape(4, 80, 640)

    gathers = []

    def finish_norm(half):
        row = lax.broadcasted_iota(jnp.int32, (64, 256), 0)
        column = lax.broadcasted_iota(jnp.int32, (64, 256), 1)
        chosen = jnp.where(column == 4 * row + section, 1.0, 0.0).astype(BF16)
        values = dot_nn(chosen, tokens_ref[half * 256 : half * 256 + 256, :])
        centered = values - jnp.mean(values, axis=1, keepdims=True)
        inv = lax.rsqrt(jnp.mean(centered * centered, axis=1, keepdims=True) + EPS)
        unit = centered * inv
        wait_all(sums[half])
        grad = gn[half, section].astype(F32) + gn_in[half, 0].astype(F32)
        grad = grad + (gn_in[half, 1].astype(F32) + gn_in[half, 2].astype(F32))
        scaled = grad * gain_ref[...].reshape(1, 1280).astype(F32)
        grad = inv * (
            scaled
            - jnp.mean(scaled, axis=1, keepdims=True)
            - unit * jnp.mean(scaled * unit, axis=1, keepdims=True)
        )
        grad = grad + gl_ref[half * 64 : half * 64 + 64, :].astype(F32)
        gx_own[half] = grad.astype(BF16)
        waits = []
        for step in (2, 1, 3, 0):
            device = dev(chip, core, (section + step) % 4) if step else None
            waits.append(copies.start(gx_own.at[half], gx_all.at[half, section], device))
        gathers.append(waits)

    finish_norm(0)
    firsts = [[], []]
    for index in range(4):
        pairs[index].wait()
        summed = (p_mine[index] + p_in[index].astype(F32)).astype(BF16)
        sum_a[index] = summed[:, :, :384]
        sum_b[index] = summed[:, :, 384:]
    for step in (2, 1, 3):
        to_z, to_y = (z + step) % 4, (y + step) % 4
        device = dev(y * 4 + to_z, core, section)
        firsts[0].append(copies.start(sum_a.at[:, to_z], in_a.at[step - 1], device))
        device = dev(to_y * 4 + z, core, section)
        firsts[1].append(copies.start(sum_b.at[to_y], in_b.at[step - 1], device))
    finish_norm(1)
    seconds = []
    wait_all(firsts[1])
    grad = sum_b[y].astype(F32) + in_b[0].astype(F32)
    sub_b[...] = (grad + (in_b[1].astype(F32) + in_b[2].astype(F32))).astype(BF16)
    for step in (2, 1, 3):
        to_z = (z + step) % 4
        device = dev(y * 4 + to_z, core, section)
        seconds.append(copies.start(sub_b.at[to_z], late_b.at[step - 1], device))
    wait_all(firsts[0])
    for index in range(4):
        grad = sum_a[index, z].astype(F32) + in_a[0, index].astype(F32)
        grad = grad + (in_a[1, index].astype(F32) + in_a[2, index].astype(F32))
        sub_a[index] = grad.astype(BF16)
    for step in (2, 1, 3):
        to_y = (y + step) % 4
        device = dev(to_y * 4 + z, core, section)
        seconds.append(copies.start(sub_a.at[to_y], late_a.at[step - 1], device))

    lane = lax.broadcasted_iota(jnp.int32, (1, 512), 1)
    from_chip, from_core, side, number = lane // 32, (lane // 16) % 2, (lane // 8) % 2, lane % 8
    begin, live = live_ref[0:1, :], live_ref[8:9, :]
    block, offset = begin // 128, begin % 128
    spot = 8 * ((block + 1 - from_core) // 2) + number
    spot = spot + jnp.where(block % 2 == from_core, (offset - from_chip + 15) // 16, 0)
    slot = (2 * (spot // 8) + from_core) * 128 + 16 * (spot % 8) + from_chip - begin
    out_row = lax.broadcasted_iota(jnp.int32, (256, 512), 0)
    taken = (out_row == slot) & (out_row < live)
    wait_all(deliveries)
    rows = arrived[...].reshape(512, 640)
    for which in range(2):
        hot = jnp.where(taken & (side == which), 1.0, 0.0).astype(BF16)
        delivered_ref[:, which * 640 : which * 640 + 640] = dot_nn(hot, rows).astype(BF16)

    wait_all(seconds)
    grad = sub_a[y].astype(F32) + late_a[0].astype(F32)
    total[:, :384] = grad + (late_a[1].astype(F32) + late_a[2].astype(F32))
    grad = sub_b[z].astype(F32) + late_b[0].astype(F32)
    total[:, 384:] = grad + (late_b[1].astype(F32) + late_b[2].astype(F32))
    lasts = []
    for target, device in ((1 - core, mate), (core, None)):
        rows = pl.ds(pl.multiple_of(target * 40, 8), 40)
        lasts.append(copies.start(total.at[rows, :], weights_ref.at[core], device))
    wait_all(lasts)
    for waits in gathers:
        wait_all(waits)


def results_body(gx_ref, both_ref, arrived_ref, gx_out, w_qkv_out, w_out_out, delivered_out):
    row = lax.broadcasted_iota(jnp.int32, (256, 256), 0)
    column = lax.broadcasted_iota(jnp.int32, (256, 256), 1)
    natural = jnp.where(row == 4 * (column % 64) + column // 64, 1.0, 0.0).astype(BF16)
    for half in range(2):
        rows = gx_ref[half].reshape(256, 1280)
        gx_out[half * 256 : half * 256 + 256, :] = dot_nn(natural, rows).astype(BF16)
    w_qkv_out[0] = both_ref[0, :, :320]
    w_qkv_out[1] = both_ref[0, :, 320:]
    w_qkv_out[2] = both_ref[1, :, :320]
    w_out_out[...] = both_ref[1, :, 320:]
    delivered_out[...] = arrived_ref[...]


def halo_peers(section, chip, core):
    found = [dev(chip, 1 - core, section)]
    for step in (1, -1):
        for other in (core, 1 - core):
            found.append(dev(around(chip, step), other, section))
    return found


def row_peers(section, chip, core):
    found = []
    for step in range(4):
        for turn in range(2):
            if step or turn:
                found.append(dev(chip, (core + turn) % 2, (section + step) % 4))
    return found


def section_peers(section, chip, core):
    return [dev(chip, core, (section + step) % 4) for step in range(1, 4)]


def core_peers(section, chip, core):
    return [dev((chip + step) % 16, core, section) for step in range(1, 16)]


def plane_peers(section, chip, core):
    found = [dev(chip, 1 - core, section)]
    for step in range(1, 16):
        for turn in range(2):
            found.append(dev((chip + step) % 16, (core + turn) % 2, section))
    return found


def local(
    tokens, norm_gain, w_qkv, w_out, merge_gain, seg_blocks, mb_sizes, mb_receiver, merged_grad
):
    w_rows = w_qkv.transpose(0, 2, 1)
    q, kv, normed_t, w_full = call(
        project_body,
        [
            (VMEM, shape((PAIR, 1024))),
            (VMEM, shape((2, PAIR, 3072))),
            (HBM, shape((1280, 512))),
            (HBM, shape((1280, 1280))),
        ],
        [(HBM, tokens), (VMEM, norm_gain), (HBM, w_rows), (HBM, w_out)],
        [
            pltpu.VMEM((512, 1280), BF16),
            pltpu.VMEM((3, 320, 1280), BF16),
            pltpu.VMEM((512, 1280), BF16),
            pltpu.VMEM((1280, 512), BF16),
            pltpu.VMEM((3, 320, 512), BF16),
        ],
        copies=32,
        number=1,
        limit=20,
    )
    o, kv_kept, op, log_total = call(
        forward_body,
        [
            (HBM, shape((PAIR, 1024))),
            (HBM, shape((2, PAIR, 3072))),
            (VMEM, shape((2, 4, PAIR, 128))),
            (VMEM, shape((2, 1024), F32)),
        ],
        [(SMEM, seg_blocks), (VMEM, q), (VMEM, kv)],
        [
            pltpu.VMEM((2, 32, 128), jnp.int32),
            pltpu.SMEM((4, 2), jnp.int32),
            pltpu.VMEM((PAIR, 1024), BF16),
            pltpu.VMEM((2, 1024, 128), BF16),
            pltpu.VMEM((2, 128, 3072), BF16),
            pltpu.VMEM((2, 3072, 128), BF16),
        ],
        copies=2,
        limit=16,
    )
    gp, grad_layer, glt, att_own, table = call(
        middle_body,
        [
            (VMEM, shape((2, 4, PAIR, 128))),
            (HBM, shape((128, 1280))),
            (HBM, shape((1280, 128))),
            (HBM, shape((2, 4, PAIR, 128))),
            (HBM, shape((16, 16, 640))),
        ],
        [(VMEM, op), (HBM, w_full), (HBM, tokens), (HBM, merged_grad), (VMEM, merge_gain)],
        [
            pltpu.VMEM((1280, 1280), BF16),
            pltpu.VMEM((512, 1280), BF16),
            pltpu.VMEM((128, 1280), BF16),
            pltpu.VMEM((128, 1280), BF16),
            pltpu.VMEM((1280, 128), BF16),
            pltpu.VMEM((1280, 128), BF16),
            pltpu.VMEM((1280, 128), BF16),
            pltpu.VMEM((16, 16, 640), BF16),
        ],
        copies=40,
        number=2,
        limit=20,
    )
    dq, dkv, start_rows, here = call(
        backward_body,
        [
            (VMEM, shape((PAIR, 1024))),
            (VMEM, shape((2, PAIR, 3072))),
            (VMEM, shape((512, 128), jnp.int32)),
            (VMEM, shape((16, 512), jnp.int32)),
        ],
        [
            (SMEM, seg_blocks), (SMEM, mb_sizes), (SMEM, mb_receiver),
            (VMEM, q), (HBM, kv_kept), (HBM, o), (VMEM, log_total), (VMEM, gp),
        ],
        [
            pltpu.VMEM((2, 32, 128), jnp.int32),
            pltpu.SMEM((4, 2), jnp.int32),
            pltpu.VMEM((2, PAIR, 3072), BF16),
            pltpu.VMEM((PAIR, 1024), BF16),
            pltpu.VMEM((2, 1024, 128), BF16),
            pltpu.VMEM((2, 128, 3072), BF16),
            pltpu.VMEM((2, 128, 3072), BF16),
            pltpu.VMEM((2, 3072, 128), BF16),
            pltpu.VMEM((2, 1024, 128), BF16),
            pltpu.VMEM((PAIR, 1024), BF16),
            pltpu.VMEM((2, PAIR, 3072), F32),
        ],
        copies=2,
        limit=26,
    )
    arrived, gx_all, weights = call(
        tail_body,
        [
            (VMEM, shape((256, 1280))),
            (VMEM, shape((2, 4, 64, 1280))),
            (VMEM, shape((2, 40, 640), F32)),
        ],
        [
            (VMEM, dq), (VMEM, dkv), (VMEM, start_rows), (VMEM, here), (HBM, glt), (HBM, att_own),
            (HBM, table), (HBM, grad_layer), (HBM, tokens), (VMEM, norm_gain), (HBM, w_rows),
            (HBM, normed_t),
        ],
        [
            pltpu.VMEM((16, 16, 640), BF16),
            pltpu.VMEM((128, 1280), BF16),
            pltpu.VMEM((512, 1280), BF16),
            pltpu.VMEM((3, 320, 1280), BF16),
            pltpu.VMEM((1280, 512), BF16),
            pltpu.VMEM((2, 3, 2, 2, PAIR, 256), BF16),
            pltpu.VMEM((960, 512), BF16),
            pltpu.VMEM((256, 960), BF16),
            pltpu.VMEM((2, 4, 64, 1280), BF16),
            pltpu.VMEM((2, 3, 64, 1280), BF16),
            pltpu.VMEM((2, 64, 1280), BF16),
            pltpu.VMEM((320, 512), BF16),
            pltpu.VMEM((1280, 512), BF16),
            pltpu.VMEM((32, 16, 640), BF16),
            pltpu.VMEM((32, 16, 640), BF16),
            pltpu.VMEM((4, 4, 80, 640), F32),
            pltpu.VMEM((4, 4, 80, 640), BF16),
            pltpu.VMEM((4, 4, 80, 640), BF16),
            pltpu.VMEM((4, 4, 80, 384), BF16),
            pltpu.VMEM((4, 4, 80, 256), BF16),
            pltpu.VMEM((3, 4, 80, 384), BF16),
            pltpu.VMEM((3, 4, 80, 256), BF16),
            pltpu.VMEM((4, 80, 384), BF16),
            pltpu.VMEM((4, 80, 256), BF16),
            pltpu.VMEM((3, 80, 384), BF16),
            pltpu.VMEM((3, 80, 256), BF16),
            pltpu.VMEM((80, 640), F32),
        ],
        copies=112,
        number=3,
        limit=42,
    )
    grad_x, grad_w_qkv, grad_w_out, delivered = call(
        results_body,
        [
            (VMEM, shape((512, 1280))),
            (VMEM, shape((3, 40, 320), F32)),
            (VMEM, shape((40, 320), F32)),
            (VMEM, shape((256, 1280))),
        ],
        [(VMEM, gx_all), (VMEM, weights), (VMEM, arrived)],
        limit=14,
    )
    return (delivered, grad_x, grad_w_qkv, grad_w_out.T)


def solution(mesh):
    placed = (
        P("seq", None),
        P(),
        P(None, None, "section"),
        P("section", None),
        P(),
        P(),
        P(),
        P(),
        P("seq", None),
    )
    return jax.shard_map(
        local,
        mesh=mesh,
        in_specs=placed,
        out_specs=(
            P("seq", "section"),
            P("seq", None),
            P(None, "seq", "section"),
            P("section", "seq"),
        ),
        check_vma=False,
    )
```

```python
import math

import jax
import jax.numpy as jnp
from jax import lax
from jax.experimental import pallas as pl
from jax.experimental.pallas import tpu as pltpu
from jax.sharding import PartitionSpec as P

HEADS = 16
EPS = 1e-06
HEAD_DIM = 80
PAIR = 160
BIG = -1e30
CHUNK = 256
SAFE = 60.0
BF16 = jnp.bfloat16
F32 = jnp.float32
MESH = pl.DeviceIdType.MESH
FACTOR = HEAD_DIM ** -0.5
LOG2E = 1.0 / math.log(2.0)
LN2 = math.log(2.0)


def dot_nn(left, right):
    return lax.dot_general(left, right, (((1,), (0,)), ((), ())), preferred_element_type=F32)


def dot_nt(left, right):
    return lax.dot_general(left, right, (((1,), (1,)), ((), ())), preferred_element_type=F32)


def place():
    section = lax.axis_index("section")
    seq = lax.axis_index("seq")
    return section, seq // 2, seq % 2


def shape(dims, dtype=BF16):
    return jax.ShapeDtypeStruct(dims, dtype)


class Copies:
    def __init__(self, send_sems, recv_sems):
        self.send_sems, self.recv_sems, self.used = send_sems, recv_sems, 0

    def start(self, source, target, device):
        index = self.used
        self.used = index + 1
        if device is None:
            copy = pltpu.make_async_copy(source, target, self.recv_sems.at[index])
        else:
            copy = pltpu.make_async_remote_copy(
                src_ref=source,
                dst_ref=target,
                send_sem=self.send_sems.at[index],
                recv_sem=self.recv_sems.at[index],
                device_id=device,
                device_id_type=MESH,
            )
        copy.start()
        return copy


def wait_all(copies):
    for copy in copies:
        copy.wait()


def greet(peers):
    barrier = pltpu.get_barrier_semaphore()
    for peer in peers:
        pl.semaphore_signal(barrier, inc=1, device_id=peer, device_id_type=MESH)
    pl.semaphore_wait(barrier, len(peers))


VMEM = pl.BlockSpec(memory_space=pltpu.VMEM)
SMEM = pl.BlockSpec(memory_space=pltpu.SMEM)
HBM = pl.BlockSpec(memory_space=pltpu.HBM)


def call(body, outs, ins, scratch=(), copies=0, number=None, limit=14):
    more = {} if number is None else {"collective_id": number, "has_side_effects": True}
    semaphores = [pltpu.SemaphoreType.DMA((copies,))] * (0 if not copies else 1 if number is None else 2)
    return pl.pallas_call(
        body,
        out_shape=[array for _, array in outs],
        in_specs=[place for place, _ in ins],
        out_specs=[place for place, _ in outs],
        scratch_shapes=list(scratch) + semaphores,
        compiler_params=pltpu.CompilerParams(vmem_limit_bytes=limit << 20, **more),
    )(*[array for _, array in ins])


def dev(chip, core, section):
    return (chip * 2 + core, section)


def around(chip, step):
    return (chip + step + 16) % 16


def project_body(
    tokens_hbm, gain_ref, w_hbm, w_out_hbm, q_ref, kv_ref, normed_t_hbm, w_full,
    tokens_ref, w_ref, normed_ref, normed_t_ref, out_ref, send, recv,
):
    section, chip, core = place()
    copies = Copies(send, recv)
    load_tokens = copies.start(tokens_hbm, tokens_ref, None)
    load_w = copies.start(w_hbm, w_ref, None)
    greet(halo_peers(section, chip, core) + section_peers(section, chip, core)[::2])
    mate = dev(chip, 1 - core, section)
    ahead, behind = (section + 1) % 4, (section + 3) % 4
    ahead_dev, behind_dev = dev(chip, core, ahead), dev(chip, core, behind)

    def w_rows(owner, start, count):
        return w_full.at[pl.ds(pl.multiple_of(owner * 320 + core * PAIR + start, 16), count), :]

    mine = w_out_hbm.at[pl.ds(pl.multiple_of(core * PAIR, 16), PAIR), :]
    to_ahead = copies.start(mine, w_rows(section, 0, PAIR), ahead_dev)
    to_behind = copies.start(mine, w_rows(section, 0, PAIR), behind_dev)
    keep = w_full.at[pl.ds(pl.multiple_of(section * 320, 16), 320), :]
    waits = [copies.start(w_out_hbm, keep, None)]
    load_tokens.wait()
    gain = gain_ref[...].reshape(1, 1280).astype(F32)
    for tile in range(4):
        rows = pl.ds(tile * 128, 128)
        values = tokens_ref[rows, :].astype(F32)
        centered = values - jnp.mean(values, axis=1, keepdims=True)
        inv = lax.rsqrt(jnp.mean(centered * centered, axis=1, keepdims=True) + EPS)
        normed_ref[rows, :] = (centered * inv * gain).astype(BF16)
    own = pl.ds(pl.multiple_of(core * PAIR, 16), PAIR)
    other = pl.ds(pl.multiple_of((1 - core) * PAIR, 16), PAIR)
    load_w.wait()
    for which in (1, 2, 0):
        out = dot_nt(w_ref[which], normed_ref[...])
        if which == 0:
            out = out * (FACTOR * LOG2E)
        out_ref[which] = out.astype(BF16)
        if which:
            for step, base in ((1, 0), (-1, 2048)):
                lanes = pl.ds(pl.multiple_of(base + core * 512, 512), 512)
                for rows, target in ((own, core), (other, 1 - core)):
                    device = dev(around(chip, step), target, section)
                    waits.append(
                        copies.start(out_ref.at[which, rows, :], kv_ref.at[which - 1, :, lanes], device)
                    )
            lanes = pl.ds(pl.multiple_of(1024 + core * 512, 512), 512)
            target = kv_ref.at[which - 1, :, lanes]
        else:
            target = q_ref.at[:, pl.ds(pl.multiple_of(core * 512, 512), 512)]
        waits.append(copies.start(out_ref.at[which, other, :], target, mate))
        waits.append(copies.start(out_ref.at[which, own, :], target, None))
    for tile in range(4):
        rows = pl.ds(tile * 128, 128)
        normed_t_ref[:, rows] = normed_ref[rows, :].T
    waits.append(copies.start(normed_t_ref, normed_t_hbm, None))

    to_ahead.wait()
    relay = [copies.start(w_rows(behind, 0, 80), w_rows(behind, 0, 80), ahead_dev)]
    to_behind.wait()
    relay.append(copies.start(w_rows(ahead, 80, 80), w_rows(ahead, 80, 80), behind_dev))
    waits.append(copies.start(w_rows(behind, 0, PAIR), w_rows(behind, 0, PAIR), mate))
    waits.append(copies.start(w_rows(ahead, 0, PAIR), w_rows(ahead, 0, PAIR), mate))
    far = (section + 2) % 4
    for copy, start in zip(relay, (0, 80)):
        copy.wait()
        waits.append(copies.start(w_rows(far, start, 80), w_rows(far, start, 80), mate))
    wait_all(waits)


def spans_and_bounds(seg_ref, first, spans_ref, bounds_ref):
    row = lax.broadcasted_iota(jnp.int32, (32, 128), 0)
    begins, ends = jnp.zeros((32, 128), jnp.int32), jnp.zeros((32, 128), jnp.int32)
    end = jnp.int32(0)
    low = [jnp.int32(0)] * 4
    high = [jnp.int32(16384)] * 4
    for image in range(32):
        begin = end
        end = begin + 64 * seg_ref[image]
        begins = jnp.where(row == image, begin, begins)
        ends = jnp.where(row == image, end, ends)
        for tile in range(4):
            start = first + 256 * tile
            low[tile] = jnp.where(begin <= start, begin, low[tile])
            high[tile] = jnp.where((begin < start + 256) & (end >= start + 256), end, high[tile])
    spans_ref[0] = begins
    spans_ref[1] = ends
    for tile in range(4):
        bounds_ref[tile, 0] = (low[tile] - (first - 1024)) // CHUNK
        bounds_ref[tile, 1] = (high[tile] - (first - 1024) + CHUNK - 1) // CHUNK


def membership(spans_ref, first, count):
    spots = first + lax.broadcasted_iota(jnp.int32, (32, count), 1)
    return (spots >= spans_ref[0, :, 0:1]) & (spots < spans_ref[1, :, 0:1])


def three_parts(row):
    high = row.astype(BF16)
    rest = row - high.astype(F32)
    middle = rest.astype(BF16)
    low = (rest - middle.astype(F32)).astype(BF16)
    return jnp.concatenate([high, middle, low, jnp.zeros((13, row.shape[1]), BF16)], axis=0)


def permutation(transposed):
    moved = lax.broadcasted_iota(jnp.int32, (512, 1) if transposed else (1, 512), 0 if transposed else 1)
    natural = lax.broadcasted_iota(jnp.int32, (512, 512), 1 if transposed else 0)
    return jnp.where(natural == 4 * (moved % 128) + moved // 128, 1.0, 0.0).astype(BF16)


def forward_body(
    seg_ref, q_ref, kv_ref, o_hbm, kv_hbm, op_ref, log_ref,
    spans_ref, bounds_ref, o_ref, qrow, kx, vrow, sems,
):
    first = (lax.axis_index("seq") // 2) * 1024
    keep = pltpu.make_async_copy(kv_ref, kv_hbm, sems.at[0])
    keep.start()
    spans_and_bounds(seg_ref, first, spans_ref, bounds_ref)
    longest = []
    for head in range(2):
        feats = pl.ds(head * HEAD_DIM, HEAD_DIM)
        for block in range(4):
            lanes = pl.ds(block * 256, 256)
            inside = membership(spans_ref, first + block * 256, 256)
            joined = jnp.concatenate(
                [
                    q_ref[feats, lanes],
                    jnp.where(inside, 0.0, BIG).astype(BF16),
                    jnp.zeros((16, 256), BF16),
                ],
                axis=0,
            )
            qrow[head, lanes, :] = joined.T
        values = q_ref[feats, :].astype(F32)
        longest.append(jnp.max(jnp.sum(values * values, axis=0, keepdims=True)))

    ones = jnp.where(lax.broadcasted_iota(jnp.int32, (16, CHUNK), 0) < 3, 1.0, 0.0).astype(BF16)

    def build(chunk, tops):
        found = []
        lanes = pl.ds(pl.multiple_of(chunk * CHUNK, CHUNK), CHUNK)
        inside = membership(spans_ref, first - 1024 + chunk * CHUNK, CHUNK)
        hot = jnp.where(inside, 1.0, 0.0).astype(BF16)
        for head in range(2):
            feats = pl.ds(head * HEAD_DIM, HEAD_DIM)
            kx[head, 0:80, lanes] = kv_ref[0, feats, lanes]
            kx[head, 80:112, lanes] = hot
            kx[head, 112:128, lanes] = ones
            joined = jnp.concatenate(
                [kv_ref[1, feats, lanes], ones, jnp.zeros((32, CHUNK), BF16)], axis=0
            )
            vrow[head, lanes, :] = joined.T
            values = kv_ref[0, feats, lanes].astype(F32)
            found.append(jnp.maximum(tops[head], jnp.sum(values * values, axis=0, keepdims=True)))
        return tuple(found)

    start = jnp.zeros((1, CHUNK), F32)
    tops = lax.fori_loop(bounds_ref[0, 0], bounds_ref[3, 1], build, (start, start))
    small = longest[0] * jnp.max(tops[0]) <= SAFE * SAFE
    small = small & (longest[1] * jnp.max(tops[1]) <= SAFE * SAFE)
    lane = lax.broadcasted_iota(jnp.int32, (256, 128), 1)

    def sum_tile(tile, rows):
        def sum_step(chunk, sums):
            lanes = pl.ds(pl.multiple_of(chunk * CHUNK, CHUNK), CHUNK)
            probs = [
                jnp.exp2(dot_nn(qrow[head, rows, :], kx[head, :, lanes])).astype(BF16)
                for head in range(2)
            ]
            return tuple(sums[head] + dot_nn(probs[head], vrow[head, lanes, :]) for head in range(2))

        start = jnp.zeros((256, 128), F32)
        return lax.fori_loop(bounds_ref[tile, 0], bounds_ref[tile, 1], sum_step, (start, start))

    def write(head, rows, sums, top_row):
        out = sums.T
        total_row = out[80:81, :]
        o_ref[pl.ds(head * HEAD_DIM, HEAD_DIM), rows] = (out[:80] * (1.0 / total_row)).astype(BF16)
        log_ref[head : head + 1, rows] = top_row + jnp.log(total_row) * LOG2E

    def plain_step(tile, carry):
        rows = pl.ds(pl.multiple_of(tile * 256, 256), 256)
        sums = sum_tile(tile, rows)
        for head in range(2):
            write(head, rows, sums[head], 0.0)
        return carry

    def shifted_step(tile, carry):
        low, high = bounds_ref[tile, 0], bounds_ref[tile, 1]
        rows = pl.ds(pl.multiple_of(tile * 256, 256), 256)

        def score_step(chunk, tops):
            lanes = pl.ds(pl.multiple_of(chunk * CHUNK, CHUNK), CHUNK)
            found = []
            for head in range(2):
                part = dot_nn(qrow[head, rows, :], kx[head, :, lanes])
                found.append(jnp.maximum(tops[head], jnp.maximum(part[:, :128], part[:, 128:])))
            return tuple(found)

        start = jnp.full((256, 128), BIG, F32)
        tops = lax.fori_loop(low, high, score_step, (start, start))
        for head in range(2):
            shift = -jnp.max(tops[head], axis=1, keepdims=True)
            part_one = shift.astype(BF16).astype(F32)
            part_two = (shift - part_one).astype(BF16).astype(F32)
            part_three = shift - part_one - part_two
            moved = jnp.where(lane == 112, part_one, qrow[head, rows, :].astype(F32))
            moved = jnp.where(lane == 113, part_two, moved)
            qrow[head, rows, :] = jnp.where(lane == 114, part_three, moved).astype(BF16)

        sums = sum_tile(tile, rows)
        for head in range(2):
            write(head, rows, sums[head], jnp.max(tops[head].T, axis=0, keepdims=True))
        return carry

    @pl.when(small)
    def _():
        lax.fori_loop(0, 4, plain_step, 0)

    @pl.when(jnp.logical_not(small))
    def _():
        lax.fori_loop(0, 4, shifted_step, 0)

    keep_o = pltpu.make_async_copy(o_ref, o_hbm, sems.at[1])
    keep_o.start()
    perm = permutation(False)
    for half in range(2):
        moved = dot_nn(o_ref[:, half * 512 : half * 512 + 512], perm).astype(BF16)
        for part in range(4):
            op_ref[half, part] = moved[:, part * 128 : part * 128 + 128]
    keep.wait()
    keep_o.wait()


def build_keys(spans_ref, position, kv_ref, lanes, kx, vx, krow, into):
    ones = jnp.where(lax.broadcasted_iota(jnp.int32, (16, CHUNK), 0) < 3, 1.0, 0.0).astype(BF16)
    hot = jnp.where(membership(spans_ref, position, CHUNK), 1.0, 0.0).astype(BF16)
    for head in range(2):
        feats = pl.ds(head * HEAD_DIM, HEAD_DIM)
        keys = jnp.concatenate([kv_ref[0, feats, lanes], hot, ones], axis=0)
        kx[head, :, into] = keys
        krow[head, into, :] = keys.T
        vx[head, :, into] = jnp.concatenate(
            [kv_ref[1, feats, lanes], ones, jnp.zeros((32, CHUNK), BF16)], axis=0
        )


def backward_step(rows, chunks, q_ref, g_ref, qrow, grow, kx, vx, krow, dk_acc, dv_acc, sums):
    pairs = [(head, lanes) for lanes in chunks for head in range(2)]
    feats = [pl.ds(head * HEAD_DIM, HEAD_DIM) for head in range(2)]
    probs = [jnp.exp2(dot_nn(qrow[head, rows, :], kx[head, :, lanes])) for head, lanes in pairs]
    shifted = [dot_nn(grow[head, rows, :], vx[head, :, lanes]) for head, lanes in pairs]
    dscores = [(prob * part).astype(BF16) for prob, part in zip(probs, shifted)]
    weights = [prob.astype(BF16) for prob in probs]
    dk = [dot_nn(q_ref[feats[head], rows], part) for (head, _), part in zip(pairs, dscores)]
    dv = [dot_nn(g_ref[feats[head], rows], part) for (head, _), part in zip(pairs, weights)]
    sums = list(sums)
    for (head, lanes), part in zip(pairs, dscores):
        sums[head] = sums[head] + dot_nn(part, krow[head, lanes, :])
    for (head, lanes), dk_part, dv_part in zip(pairs, dk, dv):
        dk_acc[head, :, lanes] += dk_part
        dv_acc[head, :, lanes] += dv_part
    return tuple(sums)


def backward_body(
    seg_ref, sizes_ref, receiver_ref, q_ref, kv_hbm, o_hbm, log_ref, gp_ref,
    dq_ref, dkv_ref, starts_ref, here_ref, qrow, grow, gnat, spans_ref,
    bounds_ref, kv_ref, o_ref, kx, vx, krow, dk_acc, dv_acc, sems,
):
    seq = lax.axis_index("seq")
    first = (seq // 2) * 1024
    load_kv = pltpu.make_async_copy(kv_hbm, kv_ref, sems.at[0])
    load_o = pltpu.make_async_copy(o_hbm, o_ref, sems.at[1])
    load_kv.start()
    load_o.start()
    spans_and_bounds(seg_ref, first, spans_ref, bounds_ref)
    start = jnp.int32(0)
    my_start, my_size = jnp.int32(0), jnp.int32(0)
    for batch in range(32):
        size, receiver = sizes_ref[batch], receiver_ref[batch]
        starts_ref[pl.ds(pl.multiple_of(receiver * 16, 16), 16), :] = jnp.full((16, 128), start)
        my_start = jnp.where(receiver == seq, start, my_start)
        my_size = jnp.where(receiver == seq, size, my_size)
        start = start + size
    here_ref[0:8, :] = jnp.full((8, 512), my_start)
    here_ref[8:16, :] = jnp.full((8, 512), my_size)
    back = permutation(True)
    for half in range(2):
        joined = jnp.concatenate([gp_ref[half, part] for part in range(4)], axis=1)
        gnat[:, half * 512 : half * 512 + 512] = dot_nn(joined, back).astype(BF16)
    load_kv.wait()
    load_o.wait()
    for head in range(2):
        feats = pl.ds(head * HEAD_DIM, HEAD_DIM)
        for block in range(4):
            lanes = pl.ds(block * 256, 256)
            inside = membership(spans_ref, first + block * 256, 256)
            joined = jnp.concatenate(
                [
                    q_ref[feats, lanes],
                    jnp.where(inside, 0.0, BIG).astype(BF16),
                    three_parts(-log_ref[head : head + 1, lanes]),
                ],
                axis=0,
            )
            qrow[head, lanes, :] = joined.T
            grads = gnat[feats, lanes]
            delta = jnp.sum(
                grads.astype(F32) * o_ref[feats, lanes].astype(F32), axis=0, keepdims=True
            )
            joined = jnp.concatenate(
                [grads, three_parts(-delta), jnp.zeros((32, 256), BF16)], axis=0
            )
            grow[head, lanes, :] = joined.T

    def outside(low, high, step, carry):
        carry = lax.fori_loop(low, jnp.minimum(high, 4), step, carry)
        return lax.fori_loop(jnp.maximum(low, 8), high, step, carry)

    def place_of(chunk):
        return pl.ds(pl.multiple_of(jnp.where(chunk < 4, chunk, chunk - 4) * CHUNK, CHUNK), CHUNK)

    def build(chunk, carry):
        lanes = pl.ds(pl.multiple_of(chunk * CHUNK, CHUNK), CHUNK)
        build_keys(
            spans_ref, first - 1024 + chunk * CHUNK, kv_ref, lanes, kx, vx, krow, place_of(chunk)
        )
        return carry

    outside(bounds_ref[0, 0], bounds_ref[3, 1], build, 0)
    dk_acc[...] = jnp.zeros_like(dk_acc)
    dv_acc[...] = jnp.zeros_like(dv_acc)

    def tile_step(tile, carry):
        rows = pl.ds(pl.multiple_of(tile * 256, 256), 256)

        def step(chunk, sums):
            return backward_step(
                rows, [place_of(chunk)], q_ref, gnat, qrow, grow, kx, vx, krow, dk_acc, dv_acc, sums
            )

        start = jnp.zeros((256, 128), F32)
        sums = outside(bounds_ref[tile, 0], bounds_ref[tile, 1], step, (start, start))
        for head in range(2):
            dq_ref[head, rows, :] = sums[head]
        return carry

    lax.fori_loop(0, 4, tile_step, 0)
    for head in range(2):
        feats = pl.ds(head * HEAD_DIM, HEAD_DIM)
        dkv_ref[0, feats, :] = (dk_acc[head] * LN2).astype(BF16)
        dkv_ref[1, feats, :] = dv_acc[head].astype(BF16)


def middle_body(
    op_ref, w_hbm, tokens_hbm, mgrad_hbm, gain_ref,
    gp_ref, gl_hbm, glt_hbm, own_ref, table_ref,
    w_ref, tokens_ref, mgrad_ref, gl_ref, glt_ref, att, gat, packed, send, recv,
):
    section, chip, core = place()
    copies = Copies(send, recv)
    columns = pl.ds(pl.multiple_of(section * 1280, 128), 1280)
    load_mgrad = copies.start(mgrad_hbm.at[:, columns], mgrad_ref, None)
    load_tokens = copies.start(tokens_hbm, tokens_ref, None)
    load_w = copies.start(w_hbm, w_ref, None)
    greet(row_peers(section, chip, core) + core_peers(section, chip, core))
    rows = pl.ds(pl.multiple_of((section * 2 + core) * PAIR, 16), PAIR)
    waits = []
    for step in (2, 1, 3, 0):
        for turn in range(2):
            to_section, to_core = (section + step) % 4, (core + turn) % 2
            device = dev(chip, to_core, to_section) if step or turn else None
            waits.append(copies.start(op_ref.at[to_core, to_section], att.at[rows, :], device))
    late = [
        copies.start(op_ref.at[1 - core], own_ref.at[core], dev(chip, 1 - core, section)),
        copies.start(op_ref.at[core], own_ref.at[core], None),
    ]
    row = lax.broadcasted_iota(jnp.int32, (128, 512), 0)
    column = lax.broadcasted_iota(jnp.int32, (128, 512), 1)
    chosen = jnp.where(column == 4 * row + section, 1.0, 0.0).astype(BF16)
    load_tokens.wait()
    load_mgrad.wait()
    values = dot_nn(chosen, tokens_ref[...])
    gain = gain_ref[...].reshape(1, 1280).astype(F32)
    scaled = mgrad_ref[...].astype(F32) * gain
    scaled_mean = jnp.mean(scaled, axis=1, keepdims=True)
    row = lax.broadcasted_iota(jnp.int32, (128, 128), 0)
    column = lax.broadcasted_iota(jnp.int32, (128, 128), 1)
    order = jnp.where(column == 16 * (row % 8) + row // 8, 1.0, 0.0).astype(BF16)
    load_w.wait()
    wait_all(waits)
    layer = values + dot_nn(att[...].T, w_ref[...])
    centered = layer - jnp.mean(layer, axis=1, keepdims=True)
    inv = lax.rsqrt(jnp.mean(centered * centered, axis=1, keepdims=True) + EPS)
    unit = centered * inv
    grad_layer = inv * (
        scaled - scaled_mean - unit * jnp.mean(scaled * unit, axis=1, keepdims=True)
    )
    grad_layer = grad_layer.astype(BF16)
    gat[...] = dot_nt(w_ref[...], grad_layer).astype(BF16)
    for step in (2, 1, 3, 0):
        for turn in range(2):
            to_section, to_core = (section + step) % 4, (core + turn) % 2
            device = dev(chip, to_core, to_section) if step or turn else None
            rows = pl.ds(pl.multiple_of((to_section * 2 + to_core) * PAIR, 16), PAIR)
            late.append(copies.start(gat.at[rows, :], gp_ref.at[core, section], device))
    moved = dot_nn(order, (unit * gain).astype(BF16))
    for chip_to in range(16):
        eight = moved[chip_to * 8 : chip_to * 8 + 8]
        packed[chip_to] = jnp.concatenate([eight[:, :640], eight[:, 640:]], axis=0).astype(BF16)
    for step in range(16):
        to_chip = (chip + step) % 16
        device = dev(to_chip, core, section) if step else None
        late.append(copies.start(packed.at[to_chip], table_ref.at[chip], device))
    gl_ref[...] = grad_layer
    glt_ref[...] = grad_layer.T
    late.append(copies.start(gl_ref, gl_hbm, None))
    late.append(copies.start(glt_ref, glt_hbm, None))
    wait_all(late)


def tail_body(
    dkv_ref, starts_ref, live_ref, dq_ref, qrow, grow, gnat, spans_ref, q_ref, kv_hbm,
    glt_hbm, own_hbm, table_hbm, gl_hbm, tokens_hbm, gain_ref, w_hbm, normed_t_hbm,
    delivered_ref, gx_all, weights_ref,
    table_ref, gl_ref, tokens_ref, w_ref, normed_t_ref,
    kv_ref, kx, vx, krow, dk_acc, dv_acc, dq_acc, own_out, mate_in,
    dkv_in, dj, rows_ref, gn, gn_in, gx_own, att, glt,
    parcels, arrived, p_mine, p_away, p_in,
    sum_a, sum_b, in_a, in_b, sub_a, sub_b, late_a, late_b, total, send, recv,
):
    section, chip, core = place()
    y, z = chip // 4, chip % 4
    copies = Copies(send, recv)
    mate = dev(chip, 1 - core, section)
    greet(plane_peers(section, chip, core) + section_peers(section, chip, core))
    back = []
    for half in range(2):
        waits = []
        for step, base, slot in ((-1, 0, 0), (1, 1024, 1)):
            for target in (core, 1 - core):
                lanes = pl.ds(pl.multiple_of(base + target * 512 + half * 256, 256), 256)
                device = dev(around(chip, step), target, section)
                waits.append(
                    copies.start(dkv_ref.at[:, :, lanes], dkv_in.at[half, slot, core], device)
                )
        back.append(waits)
    gathered = []
    lanes = pl.ds(pl.multiple_of(section * 128, 128), 128)
    for step in (2, 1, 3, 0):
        device = dev(chip, core, (section + step) % 4) if step else None
        gathered.append(copies.start(glt_hbm, glt.at[:, lanes], device))
    load_kv = copies.start(kv_hbm.at[:, :, 1024:2048], kv_ref, None)
    load_table = copies.start(table_hbm, table_ref, None)
    load_w = copies.start(w_hbm, w_ref, None)
    loads = [
        copies.start(source, target, None)
        for source, target in (
            (normed_t_hbm, normed_t_ref), (tokens_hbm, tokens_ref), (gl_hbm, gl_ref)
        )
    ]
    for head in range(2):
        for part in range(4):
            target = att.at[head * PAIR : head * PAIR + PAIR, part * 128 : part * 128 + 128]
            loads.append(copies.start(own_hbm.at[head, part], target, None))

    load_kv.wait()
    for chunk in range(4):
        lanes = pl.ds(chunk * CHUNK, CHUNK)
        build_keys(
            spans_ref, chip * 1024 + chunk * CHUNK, kv_ref, lanes, kx, vx, krow, lanes
        )
    dk_acc[...] = jnp.zeros_like(dk_acc)
    dv_acc[...] = jnp.zeros_like(dv_acc)
    dq_acc[...] = dq_ref[...]

    def own_step(tile, group):
        rows = pl.ds(pl.multiple_of(tile * 256, 256), 256)
        chunks = [pl.ds((group + 2 * which) * CHUNK, CHUNK) for which in range(2)]
        sums = backward_step(
            rows, chunks, q_ref, gnat, qrow, grow, kx, vx, krow, dk_acc, dv_acc,
            (dq_acc[0, rows, :], dq_acc[1, rows, :]),
        )
        for head in range(2):
            dq_acc[head, rows, :] = sums[head]

    def finish_own(half):
        for of_core in range(2):
            lanes = pl.ds(of_core * 512 + half * 256, 256)
            for head in range(2):
                feats = pl.ds(head * HEAD_DIM, HEAD_DIM)
                part = dq_acc[head, lanes, :].T[:80] * FACTOR
                own_out[half, of_core, 0, feats, :] = part.astype(BF16)
                own_out[half, of_core, 1, feats, :] = (dk_acc[head, :, lanes] * LN2).astype(BF16)
                own_out[half, of_core, 2, feats, :] = dv_acc[head, :, lanes].astype(BF16)
        back[half].append(copies.start(own_out.at[half, 1 - core], mate_in.at[half], mate))

    def first_step(tile, carry):
        own_step(tile, 0)
        return carry

    def even_step(index, carry):
        own_step(index * 2, 1)
        return carry

    def odd_step(index, carry):
        own_step(index * 2 + 1, 1)
        return carry

    lax.fori_loop(0, 4, first_step, 0)
    lax.fori_loop(0, 2, even_step, 0)
    finish_own(0)
    lax.fori_loop(0, 2, odd_step, 0)
    finish_own(1)

    begin = starts_ref[:, 0:1]
    block, offset = begin // 128, begin % 128
    first = 8 * ((block + 1 - core) // 2)
    first = first + jnp.where(block % 2 == core, (offset - chip + 15) // 16, 0)
    out_row = lax.broadcasted_iota(jnp.int32, (512, 256), 0)
    in_row = lax.broadcasted_iota(jnp.int32, (512, 256), 1)
    wanted = first + out_row % 8
    wanted = (wanted // 8) * 16 + wanted % 8 + 8 * ((out_row // 8) % 2)
    hot = jnp.where(in_row == wanted, 1.0, 0.0).astype(BF16)
    load_table.wait()
    table = table_ref[...].reshape(256, 640)
    parcels[...] = dot_nn(hot, table).astype(BF16).reshape(32, 16, 640)

    row = lax.broadcasted_iota(jnp.int32, (256, 256), 0)
    column = lax.broadcasted_iota(jnp.int32, (256, 256), 1)
    by_part = jnp.where(column == 4 * (row % 64) + row // 64, 1.0, 0.0).astype(BF16)
    load_w.wait()
    w_all = w_ref[...].reshape(960, 1280)
    sums = []
    for half in range(2):
        wait_all(back[half])
        lanes = pl.ds(half * 256, 256)
        for near, head in ((True, core), (False, 1 - core)):
            for which in range(3):
                grad = own_out[half, core, which] if near else mate_in[half, which]
                if which:
                    grad = grad.astype(F32) + dkv_in[half, 0, head, which - 1].astype(F32)
                    grad = (grad + dkv_in[half, 1, head, which - 1].astype(F32)).astype(BF16)
                dj[pl.ds(pl.multiple_of(320 * which + head * PAIR, 16), PAIR), lanes] = grad
        rows_ref[...] = dot_nt(by_part, dj[:, lanes]).astype(BF16)
        gn[half] = dot_nn(rows_ref[...], w_all).astype(BF16).reshape(4, 64, 1280)
        waits = []
        for step in (2, 1, 3):
            to_section = (section + step) % 4
            device = dev(chip, core, to_section)
            waits.append(copies.start(gn.at[half, to_section], gn_in.at[half, step - 1], device))
        sums.append(waits)

    deliveries = []
    for step in range(16):
        for turn in range(2):
            to_chip, to_core = (chip + step) % 16, (core + turn) % 2
            device = dev(to_chip, to_core, section) if step or turn else None
            deliveries.append(
                copies.start(parcels.at[to_chip * 2 + to_core], arrived.at[chip * 2 + core], device)
            )

    def products(index, core_of):
        rows = pl.ds(index * 320, 320)
        normed = normed_t_ref[rows, :]
        if core_of == 0:
            return dot_nt(normed, dj[0:640, :])
        return jnp.concatenate(
            [dot_nt(normed, dj[640:960, :]), dot_nt(glt[rows, :], att[...])], axis=1
        )

    wait_all(gathered)
    wait_all(loads)
    pairs = []
    for index in range(4):
        for core_of in range(2):
            @pl.when(core != core_of)
            def _():
                p_away[index] = products(index, core_of).astype(BF16).reshape(4, 80, 640)

        pairs.append(copies.start(p_away.at[index], p_in.at[index], mate))
    for index in range(4):
        for core_of in range(2):
            @pl.when(core == core_of)
            def _():
                p_mine[index] = products(index, core_of).reshape(4, 80, 640)

    gathers = []

    def finish_norm(half):
        row = lax.broadcasted_iota(jnp.int32, (64, 256), 0)
        column = lax.broadcasted_iota(jnp.int32, (64, 256), 1)
        chosen = jnp.where(column == 4 * row + section, 1.0, 0.0).astype(BF16)
        values = dot_nn(chosen, tokens_ref[half * 256 : half * 256 + 256, :])
        centered = values - jnp.mean(values, axis=1, keepdims=True)
        inv = lax.rsqrt(jnp.mean(centered * centered, axis=1, keepdims=True) + EPS)
        unit = centered * inv
        wait_all(sums[half])
        grad = gn[half, section].astype(F32) + gn_in[half, 0].astype(F32)
        grad = grad + (gn_in[half, 1].astype(F32) + gn_in[half, 2].astype(F32))
        scaled = grad * gain_ref[...].reshape(1, 1280).astype(F32)
        grad = inv * (
            scaled
            - jnp.mean(scaled, axis=1, keepdims=True)
            - unit * jnp.mean(scaled * unit, axis=1, keepdims=True)
        )
        grad = grad + gl_ref[half * 64 : half * 64 + 64, :].astype(F32)
        gx_own[half] = grad.astype(BF16)
        waits = []
        for step in (2, 1, 3, 0):
            device = dev(chip, core, (section + step) % 4) if step else None
            waits.append(copies.start(gx_own.at[half], gx_all.at[half, section], device))
        gathers.append(waits)

    finish_norm(0)
    firsts = [[], []]
    for index in range(4):
        pairs[index].wait()
        summed = (p_mine[index] + p_in[index].astype(F32)).astype(BF16)
        sum_a[index] = summed[:, :, :384]
        sum_b[index] = summed[:, :, 384:]
    for step in (2, 1, 3):
        to_z, to_y = (z + step) % 4, (y + step) % 4
        device = dev(y * 4 + to_z, core, section)
        firsts[0].append(copies.start(sum_a.at[:, to_z], in_a.at[step - 1], device))
        device = dev(to_y * 4 + z, core, section)
        firsts[1].append(copies.start(sum_b.at[to_y], in_b.at[step - 1], device))
    finish_norm(1)
    seconds = []
    wait_all(firsts[1])
    grad = sum_b[y].astype(F32) + in_b[0].astype(F32)
    sub_b[...] = (grad + (in_b[1].astype(F32) + in_b[2].astype(F32))).astype(BF16)
    for step in (2, 1, 3):
        to_z = (z + step) % 4
        device = dev(y * 4 + to_z, core, section)
        seconds.append(copies.start(sub_b.at[to_z], late_b.at[step - 1], device))
    wait_all(firsts[0])
    for index in range(4):
        grad = sum_a[index, z].astype(F32) + in_a[0, index].astype(F32)
        grad = grad + (in_a[1, index].astype(F32) + in_a[2, index].astype(F32))
        sub_a[index] = grad.astype(BF16)
    for step in (2, 1, 3):
        to_y = (y + step) % 4
        device = dev(to_y * 4 + z, core, section)
        seconds.append(copies.start(sub_a.at[to_y], late_a.at[step - 1], device))

    lane = lax.broadcasted_iota(jnp.int32, (1, 512), 1)
    from_chip, from_core, side, number = lane // 32, (lane // 16) % 2, (lane // 8) % 2, lane % 8
    begin, live = live_ref[0:1, :], live_ref[8:9, :]
    block, offset = begin // 128, begin % 128
    spot = 8 * ((block + 1 - from_core) // 2) + number
    spot = spot + jnp.where(block % 2 == from_core, (offset - from_chip + 15) // 16, 0)
    slot = (2 * (spot // 8) + from_core) * 128 + 16 * (spot % 8) + from_chip - begin
    out_row = lax.broadcasted_iota(jnp.int32, (256, 512), 0)
    taken = (out_row == slot) & (out_row < live)
    wait_all(deliveries)
    rows = arrived[...].reshape(512, 640)
    for which in range(2):
        hot = jnp.where(taken & (side == which), 1.0, 0.0).astype(BF16)
        delivered_ref[:, which * 640 : which * 640 + 640] = dot_nn(hot, rows).astype(BF16)

    wait_all(seconds)
    grad = sub_a[y].astype(F32) + late_a[0].astype(F32)
    total[:, :384] = grad + (late_a[1].astype(F32) + late_a[2].astype(F32))
    grad = sub_b[z].astype(F32) + late_b[0].astype(F32)
    total[:, 384:] = grad + (late_b[1].astype(F32) + late_b[2].astype(F32))
    lasts = []
    for target, device in ((1 - core, mate), (core, None)):
        rows = pl.ds(pl.multiple_of(target * 40, 8), 40)
        lasts.append(copies.start(total.at[rows, :], weights_ref.at[core], device))
    wait_all(lasts)
    for waits in gathers:
        wait_all(waits)


def results_body(gx_ref, both_ref, arrived_ref, gx_out, w_qkv_out, w_out_out, delivered_out):
    row = lax.broadcasted_iota(jnp.int32, (256, 256), 0)
    column = lax.broadcasted_iota(jnp.int32, (256, 256), 1)
    natural = jnp.where(row == 4 * (column % 64) + column // 64, 1.0, 0.0).astype(BF16)
    for half in range(2):
        rows = gx_ref[half].reshape(256, 1280)
        gx_out[half * 256 : half * 256 + 256, :] = dot_nn(natural, rows).astype(BF16)
    w_qkv_out[0] = both_ref[0, :, :320]
    w_qkv_out[1] = both_ref[0, :, 320:]
    w_qkv_out[2] = both_ref[1, :, :320]
    w_out_out[...] = both_ref[1, :, 320:]
    delivered_out[...] = arrived_ref[...]


def halo_peers(section, chip, core):
    found = [dev(chip, 1 - core, section)]
    for step in (1, -1):
        for other in (core, 1 - core):
            found.append(dev(around(chip, step), other, section))
    return found


def row_peers(section, chip, core):
    found = []
    for step in range(4):
        for turn in range(2):
            if step or turn:
                found.append(dev(chip, (core + turn) % 2, (section + step) % 4))
    return found


def section_peers(section, chip, core):
    return [dev(chip, core, (section + step) % 4) for step in range(1, 4)]


def core_peers(section, chip, core):
    return [dev((chip + step) % 16, core, section) for step in range(1, 16)]


def plane_peers(section, chip, core):
    found = [dev(chip, 1 - core, section)]
    for step in range(1, 16):
        for turn in range(2):
            found.append(dev((chip + step) % 16, (core + turn) % 2, section))
    return found


def local(
    tokens, norm_gain, w_qkv, w_out, merge_gain, seg_blocks, mb_sizes, mb_receiver, merged_grad
):
    w_rows = w_qkv.transpose(0, 2, 1)
    q, kv, normed_t, w_full = call(
        project_body,
        [
            (VMEM, shape((PAIR, 1024))),
            (VMEM, shape((2, PAIR, 3072))),
            (HBM, shape((1280, 512))),
            (HBM, shape((1280, 1280))),
        ],
        [(HBM, tokens), (VMEM, norm_gain), (HBM, w_rows), (HBM, w_out)],
        [
            pltpu.VMEM((512, 1280), BF16),
            pltpu.VMEM((3, 320, 1280), BF16),
            pltpu.VMEM((512, 1280), BF16),
            pltpu.VMEM((1280, 512), BF16),
            pltpu.VMEM((3, 320, 512), BF16),
        ],
        copies=32,
        number=1,
        limit=20,
    )
    o, kv_kept, op, log_total = call(
        forward_body,
        [
            (HBM, shape((PAIR, 1024))),
            (HBM, shape((2, PAIR, 3072))),
            (VMEM, shape((2, 4, PAIR, 128))),
            (VMEM, shape((2, 1024), F32)),
        ],
        [(SMEM, seg_blocks), (VMEM, q), (VMEM, kv)],
        [
            pltpu.VMEM((2, 32, 128), jnp.int32),
            pltpu.SMEM((4, 2), jnp.int32),
            pltpu.VMEM((PAIR, 1024), BF16),
            pltpu.VMEM((2, 1024, 128), BF16),
            pltpu.VMEM((2, 128, 3072), BF16),
            pltpu.VMEM((2, 3072, 128), BF16),
        ],
        copies=2,
        limit=16,
    )
    gp, grad_layer, glt, att_own, table = call(
        middle_body,
        [
            (VMEM, shape((2, 4, PAIR, 128))),
            (HBM, shape((128, 1280))),
            (HBM, shape((1280, 128))),
            (HBM, shape((2, 4, PAIR, 128))),
            (HBM, shape((16, 16, 640))),
        ],
        [(VMEM, op), (HBM, w_full), (HBM, tokens), (HBM, merged_grad), (VMEM, merge_gain)],
        [
            pltpu.VMEM((1280, 1280), BF16),
            pltpu.VMEM((512, 1280), BF16),
            pltpu.VMEM((128, 1280), BF16),
            pltpu.VMEM((128, 1280), BF16),
            pltpu.VMEM((1280, 128), BF16),
            pltpu.VMEM((1280, 128), BF16),
            pltpu.VMEM((1280, 128), BF16),
            pltpu.VMEM((16, 16, 640), BF16),
        ],
        copies=40,
        number=2,
        limit=20,
    )
    dq, dkv, start_rows, here, qrow, grow, gnat, spans = call(
        backward_body,
        [
            (VMEM, shape((2, 1024, 128), F32)),
            (VMEM, shape((2, PAIR, 2048))),
            (VMEM, shape((512, 128), jnp.int32)),
            (VMEM, shape((16, 512), jnp.int32)),
            (VMEM, shape((2, 1024, 128))),
            (VMEM, shape((2, 1024, 128))),
            (VMEM, shape((PAIR, 1024))),
            (VMEM, shape((2, 32, 128), jnp.int32)),
        ],
        [
            (SMEM, seg_blocks), (SMEM, mb_sizes), (SMEM, mb_receiver),
            (VMEM, q), (HBM, kv_kept), (HBM, o), (VMEM, log_total), (VMEM, gp),
        ],
        [
            pltpu.SMEM((4, 2), jnp.int32),
            pltpu.VMEM((2, PAIR, 3072), BF16),
            pltpu.VMEM((PAIR, 1024), BF16),
            pltpu.VMEM((2, 128, 2048), BF16),
            pltpu.VMEM((2, 128, 2048), BF16),
            pltpu.VMEM((2, 2048, 128), BF16),
            pltpu.VMEM((2, HEAD_DIM, 2048), F32),
            pltpu.VMEM((2, HEAD_DIM, 2048), F32),
        ],
        copies=2,
        limit=22,
    )
    arrived, gx_all, weights = call(
        tail_body,
        [
            (VMEM, shape((256, 1280))),
            (VMEM, shape((2, 4, 64, 1280))),
            (VMEM, shape((2, 40, 640), F32)),
        ],
        [
            (VMEM, dkv), (VMEM, start_rows), (VMEM, here), (VMEM, dq), (VMEM, qrow), (VMEM, grow),
            (VMEM, gnat), (VMEM, spans), (VMEM, q), (HBM, kv_kept), (HBM, glt), (HBM, att_own),
            (HBM, table), (HBM, grad_layer), (HBM, tokens), (VMEM, norm_gain), (HBM, w_rows),
            (HBM, normed_t),
        ],
        [
            pltpu.VMEM((16, 16, 640), BF16),
            pltpu.VMEM((128, 1280), BF16),
            pltpu.VMEM((512, 1280), BF16),
            pltpu.VMEM((3, 320, 1280), BF16),
            pltpu.VMEM((1280, 512), BF16),
            pltpu.VMEM((2, PAIR, 1024), BF16),
            pltpu.VMEM((2, 128, 1024), BF16),
            pltpu.VMEM((2, 128, 1024), BF16),
            pltpu.VMEM((2, 1024, 128), BF16),
            pltpu.VMEM((2, HEAD_DIM, 1024), F32),
            pltpu.VMEM((2, HEAD_DIM, 1024), F32),
            pltpu.VMEM((2, 1024, 128), F32),
            pltpu.VMEM((2, 2, 3, PAIR, 256), BF16),
            pltpu.VMEM((2, 3, PAIR, 256), BF16),
            pltpu.VMEM((2, 2, 2, 2, PAIR, 256), BF16),
            pltpu.VMEM((960, 512), BF16),
            pltpu.VMEM((256, 960), BF16),
            pltpu.VMEM((2, 4, 64, 1280), BF16),
            pltpu.VMEM((2, 3, 64, 1280), BF16),
            pltpu.VMEM((2, 64, 1280), BF16),
            pltpu.VMEM((320, 512), BF16),
            pltpu.VMEM((1280, 512), BF16),
            pltpu.VMEM((32, 16, 640), BF16),
            pltpu.VMEM((32, 16, 640), BF16),
            pltpu.VMEM((4, 4, 80, 640), F32),
            pltpu.VMEM((4, 4, 80, 640), BF16),
            pltpu.VMEM((4, 4, 80, 640), BF16),
            pltpu.VMEM((4, 4, 80, 384), BF16),
            pltpu.VMEM((4, 4, 80, 256), BF16),
            pltpu.VMEM((3, 4, 80, 384), BF16),
            pltpu.VMEM((3, 4, 80, 256), BF16),
            pltpu.VMEM((4, 80, 384), BF16),
            pltpu.VMEM((4, 80, 256), BF16),
            pltpu.VMEM((3, 80, 384), BF16),
            pltpu.VMEM((3, 80, 256), BF16),
            pltpu.VMEM((80, 640), F32),
        ],
        copies=112,
        number=3,
        limit=48,
    )
    grad_x, grad_w_qkv, grad_w_out, delivered = call(
        results_body,
        [
            (VMEM, shape((512, 1280))),
            (VMEM, shape((3, 40, 320), F32)),
            (VMEM, shape((40, 320), F32)),
            (VMEM, shape((256, 1280))),
        ],
        [(VMEM, gx_all), (VMEM, weights), (VMEM, arrived)],
        limit=14,
    )
    return (delivered, grad_x, grad_w_qkv, grad_w_out.T)


def solution(mesh):
    placed = (
        P("seq", None),
        P(),
        P(None, None, "section"),
        P("section", None),
        P(),
        P(),
        P(),
        P(),
        P("seq", None),
    )
    return jax.shard_map(
        local,
        mesh=mesh,
        in_specs=placed,
        out_specs=(
            P("seq", "section"),
            P("seq", None),
            P(None, "seq", "section"),
            P("section", "seq"),
        ),
        check_vma=False,
    )
```

```python
import math

import jax
import jax.numpy as jnp
from jax import lax
from jax.experimental import pallas as pl
from jax.experimental.pallas import tpu as pltpu
from jax.sharding import PartitionSpec as P

HEADS = 16
EPS = 1e-06
HEAD_DIM = 80
PAIR = 160
BIG = -1e30
CHUNK = 256
SAFE = 60.0
BF16 = jnp.bfloat16
F32 = jnp.float32
MESH = pl.DeviceIdType.MESH
FACTOR = HEAD_DIM ** -0.5
LOG2E = 1.0 / math.log(2.0)
LN2 = math.log(2.0)


def dot_nn(left, right):
    return lax.dot_general(left, right, (((1,), (0,)), ((), ())), preferred_element_type=F32)


def dot_nt(left, right):
    return lax.dot_general(left, right, (((1,), (1,)), ((), ())), preferred_element_type=F32)


def place():
    section = lax.axis_index("section")
    seq = lax.axis_index("seq")
    return section, seq // 2, seq % 2


def shape(dims, dtype=BF16):
    return jax.ShapeDtypeStruct(dims, dtype)


class Copies:
    def __init__(self, send_sems, recv_sems):
        self.send_sems, self.recv_sems, self.used = send_sems, recv_sems, 0

    def start(self, source, target, device):
        index = self.used
        self.used = index + 1
        if device is None:
            copy = pltpu.make_async_copy(source, target, self.recv_sems.at[index])
        else:
            copy = pltpu.make_async_remote_copy(
                src_ref=source,
                dst_ref=target,
                send_sem=self.send_sems.at[index],
                recv_sem=self.recv_sems.at[index],
                device_id=device,
                device_id_type=MESH,
            )
        copy.start()
        return copy


def wait_all(copies):
    for copy in copies:
        copy.wait()


def greet(peers):
    barrier = pltpu.get_barrier_semaphore()
    for peer in peers:
        pl.semaphore_signal(barrier, inc=1, device_id=peer, device_id_type=MESH)
    pl.semaphore_wait(barrier, len(peers))


VMEM = pl.BlockSpec(memory_space=pltpu.VMEM)
SMEM = pl.BlockSpec(memory_space=pltpu.SMEM)
HBM = pl.BlockSpec(memory_space=pltpu.HBM)


def call(body, outs, ins, scratch=(), copies=0, number=None, limit=14):
    more = {} if number is None else {"collective_id": number, "has_side_effects": True}
    semaphores = [pltpu.SemaphoreType.DMA((copies,))] * (0 if not copies else 1 if number is None else 2)
    return pl.pallas_call(
        body,
        out_shape=[array for _, array in outs],
        in_specs=[place for place, _ in ins],
        out_specs=[place for place, _ in outs],
        scratch_shapes=list(scratch) + semaphores,
        compiler_params=pltpu.CompilerParams(vmem_limit_bytes=limit << 20, **more),
    )(*[array for _, array in ins])


def dev(chip, core, section):
    return (chip * 2 + core, section)


def around(chip, step):
    return (chip + step + 16) % 16


def project_body(
    seg_ref, tokens_hbm, gain_hbm, w_hbm, w_out_hbm,
    q_hbm, kv_hbm, normed_t_hbm, w_full, qrow_hbm, sums_hbm, norms_hbm,
    tokens_ref, gain_ref, w_ref, normed_t_ref, out_ref,
    q_ref, kv_ref, spans_ref, qrow, kx, vrow, sums_ref, norms_ref, send, recv,
):
    section, chip, core = place()
    copies = Copies(send, recv)
    load_tokens = copies.start(tokens_hbm, tokens_ref, None)
    load_w = copies.start(w_hbm, w_ref, None)
    load_gain = copies.start(gain_hbm, gain_ref, None)
    greet(halo_peers(section, chip, core) + section_peers(section, chip, core)[::2])
    mate = dev(chip, 1 - core, section)
    ahead, behind = (section + 1) % 4, (section + 3) % 4
    ahead_dev, behind_dev = dev(chip, core, ahead), dev(chip, core, behind)

    def w_rows(owner, start, count):
        return w_full.at[pl.ds(pl.multiple_of(owner * 320 + core * PAIR + start, 16), count), :]

    mine = w_out_hbm.at[pl.ds(pl.multiple_of(core * PAIR, 16), PAIR), :]
    to_ahead = copies.start(mine, w_rows(section, 0, PAIR), ahead_dev)
    to_behind = copies.start(mine, w_rows(section, 0, PAIR), behind_dev)
    waits, inner = [], []
    image_spans(seg_ref, spans_ref)
    load_tokens.wait()
    load_gain.wait()
    gain = gain_ref[...].reshape(1, 1280).astype(F32)
    for tile in range(4):
        rows = pl.ds(tile * 128, 128)
        values = tokens_ref[rows, :].astype(F32)
        centered = values - jnp.mean(values, axis=1, keepdims=True)
        inv = lax.rsqrt(jnp.mean(centered * centered, axis=1, keepdims=True) + EPS)
        normed_t_ref[:, rows] = (centered * inv * gain).astype(BF16).T
    own = pl.ds(pl.multiple_of(core * PAIR, 16), PAIR)
    other = pl.ds(pl.multiple_of((1 - core) * PAIR, 16), PAIR)
    load_w.wait()
    for which in (1, 2, 0):
        out = dot_nn(w_ref[which], normed_t_ref[...])
        if which == 0:
            out = out * (FACTOR * LOG2E)
        out_ref[which] = out.astype(BF16)
        mine = pl.ds(pl.multiple_of(core * 512, 512), 512)
        target = q_ref.at[:, mine]
        if which:
            for step, base in ((1, 0), (-1, 2048)):
                lanes = pl.ds(pl.multiple_of(base + core * 512, 512), 512)
                for rows, to_core in ((own, core), (other, 1 - core)):
                    device = dev(around(chip, step), to_core, section)
                    waits.append(
                        copies.start(out_ref.at[which, rows, :], kv_hbm.at[which - 1, :, lanes], device)
                    )
            target = kv_ref.at[which - 1, :, mine]
        inner.append(copies.start(out_ref.at[which, other, :], target, mate))
        inner.append(copies.start(out_ref.at[which, own, :], target, None))
    waits.append(copies.start(normed_t_ref, normed_t_hbm, None))
    wait_all(inner)
    waits.append(copies.start(q_ref, q_hbm, None))
    waits.append(copies.start(kv_ref, kv_hbm.at[:, :, 1024:2048], None))
    first = chip * 1024
    for block in range(4):
        lanes = pl.ds(block * 256, 256)
        build_queries(spans_ref, first + block * 256, q_ref, lanes, qrow)
        build_values(spans_ref, first + block * 256, kv_ref, lanes, kx, vrow, lanes)
    for head in range(2):
        feats = pl.ds(head * HEAD_DIM, HEAD_DIM)
        for which, values in enumerate((q_ref[feats, :], kv_ref[0, feats, :])):
            norms_ref[which * 2 + head, :, :] = squares(values)

    def tile_step(tile, carry):
        rows = pl.ds(pl.multiple_of(tile * 256, 256), 256)
        sums = (jnp.zeros((256, 128), F32),) * 2
        for chunk in range(0, 4, 2):
            lanes = [pl.ds((chunk + which) * CHUNK, CHUNK) for which in range(2)]
            sums = forward_step(rows, lanes, qrow, kx, vrow, sums)
        for head in range(2):
            sums_ref[head, rows, :] = sums[head]
        return carry

    lax.fori_loop(0, 2, tile_step, 0)
    to_ahead.wait()
    relay = [copies.start(w_rows(behind, 0, 80), w_rows(behind, 0, 80), ahead_dev)]
    to_behind.wait()
    relay.append(copies.start(w_rows(ahead, 80, 80), w_rows(ahead, 80, 80), behind_dev))
    waits.append(copies.start(w_rows(behind, 0, PAIR), w_rows(behind, 0, PAIR), mate))
    waits.append(copies.start(w_rows(ahead, 0, PAIR), w_rows(ahead, 0, PAIR), mate))
    lax.fori_loop(2, 4, tile_step, 0)
    waits.append(copies.start(qrow, qrow_hbm, None))
    waits.append(copies.start(sums_ref, sums_hbm, None))
    waits.append(copies.start(norms_ref, norms_hbm, None))
    far = (section + 2) % 4
    for copy, start in zip(relay, (0, 80)):
        copy.wait()
        waits.append(copies.start(w_rows(far, start, 80), w_rows(far, start, 80), mate))
    wait_all(waits)


def image_spans(seg_ref, spans_ref):
    row = lax.broadcasted_iota(jnp.int32, (32, 128), 0)
    begins, ends = jnp.zeros((32, 128), jnp.int32), jnp.zeros((32, 128), jnp.int32)
    end = jnp.int32(0)
    for image in range(32):
        begin = end
        end = begin + 64 * seg_ref[image]
        begins = jnp.where(row == image, begin, begins)
        ends = jnp.where(row == image, end, ends)
    spans_ref[0] = begins
    spans_ref[1] = ends


def squares(values):
    values = values.astype(F32)
    total = jnp.sum(values * values, axis=0, keepdims=True)
    blocks = [total[:, start : start + 128] for start in range(0, total.shape[1], 128)]
    top = blocks[0]
    for block in blocks[1:]:
        top = jnp.maximum(top, block)
    return jnp.broadcast_to(top, (8, 128))


def build_queries(spans_ref, position, q_ref, lanes, qrow):
    inside = membership(spans_ref, position, 256)
    for head in range(2):
        joined = jnp.concatenate(
            [
                q_ref[pl.ds(head * HEAD_DIM, HEAD_DIM), lanes],
                jnp.where(inside, 0.0, BIG).astype(BF16),
                jnp.zeros((16, 256), BF16),
            ],
            axis=0,
        )
        qrow[head, lanes, :] = joined.T


def build_values(spans_ref, position, kv_ref, lanes, kx, vrow, into):
    ones = jnp.where(lax.broadcasted_iota(jnp.int32, (16, CHUNK), 0) < 3, 1.0, 0.0).astype(BF16)
    hot = jnp.where(membership(spans_ref, position, CHUNK), 1.0, 0.0).astype(BF16)
    for head in range(2):
        feats = pl.ds(head * HEAD_DIM, HEAD_DIM)
        kx[head, :, into] = jnp.concatenate([kv_ref[0, feats, lanes], hot, ones], axis=0)
        joined = jnp.concatenate(
            [kv_ref[1, feats, lanes], ones, jnp.zeros((32, CHUNK), BF16)], axis=0
        )
        vrow[head, into, :] = joined.T


def forward_step(rows, chunks, qrow, kx, vrow, sums):
    pairs = [(head, lanes) for lanes in chunks for head in range(2)]
    probs = [
        jnp.exp2(dot_nn(qrow[head, rows, :], kx[head, :, lanes])).astype(BF16)
        for head, lanes in pairs
    ]
    sums = list(sums)
    for (head, lanes), part in zip(pairs, probs):
        sums[head] = sums[head] + dot_nn(part, vrow[head, lanes, :])
    return tuple(sums)


def spans_and_bounds(seg_ref, first, spans_ref, bounds_ref):
    row = lax.broadcasted_iota(jnp.int32, (32, 128), 0)
    begins, ends = jnp.zeros((32, 128), jnp.int32), jnp.zeros((32, 128), jnp.int32)
    end = jnp.int32(0)
    low = [jnp.int32(0)] * 4
    high = [jnp.int32(16384)] * 4
    for image in range(32):
        begin = end
        end = begin + 64 * seg_ref[image]
        begins = jnp.where(row == image, begin, begins)
        ends = jnp.where(row == image, end, ends)
        for tile in range(4):
            start = first + 256 * tile
            low[tile] = jnp.where(begin <= start, begin, low[tile])
            high[tile] = jnp.where((begin < start + 256) & (end >= start + 256), end, high[tile])
    spans_ref[0] = begins
    spans_ref[1] = ends
    for tile in range(4):
        bounds_ref[tile, 0] = (low[tile] - (first - 1024)) // CHUNK
        bounds_ref[tile, 1] = (high[tile] - (first - 1024) + CHUNK - 1) // CHUNK


def membership(spans_ref, first, count):
    spots = first + lax.broadcasted_iota(jnp.int32, (32, count), 1)
    return (spots >= spans_ref[0, :, 0:1]) & (spots < spans_ref[1, :, 0:1])


def three_parts(row):
    high = row.astype(BF16)
    rest = row - high.astype(F32)
    middle = rest.astype(BF16)
    low = (rest - middle.astype(F32)).astype(BF16)
    return jnp.concatenate([high, middle, low, jnp.zeros((13, row.shape[1]), BF16)], axis=0)


def permutation(transposed):
    moved = lax.broadcasted_iota(jnp.int32, (512, 1) if transposed else (1, 512), 0 if transposed else 1)
    natural = lax.broadcasted_iota(jnp.int32, (512, 512), 1 if transposed else 0)
    return jnp.where(natural == 4 * (moved % 128) + moved // 128, 1.0, 0.0).astype(BF16)


def forward_body(
    seg_ref, kv_hbm, qrow_hbm, sums_hbm, norms_hbm, o_hbm, op_hbm, log_hbm,
    spans_ref, bounds_ref, o_ref, kv_ref, qrow, kx, vrow, sums_ref, norms_ref, op_ref, log_ref, sems,
):
    first = (lax.axis_index("seq") // 2) * 1024
    loads = [
        pltpu.make_async_copy(source, target, sems.at[index])
        for index, (source, target) in enumerate(
            (
                (kv_hbm.at[:, :, 0:1024], kv_ref.at[:, :, 0:1024]),
                (kv_hbm.at[:, :, 2048:3072], kv_ref.at[:, :, 2048:3072]),
                (qrow_hbm, qrow),
                (norms_hbm, norms_ref),
                (sums_hbm, sums_ref),
            )
        )
    ]
    for load in loads:
        load.start()
    spans_and_bounds(seg_ref, first, spans_ref, bounds_ref)
    perm = permutation(False)
    for load in loads:
        load.wait()

    def outside(low, high, step, carry):
        carry = lax.fori_loop(low, jnp.minimum(high, 4), step, carry)
        return lax.fori_loop(jnp.maximum(low, 8), high, step, carry)

    def build(chunk, tops):
        lanes = pl.ds(pl.multiple_of(chunk * CHUNK, CHUNK), CHUNK)
        build_values(spans_ref, first - 1024 + chunk * CHUNK, kv_ref, lanes, kx, vrow, lanes)
        return tuple(
            jnp.maximum(tops[head], squares(kv_ref[0, pl.ds(head * HEAD_DIM, HEAD_DIM), lanes]))
            for head in range(2)
        )

    tops = outside(bounds_ref[0, 0], bounds_ref[3, 1], build, (norms_ref[2], norms_ref[3]))
    small = jnp.max(norms_ref[0]) * jnp.max(tops[0]) <= SAFE * SAFE
    small = small & (jnp.max(norms_ref[1]) * jnp.max(tops[1]) <= SAFE * SAFE)

    def write(head, rows, sums, top_row):
        out = sums.T
        total_row = out[80:81, :]
        o_ref[pl.ds(head * HEAD_DIM, HEAD_DIM), rows] = (out[:80] * (1.0 / total_row)).astype(BF16)
        log_ref[head : head + 1, rows] = top_row + jnp.log(total_row) * LOG2E

    def plain_step(tile, carry):
        rows = pl.ds(pl.multiple_of(tile * 256, 256), 256)

        def step(chunk, sums):
            lanes = pl.ds(pl.multiple_of(chunk * CHUNK, CHUNK), CHUNK)
            return forward_step(rows, [lanes], qrow, kx, vrow, sums)

        start = (sums_ref[0, rows, :], sums_ref[1, rows, :])
        sums = outside(bounds_ref[tile, 0], bounds_ref[tile, 1], step, start)
        for head in range(2):
            write(head, rows, sums[head], 0.0)
        return carry

    lane = lax.broadcasted_iota(jnp.int32, (256, 128), 1)

    def shifted_step(tile, carry):
        low, high = bounds_ref[tile, 0], bounds_ref[tile, 1]
        rows = pl.ds(pl.multiple_of(tile * 256, 256), 256)

        def score_step(chunk, tops):
            lanes = pl.ds(pl.multiple_of(chunk * CHUNK, CHUNK), CHUNK)
            found = []
            for head in range(2):
                part = dot_nn(qrow[head, rows, :], kx[head, :, lanes])
                found.append(jnp.maximum(tops[head], jnp.maximum(part[:, :128], part[:, 128:])))
            return tuple(found)

        start = jnp.full((256, 128), BIG, F32)
        tops = lax.fori_loop(low, high, score_step, (start, start))
        for head in range(2):
            shift = -jnp.max(tops[head], axis=1, keepdims=True)
            part_one = shift.astype(BF16).astype(F32)
            part_two = (shift - part_one).astype(BF16).astype(F32)
            part_three = shift - part_one - part_two
            moved = jnp.where(lane == 112, part_one, qrow[head, rows, :].astype(F32))
            moved = jnp.where(lane == 113, part_two, moved)
            qrow[head, rows, :] = jnp.where(lane == 114, part_three, moved).astype(BF16)

        def step(chunk, sums):
            lanes = pl.ds(pl.multiple_of(chunk * CHUNK, CHUNK), CHUNK)
            return forward_step(rows, [lanes], qrow, kx, vrow, sums)

        start = jnp.zeros((256, 128), F32)
        sums = lax.fori_loop(low, high, step, (start, start))
        for head in range(2):
            write(head, rows, sums[head], jnp.max(tops[head].T, axis=0, keepdims=True))
        return carry

    @pl.when(small)
    def _():
        lax.fori_loop(0, 4, plain_step, 0)

    @pl.when(jnp.logical_not(small))
    def _():
        middle = pltpu.make_async_copy(
            kv_hbm.at[:, :, 1024:2048], kv_ref.at[:, :, 1024:2048], sems.at[5]
        )
        middle.start()
        middle.wait()
        for chunk in range(4, 8):
            lanes = pl.ds(chunk * CHUNK, CHUNK)
            build_values(spans_ref, first - 1024 + chunk * CHUNK, kv_ref, lanes, kx, vrow, lanes)
        lax.fori_loop(0, 4, shifted_step, 0)

    keep_o = pltpu.make_async_copy(o_ref, o_hbm, sems.at[6])
    keep_log = pltpu.make_async_copy(log_ref, log_hbm, sems.at[7])
    keep_o.start()
    keep_log.start()
    for half in range(2):
        moved = dot_nn(o_ref[:, half * 512 : half * 512 + 512], perm).astype(BF16)
        for part in range(4):
            op_ref[half, part] = moved[:, part * 128 : part * 128 + 128]
    keep_op = pltpu.make_async_copy(op_ref, op_hbm, sems.at[8])
    keep_op.start()
    keep_o.wait()
    keep_log.wait()
    keep_op.wait()


def build_keys(spans_ref, position, kv_ref, lanes, kx, vx, krow, into):
    ones = jnp.where(lax.broadcasted_iota(jnp.int32, (16, CHUNK), 0) < 3, 1.0, 0.0).astype(BF16)
    hot = jnp.where(membership(spans_ref, position, CHUNK), 1.0, 0.0).astype(BF16)
    for head in range(2):
        feats = pl.ds(head * HEAD_DIM, HEAD_DIM)
        keys = jnp.concatenate([kv_ref[0, feats, lanes], hot, ones], axis=0)
        kx[head, :, into] = keys
        krow[head, into, :] = keys.T
        vx[head, :, into] = jnp.concatenate(
            [kv_ref[1, feats, lanes], ones, jnp.zeros((32, CHUNK), BF16)], axis=0
        )


def backward_step(rows, chunks, q_ref, g_ref, qrow, grow, kx, vx, krow, dk_acc, dv_acc, sums):
    pairs = [(head, lanes) for lanes in chunks for head in range(2)]
    feats = [pl.ds(head * HEAD_DIM, HEAD_DIM) for head in range(2)]
    probs = [jnp.exp2(dot_nn(qrow[head, rows, :], kx[head, :, lanes])) for head, lanes in pairs]
    shifted = [dot_nn(grow[head, rows, :], vx[head, :, lanes]) for head, lanes in pairs]
    dscores = [(prob * part).astype(BF16) for prob, part in zip(probs, shifted)]
    weights = [prob.astype(BF16) for prob in probs]
    dk = [dot_nn(q_ref[feats[head], rows], part) for (head, _), part in zip(pairs, dscores)]
    dv = [dot_nn(g_ref[feats[head], rows], part) for (head, _), part in zip(pairs, weights)]
    sums = list(sums)
    for (head, lanes), part in zip(pairs, dscores):
        sums[head] = sums[head] + dot_nn(part, krow[head, lanes, :])
    for (head, lanes), dk_part, dv_part in zip(pairs, dk, dv):
        dk_acc[head, :, lanes] += dk_part
        dv_acc[head, :, lanes] += dv_part
    return tuple(sums)


def backward_body(
    seg_ref, sizes_ref, receiver_ref, q_hbm, kv_hbm, o_hbm, log_hbm, gp_hbm,
    dq_hbm, dkv_hbm, starts_hbm, here_hbm, qrow_hbm, grow_hbm, gnat_hbm, spans_hbm,
    dq_ref, dkv_ref, starts_ref, here_ref, qrow, grow, gnat, spans_ref, bounds_ref, q_ref, kv_ref, o_ref, log_ref, gp_ref, kx, vx, krow, dk_acc, dv_acc, sems,
):
    seq = lax.axis_index("seq")
    first = (seq // 2) * 1024
    load_kv = pltpu.make_async_copy(kv_hbm, kv_ref, sems.at[0])
    load_o = pltpu.make_async_copy(o_hbm, o_ref, sems.at[1])
    load_q = pltpu.make_async_copy(q_hbm, q_ref, sems.at[2])
    load_kv.start()
    load_o.start()
    load_q.start()
    load_log = pltpu.make_async_copy(log_hbm, log_ref, sems.at[3])
    load_log.start()
    load_gp = pltpu.make_async_copy(gp_hbm, gp_ref, sems.at[4])
    load_gp.start()
    spans_and_bounds(seg_ref, first, spans_ref, bounds_ref)
    start = jnp.int32(0)
    my_start, my_size = jnp.int32(0), jnp.int32(0)
    for batch in range(32):
        size, receiver = sizes_ref[batch], receiver_ref[batch]
        starts_ref[pl.ds(pl.multiple_of(receiver * 16, 16), 16), :] = jnp.full((16, 128), start)
        my_start = jnp.where(receiver == seq, start, my_start)
        my_size = jnp.where(receiver == seq, size, my_size)
        start = start + size
    here_ref[0:8, :] = jnp.full((8, 512), my_start)
    here_ref[8:16, :] = jnp.full((8, 512), my_size)
    back = permutation(True)
    load_gp.wait()
    for half in range(2):
        joined = jnp.concatenate([gp_ref[half, part] for part in range(4)], axis=1)
        gnat[:, half * 512 : half * 512 + 512] = dot_nn(joined, back).astype(BF16)
    load_kv.wait()
    load_o.wait()
    load_q.wait()
    load_log.wait()
    for head in range(2):
        feats = pl.ds(head * HEAD_DIM, HEAD_DIM)
        for block in range(4):
            lanes = pl.ds(block * 256, 256)
            inside = membership(spans_ref, first + block * 256, 256)
            joined = jnp.concatenate(
                [
                    q_ref[feats, lanes],
                    jnp.where(inside, 0.0, BIG).astype(BF16),
                    three_parts(-log_ref[head : head + 1, lanes]),
                ],
                axis=0,
            )
            qrow[head, lanes, :] = joined.T
            grads = gnat[feats, lanes]
            delta = jnp.sum(
                grads.astype(F32) * o_ref[feats, lanes].astype(F32), axis=0, keepdims=True
            )
            joined = jnp.concatenate(
                [grads, three_parts(-delta), jnp.zeros((32, 256), BF16)], axis=0
            )
            grow[head, lanes, :] = joined.T

    keeps = [
        pltpu.make_async_copy(source, target, sems.at[5 + index])
        for index, (source, target) in enumerate(
            (
                (starts_ref, starts_hbm), (here_ref, here_hbm), (spans_ref, spans_hbm),
                (gnat, gnat_hbm), (qrow, qrow_hbm), (grow, grow_hbm),
            )
        )
    ]
    for keep in keeps:
        keep.start()

    def outside(low, high, step, carry):
        carry = lax.fori_loop(low, jnp.minimum(high, 4), step, carry)
        return lax.fori_loop(jnp.maximum(low, 8), high, step, carry)

    def place_of(chunk):
        return pl.ds(pl.multiple_of(jnp.where(chunk < 4, chunk, chunk - 4) * CHUNK, CHUNK), CHUNK)

    def build(chunk, carry):
        lanes = pl.ds(pl.multiple_of(chunk * CHUNK, CHUNK), CHUNK)
        build_keys(
            spans_ref, first - 1024 + chunk * CHUNK, kv_ref, lanes, kx, vx, krow, place_of(chunk)
        )
        return carry

    outside(bounds_ref[0, 0], bounds_ref[3, 1], build, 0)
    dk_acc[...] = jnp.zeros_like(dk_acc)
    dv_acc[...] = jnp.zeros_like(dv_acc)

    def tile_step(tile, carry):
        rows = pl.ds(pl.multiple_of(tile * 256, 256), 256)

        def step(chunk, sums):
            return backward_step(
                rows, [place_of(chunk)], q_ref, gnat, qrow, grow, kx, vx, krow, dk_acc, dv_acc, sums
            )

        start = jnp.zeros((256, 128), F32)
        sums = outside(bounds_ref[tile, 0], bounds_ref[tile, 1], step, (start, start))
        for head in range(2):
            dq_ref[head, rows, :] = sums[head]
        return carry

    lax.fori_loop(0, 4, tile_step, 0)
    keeps.append(pltpu.make_async_copy(dq_ref, dq_hbm, sems.at[12]))
    keeps[-1].start()
    for head in range(2):
        feats = pl.ds(head * HEAD_DIM, HEAD_DIM)
        dkv_ref[0, feats, :] = (dk_acc[head] * LN2).astype(BF16)
        dkv_ref[1, feats, :] = dv_acc[head].astype(BF16)
    keeps.append(pltpu.make_async_copy(dkv_ref, dkv_hbm, sems.at[11]))
    keeps[-1].start()
    for keep in keeps:
        keep.wait()


def middle_body(
    op_ref, w_hbm, w_out_hbm, tokens_hbm, mgrad_hbm, gain_hbm,
    gp_ref, gl_hbm, glt_hbm, own_ref, table_ref,
    w_ref, tokens_ref, mgrad_ref, gain_ref, gl_ref, glt_ref, att, gat, packed, send, recv,
):
    section, chip, core = place()
    copies = Copies(send, recv)
    columns = pl.ds(pl.multiple_of(section * 1280, 128), 1280)
    load_gain = copies.start(gain_hbm, gain_ref, None)
    load_mgrad = copies.start(mgrad_hbm.at[:, columns], mgrad_ref, None)
    load_tokens = copies.start(tokens_hbm, tokens_ref, None)
    loads = []
    for step in range(4):
        w_rows = pl.ds(pl.multiple_of((section + step) % 4 * 320, 16), 320)
        source = w_hbm.at[w_rows, :] if step else w_out_hbm
        loads.append(copies.start(source, w_ref.at[w_rows, :], None))
    greet(row_peers(section, chip, core) + core_peers(section, chip, core))
    rows = pl.ds(pl.multiple_of((section * 2 + core) * PAIR, 16), PAIR)
    waits = []
    for step in (2, 1, 3, 0):
        for turn in range(2):
            to_section, to_core = (section + step) % 4, (core + turn) % 2
            device = dev(chip, to_core, to_section) if step or turn else None
            waits.append(copies.start(op_ref.at[to_core, to_section], att.at[rows, :], device))
    late = [copies.start(op_ref.at[1 - core], own_ref, dev(chip, 1 - core, section))]
    row = lax.broadcasted_iota(jnp.int32, (128, 512), 0)
    column = lax.broadcasted_iota(jnp.int32, (128, 512), 1)
    chosen = jnp.where(column == 4 * row + section, 1.0, 0.0).astype(BF16)
    load_tokens.wait()
    load_gain.wait()
    load_mgrad.wait()
    values = dot_nn(chosen, tokens_ref[...])
    gain = gain_ref[...].reshape(1, 1280).astype(F32)
    scaled = mgrad_ref[...].astype(F32) * gain
    scaled_mean = jnp.mean(scaled, axis=1, keepdims=True)
    row = lax.broadcasted_iota(jnp.int32, (128, 128), 0)
    column = lax.broadcasted_iota(jnp.int32, (128, 128), 1)
    order = jnp.where(column == 16 * (row % 8) + row // 8, 1.0, 0.0).astype(BF16)
    wait_all(loads)
    wait_all(waits)
    layer = values + dot_nn(att[...].T, w_ref[...])
    centered = layer - jnp.mean(layer, axis=1, keepdims=True)
    inv = lax.rsqrt(jnp.mean(centered * centered, axis=1, keepdims=True) + EPS)
    unit = centered * inv
    grad_layer = inv * (
        scaled - scaled_mean - unit * jnp.mean(scaled * unit, axis=1, keepdims=True)
    )
    grad_layer = grad_layer.astype(BF16)
    gat[...] = dot_nt(w_ref[...], grad_layer).astype(BF16)
    for step in (2, 1, 3, 0):
        for turn in range(2):
            to_section, to_core = (section + step) % 4, (core + turn) % 2
            device = dev(chip, to_core, to_section) if step or turn else None
            rows = pl.ds(pl.multiple_of((to_section * 2 + to_core) * PAIR, 16), PAIR)
            late.append(copies.start(gat.at[rows, :], gp_ref.at[core, section], device))
    moved = dot_nn(order, (unit * gain).astype(BF16))
    for chip_to in range(16):
        eight = moved[chip_to * 8 : chip_to * 8 + 8]
        packed[chip_to] = jnp.concatenate([eight[:, :640], eight[:, 640:]], axis=0).astype(BF16)
    for step in range(16):
        to_chip = (chip + step) % 16
        device = dev(to_chip, core, section) if step else None
        late.append(copies.start(packed.at[to_chip], table_ref.at[chip], device))
    gl_ref[...] = grad_layer
    glt_ref[...] = grad_layer.T
    late.append(copies.start(gl_ref, gl_hbm, None))
    late.append(copies.start(glt_ref, glt_hbm, None))
    wait_all(late)


def tail_body(
    dkv_ref, starts_hbm, live_hbm, dq_hbm, qrow_hbm, grow_hbm, gnat_hbm, spans_hbm, q_hbm, kv_hbm,
    glt_hbm, op_hbm, own_hbm, table_hbm, gl_hbm, tokens_hbm, gain_hbm, w_hbm, normed_t_hbm,
    delivered_hbm, gx_all, weights_ref,
    starts_ref, live_ref, qrow, grow, gnat, spans_ref, gain_ref, delivered_ref,
    table_ref, gl_ref, tokens_ref, w_ref, normed_t_ref,
    q_ref, kv_ref, kx, vx, krow, dk_acc, dv_acc, dq_acc, own_out, mate_in,
    dkv_in, dj, rows_ref, gn, gn_in, gx_own, att, glt,
    parcels, arrived, p_mine, p_away, p_in,
    sum_a, sum_b, in_a, in_b, sub_a, sub_b, late_a, late_b, total, send, recv,
):
    section, chip, core = place()
    y, z = chip // 4, chip % 4
    copies = Copies(send, recv)
    mate = dev(chip, 1 - core, section)
    early = [
        copies.start(source, target, None)
        for source, target in (
            (spans_hbm, spans_ref), (kv_hbm.at[:, :, 1024:2048], kv_ref), (q_hbm, q_ref),
            (qrow_hbm, qrow), (grow_hbm, grow), (gnat_hbm, gnat), (dq_hbm, dq_acc),
        )
    ]
    greet(plane_peers(section, chip, core) + section_peers(section, chip, core))
    back = []
    for half in range(2):
        waits = []
        for step, base, slot in ((-1, 0, 0), (1, 1024, 1)):
            for target in (core, 1 - core):
                lanes = pl.ds(pl.multiple_of(base + target * 512 + half * 256, 256), 256)
                device = dev(around(chip, step), target, section)
                waits.append(
                    copies.start(dkv_ref.at[:, :, lanes], dkv_in.at[half, slot, core], device)
                )
        back.append(waits)
    gathered = []
    lanes = pl.ds(pl.multiple_of(section * 128, 128), 128)
    for step in (2, 1, 3, 0):
        device = dev(chip, core, (section + step) % 4) if step else None
        gathered.append(copies.start(glt_hbm, glt.at[:, lanes], device))
    load_table = [
        copies.start(table_hbm, table_ref, None), copies.start(starts_hbm, starts_ref, None)
    ]
    load_w = copies.start(w_hbm, w_ref, None)
    loads = [
        copies.start(source, target, None)
        for source, target in (
            (normed_t_hbm, normed_t_ref), (tokens_hbm, tokens_ref), (gl_hbm, gl_ref),
            (gain_hbm, gain_ref), (live_hbm, live_ref),
        )
    ]
    for near, of_core in ((True, core), (False, 1 - core)):
        rows = pl.ds(pl.multiple_of(of_core * PAIR, 16), PAIR)
        for part in range(4):
            source = op_hbm.at[core, part] if near else own_hbm.at[part]
            loads.append(copies.start(source, att.at[rows, part * 128 : part * 128 + 128], None))

    wait_all(early)
    for chunk in range(4):
        lanes = pl.ds(chunk * CHUNK, CHUNK)
        build_keys(
            spans_ref, chip * 1024 + chunk * CHUNK, kv_ref, lanes, kx, vx, krow, lanes
        )
    dk_acc[...] = jnp.zeros_like(dk_acc)
    dv_acc[...] = jnp.zeros_like(dv_acc)

    def own_step(tile, group):
        rows = pl.ds(pl.multiple_of(tile * 256, 256), 256)
        chunks = [pl.ds((group + 2 * which) * CHUNK, CHUNK) for which in range(2)]
        sums = backward_step(
            rows, chunks, q_ref, gnat, qrow, grow, kx, vx, krow, dk_acc, dv_acc,
            (dq_acc[0, rows, :], dq_acc[1, rows, :]),
        )
        for head in range(2):
            dq_acc[head, rows, :] = sums[head]

    def finish_own(half):
        for of_core in range(2):
            lanes = pl.ds(of_core * 512 + half * 256, 256)
            for head in range(2):
                feats = pl.ds(head * HEAD_DIM, HEAD_DIM)
                part = dq_acc[head, lanes, :].T[:80] * FACTOR
                own_out[half, of_core, 0, feats, :] = part.astype(BF16)
                own_out[half, of_core, 1, feats, :] = (dk_acc[head, :, lanes] * LN2).astype(BF16)
                own_out[half, of_core, 2, feats, :] = dv_acc[head, :, lanes].astype(BF16)
        back[half].append(copies.start(own_out.at[half, 1 - core], mate_in.at[half], mate))

    def first_step(tile, carry):
        own_step(tile, 0)
        return carry

    def even_step(index, carry):
        own_step(index * 2, 1)
        return carry

    def odd_step(index, carry):
        own_step(index * 2 + 1, 1)
        return carry

    lax.fori_loop(0, 4, first_step, 0)
    lax.fori_loop(0, 2, even_step, 0)
    finish_own(0)
    lax.fori_loop(0, 2, odd_step, 0)
    finish_own(1)

    wait_all(load_table)
    begin = starts_ref[:, 0:1]
    block, offset = begin // 128, begin % 128
    first = 8 * ((block + 1 - core) // 2)
    first = first + jnp.where(block % 2 == core, (offset - chip + 15) // 16, 0)
    out_row = lax.broadcasted_iota(jnp.int32, (512, 256), 0)
    in_row = lax.broadcasted_iota(jnp.int32, (512, 256), 1)
    wanted = first + out_row % 8
    wanted = (wanted // 8) * 16 + wanted % 8 + 8 * ((out_row // 8) % 2)
    hot = jnp.where(in_row == wanted, 1.0, 0.0).astype(BF16)
    table = table_ref[...].reshape(256, 640)
    parcels[...] = dot_nn(hot, table).astype(BF16).reshape(32, 16, 640)

    row = lax.broadcasted_iota(jnp.int32, (256, 256), 0)
    column = lax.broadcasted_iota(jnp.int32, (256, 256), 1)
    by_part = jnp.where(column == 4 * (row % 64) + row // 64, 1.0, 0.0).astype(BF16)
    load_w.wait()
    w_all = w_ref[...].reshape(960, 1280)
    sums = []
    for half in range(2):
        wait_all(back[half])
        lanes = pl.ds(half * 256, 256)
        for near, head in ((True, core), (False, 1 - core)):
            for which in range(3):
                grad = own_out[half, core, which] if near else mate_in[half, which]
                if which:
                    grad = grad.astype(F32) + dkv_in[half, 0, head, which - 1].astype(F32)
                    grad = (grad + dkv_in[half, 1, head, which - 1].astype(F32)).astype(BF16)
                dj[pl.ds(pl.multiple_of(320 * which + head * PAIR, 16), PAIR), lanes] = grad
        rows_ref[...] = dot_nt(by_part, dj[:, lanes]).astype(BF16)
        gn[half] = dot_nn(rows_ref[...], w_all).astype(BF16).reshape(4, 64, 1280)
        waits = []
        for step in (2, 1, 3):
            to_section = (section + step) % 4
            device = dev(chip, core, to_section)
            waits.append(copies.start(gn.at[half, to_section], gn_in.at[half, step - 1], device))
        sums.append(waits)

    deliveries = []
    for step in range(16):
        for turn in range(2):
            to_chip, to_core = (chip + step) % 16, (core + turn) % 2
            device = dev(to_chip, to_core, section) if step or turn else None
            deliveries.append(
                copies.start(parcels.at[to_chip * 2 + to_core], arrived.at[chip * 2 + core], device)
            )

    def products(index, core_of):
        rows = pl.ds(index * 320, 320)
        normed = normed_t_ref[rows, :]
        if core_of == 0:
            return dot_nt(normed, dj[0:640, :])
        return jnp.concatenate(
            [dot_nt(normed, dj[640:960, :]), dot_nt(glt[rows, :], att[...])], axis=1
        )

    wait_all(gathered)
    wait_all(loads)
    pairs = []
    for index in range(4):
        for core_of in range(2):
            @pl.when(core != core_of)
            def _():
                p_away[index] = products(index, core_of).astype(BF16).reshape(4, 80, 640)

        pairs.append(copies.start(p_away.at[index], p_in.at[index], mate))
    for index in range(4):
        for core_of in range(2):
            @pl.when(core == core_of)
            def _():
                p_mine[index] = products(index, core_of).reshape(4, 80, 640)

    gathers = []

    def finish_norm(half):
        row = lax.broadcasted_iota(jnp.int32, (64, 256), 0)
        column = lax.broadcasted_iota(jnp.int32, (64, 256), 1)
        chosen = jnp.where(column == 4 * row + section, 1.0, 0.0).astype(BF16)
        values = dot_nn(chosen, tokens_ref[half * 256 : half * 256 + 256, :])
        centered = values - jnp.mean(values, axis=1, keepdims=True)
        inv = lax.rsqrt(jnp.mean(centered * centered, axis=1, keepdims=True) + EPS)
        unit = centered * inv
        wait_all(sums[half])
        grad = gn[half, section].astype(F32) + gn_in[half, 0].astype(F32)
        grad = grad + (gn_in[half, 1].astype(F32) + gn_in[half, 2].astype(F32))
        scaled = grad * gain_ref[...].reshape(1, 1280).astype(F32)
        grad = inv * (
            scaled
            - jnp.mean(scaled, axis=1, keepdims=True)
            - unit * jnp.mean(scaled * unit, axis=1, keepdims=True)
        )
        grad = grad + gl_ref[half * 64 : half * 64 + 64, :].astype(F32)
        gx_own[half] = grad.astype(BF16)
        waits = []
        for step in (2, 1, 3, 0):
            device = dev(chip, core, (section + step) % 4) if step else None
            waits.append(copies.start(gx_own.at[half], gx_all.at[half, section], device))
        gathers.append(waits)

    finish_norm(0)
    firsts = [[], []]
    for index in range(4):
        pairs[index].wait()
        summed = (p_mine[index] + p_in[index].astype(F32)).astype(BF16)
        sum_a[index] = summed[:, :, :384]
        sum_b[index] = summed[:, :, 384:]
    for step in (2, 1, 3):
        to_z, to_y = (z + step) % 4, (y + step) % 4
        device = dev(y * 4 + to_z, core, section)
        firsts[0].append(copies.start(sum_a.at[:, to_z], in_a.at[step - 1], device))
        device = dev(to_y * 4 + z, core, section)
        firsts[1].append(copies.start(sum_b.at[to_y], in_b.at[step - 1], device))
    finish_norm(1)
    seconds = []
    wait_all(firsts[1])
    grad = sum_b[y].astype(F32) + in_b[0].astype(F32)
    sub_b[...] = (grad + (in_b[1].astype(F32) + in_b[2].astype(F32))).astype(BF16)
    for step in (2, 1, 3):
        to_z = (z + step) % 4
        device = dev(y * 4 + to_z, core, section)
        seconds.append(copies.start(sub_b.at[to_z], late_b.at[step - 1], device))
    wait_all(firsts[0])
    for index in range(4):
        grad = sum_a[index, z].astype(F32) + in_a[0, index].astype(F32)
        grad = grad + (in_a[1, index].astype(F32) + in_a[2, index].astype(F32))
        sub_a[index] = grad.astype(BF16)
    for step in (2, 1, 3):
        to_y = (y + step) % 4
        device = dev(to_y * 4 + z, core, section)
        seconds.append(copies.start(sub_a.at[to_y], late_a.at[step - 1], device))

    lane = lax.broadcasted_iota(jnp.int32, (1, 512), 1)
    from_chip, from_core, side, number = lane // 32, (lane // 16) % 2, (lane // 8) % 2, lane % 8
    begin, live = live_ref[0:1, :], live_ref[8:9, :]
    block, offset = begin // 128, begin % 128
    spot = 8 * ((block + 1 - from_core) // 2) + number
    spot = spot + jnp.where(block % 2 == from_core, (offset - from_chip + 15) // 16, 0)
    slot = (2 * (spot // 8) + from_core) * 128 + 16 * (spot % 8) + from_chip - begin
    out_row = lax.broadcasted_iota(jnp.int32, (256, 512), 0)
    taken = (out_row == slot) & (out_row < live)
    wait_all(deliveries)
    rows = arrived[...].reshape(512, 640)
    for which in range(2):
        hot = jnp.where(taken & (side == which), 1.0, 0.0).astype(BF16)
        delivered_ref[:, which * 640 : which * 640 + 640] = dot_nn(hot, rows).astype(BF16)
    deliver = copies.start(delivered_ref, delivered_hbm, None)

    wait_all(seconds)
    grad = sub_a[y].astype(F32) + late_a[0].astype(F32)
    total[:, :384] = grad + (late_a[1].astype(F32) + late_a[2].astype(F32))
    grad = sub_b[z].astype(F32) + late_b[0].astype(F32)
    total[:, 384:] = grad + (late_b[1].astype(F32) + late_b[2].astype(F32))
    lasts = []
    for target, device in ((1 - core, mate), (core, None)):
        rows = pl.ds(pl.multiple_of(target * 40, 8), 40)
        lasts.append(copies.start(total.at[rows, :], weights_ref.at[core], device))
    wait_all(lasts + [deliver])
    for waits in gathers:
        wait_all(waits)


def results_body(
    gx_hbm, both_hbm, arrived_hbm, gx_out, w_qkv_out, w_out_out, delivered_out,
    gx_ref, both_ref, sems,
):
    loads = [
        pltpu.make_async_copy(gx_hbm.at[0], gx_ref.at[0], sems.at[0]),
        pltpu.make_async_copy(gx_hbm.at[1], gx_ref.at[1], sems.at[1]),
        pltpu.make_async_copy(both_hbm, both_ref, sems.at[2]),
        pltpu.make_async_copy(arrived_hbm, delivered_out, sems.at[3]),
    ]
    for load in loads:
        load.start()
    row = lax.broadcasted_iota(jnp.int32, (256, 256), 0)
    column = lax.broadcasted_iota(jnp.int32, (256, 256), 1)
    natural = jnp.where(row == 4 * (column % 64) + column // 64, 1.0, 0.0).astype(BF16)
    for half in range(2):
        loads[half].wait()
        rows = gx_ref[half].reshape(256, 1280)
        gx_out[half * 256 : half * 256 + 256, :] = dot_nn(natural, rows).astype(BF16)
    loads[2].wait()
    w_qkv_out[0] = both_ref[0, :, :320]
    w_qkv_out[1] = both_ref[0, :, 320:]
    w_qkv_out[2] = both_ref[1, :, :320]
    w_out_out[...] = both_ref[1, :, 320:]
    loads[3].wait()


def halo_peers(section, chip, core):
    found = [dev(chip, 1 - core, section)]
    for step in (1, -1):
        for other in (core, 1 - core):
            found.append(dev(around(chip, step), other, section))
    return found


def row_peers(section, chip, core):
    found = []
    for step in range(4):
        for turn in range(2):
            if step or turn:
                found.append(dev(chip, (core + turn) % 2, (section + step) % 4))
    return found


def section_peers(section, chip, core):
    return [dev(chip, core, (section + step) % 4) for step in range(1, 4)]


def core_peers(section, chip, core):
    return [dev((chip + step) % 16, core, section) for step in range(1, 16)]


def plane_peers(section, chip, core):
    found = [dev(chip, 1 - core, section)]
    for step in range(1, 16):
        for turn in range(2):
            found.append(dev((chip + step) % 16, (core + turn) % 2, section))
    return found


def local(
    tokens, norm_gain, w_qkv, w_out, merge_gain, seg_blocks, mb_sizes, mb_receiver, merged_grad
):
    w_rows = w_qkv.transpose(0, 2, 1)
    q, kv, normed_t, w_full, q_rows, sums, norms = call(
        project_body,
        [
            (HBM, shape((PAIR, 1024))),
            (HBM, shape((2, PAIR, 3072))),
            (HBM, shape((1280, 512))),
            (HBM, shape((1280, 1280))),
            (HBM, shape((2, 1024, 128))),
            (HBM, shape((2, 1024, 128), F32)),
            (HBM, shape((4, 8, 128), F32)),
        ],
        [(SMEM, seg_blocks), (HBM, tokens), (HBM, norm_gain), (HBM, w_rows), (HBM, w_out)],
        [
            pltpu.VMEM((512, 1280), BF16),
            pltpu.VMEM((1280,), BF16),
            pltpu.VMEM((3, 320, 1280), BF16),
            pltpu.VMEM((1280, 512), BF16),
            pltpu.VMEM((3, 320, 512), BF16),
            pltpu.VMEM((PAIR, 1024), BF16),
            pltpu.VMEM((2, PAIR, 1024), BF16),
            pltpu.VMEM((2, 32, 128), jnp.int32),
            pltpu.VMEM((2, 1024, 128), BF16),
            pltpu.VMEM((2, 128, 1024), BF16),
            pltpu.VMEM((2, 1024, 128), BF16),
            pltpu.VMEM((2, 1024, 128), F32),
            pltpu.VMEM((4, 8, 128), F32),
        ],
        copies=40,
        number=1,
        limit=62,
    )
    o, op, log_total = call(
        forward_body,
        [
            (HBM, shape((PAIR, 1024))),
            (HBM, shape((2, 4, PAIR, 128))),
            (HBM, shape((2, 1024), F32)),
        ],
        [(SMEM, seg_blocks), (HBM, kv), (HBM, q_rows), (HBM, sums), (HBM, norms)],
        [
            pltpu.VMEM((2, 32, 128), jnp.int32),
            pltpu.SMEM((4, 2), jnp.int32),
            pltpu.VMEM((PAIR, 1024), BF16),
            pltpu.VMEM((2, PAIR, 3072), BF16),
            pltpu.VMEM((2, 1024, 128), BF16),
            pltpu.VMEM((2, 128, 3072), BF16),
            pltpu.VMEM((2, 3072, 128), BF16),
            pltpu.VMEM((2, 1024, 128), F32),
            pltpu.VMEM((4, 8, 128), F32),
            pltpu.VMEM((2, 4, PAIR, 128), BF16),
            pltpu.VMEM((2, 1024), F32),
        ],
        copies=9,
        limit=62,
    )
    gp, grad_layer, glt, att_own, table = call(
        middle_body,
        [
            (HBM, shape((2, 4, PAIR, 128))),
            (HBM, shape((128, 1280))),
            (HBM, shape((1280, 128))),
            (HBM, shape((4, PAIR, 128))),
            (HBM, shape((16, 16, 640))),
        ],
        [(HBM, op), (HBM, w_full), (HBM, w_out), (HBM, tokens), (HBM, merged_grad), (HBM, merge_gain)],
        [
            pltpu.VMEM((1280, 1280), BF16),
            pltpu.VMEM((512, 1280), BF16),
            pltpu.VMEM((128, 1280), BF16),
            pltpu.VMEM((1280,), BF16),
            pltpu.VMEM((128, 1280), BF16),
            pltpu.VMEM((1280, 128), BF16),
            pltpu.VMEM((1280, 128), BF16),
            pltpu.VMEM((1280, 128), BF16),
            pltpu.VMEM((16, 16, 640), BF16),
        ],
        copies=44,
        number=2,
        limit=62,
    )
    dq, dkv, start_rows, here, qrow, grow, gnat, spans = call(
        backward_body,
        [
            (HBM, shape((2, 1024, 128), F32)),
            (HBM, shape((2, PAIR, 2048))),
            (HBM, shape((512, 128), jnp.int32)),
            (HBM, shape((16, 512), jnp.int32)),
            (HBM, shape((2, 1024, 128))),
            (HBM, shape((2, 1024, 128))),
            (HBM, shape((PAIR, 1024))),
            (HBM, shape((2, 32, 128), jnp.int32)),
        ],
        [
            (SMEM, seg_blocks), (SMEM, mb_sizes), (SMEM, mb_receiver),
            (HBM, q), (HBM, kv), (HBM, o), (HBM, log_total), (HBM, gp),
        ],
        [
            pltpu.VMEM((2, 1024, 128), F32),
            pltpu.VMEM((2, PAIR, 2048), BF16),
            pltpu.VMEM((512, 128), jnp.int32),
            pltpu.VMEM((16, 512), jnp.int32),
            pltpu.VMEM((2, 1024, 128), BF16),
            pltpu.VMEM((2, 1024, 128), BF16),
            pltpu.VMEM((PAIR, 1024), BF16),
            pltpu.VMEM((2, 32, 128), jnp.int32),
            pltpu.SMEM((4, 2), jnp.int32),
            pltpu.VMEM((PAIR, 1024), BF16),
            pltpu.VMEM((2, PAIR, 3072), BF16),
            pltpu.VMEM((PAIR, 1024), BF16),
            pltpu.VMEM((2, 1024), F32),
            pltpu.VMEM((2, 4, PAIR, 128), BF16),
            pltpu.VMEM((2, 128, 2048), BF16),
            pltpu.VMEM((2, 128, 2048), BF16),
            pltpu.VMEM((2, 2048, 128), BF16),
            pltpu.VMEM((2, HEAD_DIM, 2048), F32),
            pltpu.VMEM((2, HEAD_DIM, 2048), F32),
        ],
        copies=13,
        limit=62,
    )
    arrived, gx_all, weights = call(
        tail_body,
        [
            (HBM, shape((256, 1280))),
            (HBM, shape((2, 4, 64, 1280))),
            (HBM, shape((2, 40, 640), F32)),
        ],
        [
            (HBM, dkv), (HBM, start_rows), (HBM, here), (HBM, dq), (HBM, qrow), (HBM, grow),
            (HBM, gnat), (HBM, spans), (HBM, q), (HBM, kv), (HBM, glt), (HBM, op), (HBM, att_own),
            (HBM, table), (HBM, grad_layer), (HBM, tokens), (HBM, norm_gain), (HBM, w_rows),
            (HBM, normed_t),
        ],
        [
            pltpu.VMEM((512, 128), jnp.int32),
            pltpu.VMEM((16, 512), jnp.int32),
            pltpu.VMEM((2, 1024, 128), BF16),
            pltpu.VMEM((2, 1024, 128), BF16),
            pltpu.VMEM((PAIR, 1024), BF16),
            pltpu.VMEM((2, 32, 128), jnp.int32),
            pltpu.VMEM((1280,), BF16),
            pltpu.VMEM((256, 1280), BF16),
            pltpu.VMEM((16, 16, 640), BF16),
            pltpu.VMEM((128, 1280), BF16),
            pltpu.VMEM((512, 1280), BF16),
            pltpu.VMEM((3, 320, 1280), BF16),
            pltpu.VMEM((1280, 512), BF16),
            pltpu.VMEM((PAIR, 1024), BF16),
            pltpu.VMEM((2, PAIR, 1024), BF16),
            pltpu.VMEM((2, 128, 1024), BF16),
            pltpu.VMEM((2, 128, 1024), BF16),
            pltpu.VMEM((2, 1024, 128), BF16),
            pltpu.VMEM((2, HEAD_DIM, 1024), F32),
            pltpu.VMEM((2, HEAD_DIM, 1024), F32),
            pltpu.VMEM((2, 1024, 128), F32),
            pltpu.VMEM((2, 2, 3, PAIR, 256), BF16),
            pltpu.VMEM((2, 3, PAIR, 256), BF16),
            pltpu.VMEM((2, 2, 2, 2, PAIR, 256), BF16),
            pltpu.VMEM((960, 512), BF16),
            pltpu.VMEM((256, 960), BF16),
            pltpu.VMEM((2, 4, 64, 1280), BF16),
            pltpu.VMEM((2, 3, 64, 1280), BF16),
            pltpu.VMEM((2, 64, 1280), BF16),
            pltpu.VMEM((320, 512), BF16),
            pltpu.VMEM((1280, 512), BF16),
            pltpu.VMEM((32, 16, 640), BF16),
            pltpu.VMEM((32, 16, 640), BF16),
            pltpu.VMEM((4, 4, 80, 640), F32),
            pltpu.VMEM((4, 4, 80, 640), BF16),
            pltpu.VMEM((4, 4, 80, 640), BF16),
            pltpu.VMEM((4, 4, 80, 384), BF16),
            pltpu.VMEM((4, 4, 80, 256), BF16),
            pltpu.VMEM((3, 4, 80, 384), BF16),
            pltpu.VMEM((3, 4, 80, 256), BF16),
            pltpu.VMEM((4, 80, 384), BF16),
            pltpu.VMEM((4, 80, 256), BF16),
            pltpu.VMEM((3, 80, 384), BF16),
            pltpu.VMEM((3, 80, 256), BF16),
            pltpu.VMEM((80, 640), F32),
        ],
        copies=124,
        number=3,
        limit=62,
    )
    grad_x, grad_w_qkv, grad_w_out, delivered = call(
        results_body,
        [
            (VMEM, shape((512, 1280))),
            (VMEM, shape((3, 40, 320), F32)),
            (VMEM, shape((40, 320), F32)),
            (VMEM, shape((256, 1280))),
        ],
        [(HBM, gx_all), (HBM, weights), (HBM, arrived)],
        [pltpu.VMEM((2, 4, 64, 1280), BF16), pltpu.VMEM((2, 40, 640), F32)],
        copies=4,
        limit=62,
    )
    return (delivered, grad_x, grad_w_qkv, grad_w_out.T)


def solution(mesh):
    placed = (
        P("seq", None),
        P(),
        P(None, None, "section"),
        P("section", None),
        P(),
        P(),
        P(),
        P(),
        P("seq", None),
    )
    return jax.shard_map(
        local,
        mesh=mesh,
        in_specs=placed,
        out_specs=(
            P("seq", "section"),
            P("seq", None),
            P(None, "seq", "section"),
            P("section", "seq"),
        ),
        check_vma=False,
    )
```

```python
import math

import jax
import jax.numpy as jnp
from jax import lax
from jax.experimental import pallas as pl
from jax.experimental.pallas import tpu as pltpu
from jax.sharding import PartitionSpec as P

HEADS = 16
EPS = 1e-06
HEAD_DIM = 80
PAIR = 160
BIG = -1e30
CHUNK = 256
SAFE = 60.0
BF16 = jnp.bfloat16
F32 = jnp.float32
MESH = pl.DeviceIdType.MESH
FACTOR = HEAD_DIM ** -0.5
LOG2E = 1.0 / math.log(2.0)
LN2 = math.log(2.0)


def dot_nn(left, right):
    return lax.dot_general(left, right, (((1,), (0,)), ((), ())), preferred_element_type=F32)


def dot_nt(left, right):
    return lax.dot_general(left, right, (((1,), (1,)), ((), ())), preferred_element_type=F32)


def place():
    section = lax.axis_index("section")
    seq = lax.axis_index("seq")
    return section, seq // 2, seq % 2


def shape(dims, dtype=BF16):
    return jax.ShapeDtypeStruct(dims, dtype)


class Copies:
    def __init__(self, send_sems, recv_sems):
        self.send_sems, self.recv_sems, self.used = send_sems, recv_sems, 0

    def start(self, source, target, device):
        index = self.used
        self.used = index + 1
        if device is None:
            copy = pltpu.make_async_copy(source, target, self.recv_sems.at[index])
        else:
            copy = pltpu.make_async_remote_copy(
                src_ref=source,
                dst_ref=target,
                send_sem=self.send_sems.at[index],
                recv_sem=self.recv_sems.at[index],
                device_id=device,
                device_id_type=MESH,
            )
        copy.start()
        return copy


def wait_all(copies):
    for copy in copies:
        copy.wait()


def greet(peers):
    barrier = pltpu.get_barrier_semaphore()
    for peer in peers:
        pl.semaphore_signal(barrier, inc=1, device_id=peer, device_id_type=MESH)


def greeted(peers):
    pl.semaphore_wait(pltpu.get_barrier_semaphore(), len(peers))


VMEM = pl.BlockSpec(memory_space=pltpu.VMEM)
SMEM = pl.BlockSpec(memory_space=pltpu.SMEM)
HBM = pl.BlockSpec(memory_space=pltpu.HBM)


def call(body, outs, ins, scratch=(), copies=0, number=None, limit=14):
    more = {} if number is None else {"collective_id": number, "has_side_effects": True}
    semaphores = [pltpu.SemaphoreType.DMA((copies,))] * (0 if not copies else 1 if number is None else 2)
    return pl.pallas_call(
        body,
        out_shape=[array for _, array in outs],
        in_specs=[place for place, _ in ins],
        out_specs=[place for place, _ in outs],
        scratch_shapes=list(scratch) + semaphores,
        compiler_params=pltpu.CompilerParams(vmem_limit_bytes=limit << 20, **more),
    )(*[array for _, array in ins])


def dev(chip, core, section):
    return (chip * 2 + core, section)


def around(chip, step):
    return (chip + step + 16) % 16


def project_body(
    seg_ref, tokens_hbm, gain_hbm, w_hbm, w_out_hbm,
    q_hbm, kv_hbm, normed_t_hbm, w_full, qrow_hbm, sums_hbm, norms_hbm,
    tokens_ref, gain_ref, w_ref, normed_t_ref, out_ref,
    q_ref, kv_ref, spans_ref, qrow, kx, vrow, sums_ref, norms_ref, send, recv,
):
    section, chip, core = place()
    copies = Copies(send, recv)
    peers = halo_peers(section, chip, core) + section_peers(section, chip, core)[::2]
    greet(peers)
    load_gain = copies.start(gain_hbm, gain_ref, None)
    load_tokens = []
    for tile in range(4):
        rows = pl.ds(tile * 128, 128)
        load_tokens.append(copies.start(tokens_hbm.at[rows, :], tokens_ref.at[rows, :], None))
    load_w = {which: copies.start(w_hbm.at[which], w_ref.at[which], None) for which in (1, 2, 0)}
    greeted(peers)
    mate = dev(chip, 1 - core, section)
    ahead, behind = (section + 1) % 4, (section + 3) % 4
    ahead_dev, behind_dev = dev(chip, core, ahead), dev(chip, core, behind)

    def w_rows(owner, start, count):
        return w_full.at[pl.ds(pl.multiple_of(owner * 320 + core * PAIR + start, 16), count), :]

    mine = w_out_hbm.at[pl.ds(pl.multiple_of(core * PAIR, 16), PAIR), :]
    to_ahead = copies.start(mine, w_rows(section, 0, PAIR), ahead_dev)
    to_behind = copies.start(mine, w_rows(section, 0, PAIR), behind_dev)
    waits, inner = [], []
    load_gain.wait()
    gain = gain_ref[...].reshape(1, 1280).astype(F32)
    for tile in range(4):
        rows = pl.ds(tile * 128, 128)
        load_tokens[tile].wait()
        values = tokens_ref[rows, :].astype(F32)
        centered = values - jnp.mean(values, axis=1, keepdims=True)
        inv = lax.rsqrt(jnp.mean(centered * centered, axis=1, keepdims=True) + EPS)
        normed_t_ref[:, rows] = (centered * inv * gain).astype(BF16).T
    own = pl.ds(pl.multiple_of(core * PAIR, 16), PAIR)
    other = pl.ds(pl.multiple_of((1 - core) * PAIR, 16), PAIR)
    for which in (1, 2, 0):
        load_w[which].wait()
        out = dot_nn(w_ref[which], normed_t_ref[...])
        if which == 0:
            out = out * (FACTOR * LOG2E)
        out_ref[which] = out.astype(BF16)
        mine = pl.ds(pl.multiple_of(core * 512, 512), 512)
        target = q_ref.at[:, mine]
        if which:
            for step, base in ((1, 0), (-1, 2048)):
                lanes = pl.ds(pl.multiple_of(base + core * 512, 512), 512)
                for rows, to_core in ((own, core), (other, 1 - core)):
                    device = dev(around(chip, step), to_core, section)
                    waits.append(
                        copies.start(out_ref.at[which, rows, :], kv_hbm.at[which - 1, :, lanes], device)
                    )
            target = kv_ref.at[which - 1, :, mine]
        inner.append(copies.start(out_ref.at[which, other, :], target, mate))
        inner.append(copies.start(out_ref.at[which, own, :], target, None))
    waits.append(copies.start(normed_t_ref, normed_t_hbm, None))
    image_spans(seg_ref, spans_ref)
    wait_all(inner)
    waits.append(copies.start(q_ref, q_hbm, None))
    waits.append(copies.start(kv_ref, kv_hbm.at[:, :, 1024:2048], None))
    first = chip * 1024
    for block in range(4):
        lanes = pl.ds(block * 256, 256)
        build_queries(spans_ref, first + block * 256, q_ref, lanes, qrow)
        build_values(spans_ref, first + block * 256, kv_ref, lanes, kx, vrow, lanes)
    for head in range(2):
        feats = pl.ds(head * HEAD_DIM, HEAD_DIM)
        for which, values in enumerate((q_ref[feats, :], kv_ref[0, feats, :])):
            norms_ref[which * 2 + head, :, :] = squares(values)

    def tile_step(tile, carry):
        rows = pl.ds(pl.multiple_of(tile * 256, 256), 256)
        sums = (jnp.zeros((256, 128), F32),) * 2
        for chunk in range(0, 4, 2):
            lanes = [pl.ds((chunk + which) * CHUNK, CHUNK) for which in range(2)]
            sums = forward_step(rows, lanes, qrow, kx, vrow, sums)
        for head in range(2):
            sums_ref[head, rows, :] = sums[head]
        return carry

    lax.fori_loop(0, 2, tile_step, 0)
    to_ahead.wait()
    relay = [copies.start(w_rows(behind, 0, 80), w_rows(behind, 0, 80), ahead_dev)]
    to_behind.wait()
    relay.append(copies.start(w_rows(ahead, 80, 80), w_rows(ahead, 80, 80), behind_dev))
    waits.append(copies.start(w_rows(behind, 0, PAIR), w_rows(behind, 0, PAIR), mate))
    waits.append(copies.start(w_rows(ahead, 0, PAIR), w_rows(ahead, 0, PAIR), mate))
    lax.fori_loop(2, 4, tile_step, 0)
    waits.append(copies.start(qrow, qrow_hbm, None))
    waits.append(copies.start(sums_ref, sums_hbm, None))
    waits.append(copies.start(norms_ref, norms_hbm, None))
    far = (section + 2) % 4
    for copy, start in zip(relay, (0, 80)):
        copy.wait()
        waits.append(copies.start(w_rows(far, start, 80), w_rows(far, start, 80), mate))
    wait_all(waits)


def image_spans(seg_ref, spans_ref):
    row = lax.broadcasted_iota(jnp.int32, (32, 128), 0)
    begins, ends = jnp.zeros((32, 128), jnp.int32), jnp.zeros((32, 128), jnp.int32)
    end = jnp.int32(0)
    for image in range(32):
        begin = end
        end = begin + 64 * seg_ref[image]
        begins = jnp.where(row == image, begin, begins)
        ends = jnp.where(row == image, end, ends)
    spans_ref[0] = begins
    spans_ref[1] = ends


def squares(values):
    values = values.astype(F32)
    total = jnp.sum(values * values, axis=0, keepdims=True)
    blocks = [total[:, start : start + 128] for start in range(0, total.shape[1], 128)]
    top = blocks[0]
    for block in blocks[1:]:
        top = jnp.maximum(top, block)
    return jnp.broadcast_to(top, (8, 128))


def build_queries(spans_ref, position, q_ref, lanes, qrow):
    inside = membership(spans_ref, position, 256)
    for head in range(2):
        joined = jnp.concatenate(
            [
                q_ref[pl.ds(head * HEAD_DIM, HEAD_DIM), lanes],
                jnp.where(inside, 0.0, BIG).astype(BF16),
                jnp.zeros((16, 256), BF16),
            ],
            axis=0,
        )
        qrow[head, lanes, :] = joined.T


def build_values(spans_ref, position, kv_ref, lanes, kx, vrow, into):
    ones = jnp.where(lax.broadcasted_iota(jnp.int32, (16, CHUNK), 0) < 3, 1.0, 0.0).astype(BF16)
    hot = jnp.where(membership(spans_ref, position, CHUNK), 1.0, 0.0).astype(BF16)
    for head in range(2):
        feats = pl.ds(head * HEAD_DIM, HEAD_DIM)
        kx[head, :, into] = jnp.concatenate([kv_ref[0, feats, lanes], hot, ones], axis=0)
        joined = jnp.concatenate(
            [kv_ref[1, feats, lanes], ones, jnp.zeros((32, CHUNK), BF16)], axis=0
        )
        vrow[head, into, :] = joined.T


def forward_step(rows, chunks, qrow, kx, vrow, sums):
    pairs = [(head, lanes) for lanes in chunks for head in range(2)]
    probs = [
        jnp.exp2(dot_nn(qrow[head, rows, :], kx[head, :, lanes])).astype(BF16)
        for head, lanes in pairs
    ]
    sums = list(sums)
    for (head, lanes), part in zip(pairs, probs):
        sums[head] = sums[head] + dot_nn(part, vrow[head, lanes, :])
    return tuple(sums)


def spans_and_bounds(seg_ref, first, spans_ref, bounds_ref):
    row = lax.broadcasted_iota(jnp.int32, (32, 128), 0)
    begins, ends = jnp.zeros((32, 128), jnp.int32), jnp.zeros((32, 128), jnp.int32)
    end = jnp.int32(0)
    low = [jnp.int32(0)] * 4
    high = [jnp.int32(16384)] * 4
    for image in range(32):
        begin = end
        end = begin + 64 * seg_ref[image]
        begins = jnp.where(row == image, begin, begins)
        ends = jnp.where(row == image, end, ends)
        for tile in range(4):
            start = first + 256 * tile
            low[tile] = jnp.where(begin <= start, begin, low[tile])
            high[tile] = jnp.where((begin < start + 256) & (end >= start + 256), end, high[tile])
    spans_ref[0] = begins
    spans_ref[1] = ends
    for tile in range(4):
        bounds_ref[tile, 0] = (low[tile] - (first - 1024)) // CHUNK
        bounds_ref[tile, 1] = (high[tile] - (first - 1024) + CHUNK - 1) // CHUNK


def membership(spans_ref, first, count):
    spots = first + lax.broadcasted_iota(jnp.int32, (32, count), 1)
    return (spots >= spans_ref[0, :, 0:1]) & (spots < spans_ref[1, :, 0:1])


def three_parts(row):
    high = row.astype(BF16)
    rest = row - high.astype(F32)
    middle = rest.astype(BF16)
    low = (rest - middle.astype(F32)).astype(BF16)
    return jnp.concatenate([high, middle, low, jnp.zeros((13, row.shape[1]), BF16)], axis=0)


def permutation(transposed):
    moved = lax.broadcasted_iota(jnp.int32, (512, 1) if transposed else (1, 512), 0 if transposed else 1)
    natural = lax.broadcasted_iota(jnp.int32, (512, 512), 1 if transposed else 0)
    return jnp.where(natural == 4 * (moved % 128) + moved // 128, 1.0, 0.0).astype(BF16)


def forward_body(
    seg_ref, kv_hbm, qrow_hbm, sums_hbm, norms_hbm, o_hbm, op_hbm, log_hbm,
    spans_ref, bounds_ref, o_ref, kv_ref, qrow, kx, vrow, sums_ref, norms_ref, op_ref, log_ref, sems,
):
    first = (lax.axis_index("seq") // 2) * 1024
    loads = [
        pltpu.make_async_copy(source, target, sems.at[index])
        for index, (source, target) in enumerate(
            (
                (kv_hbm.at[:, :, 0:1024], kv_ref.at[:, :, 0:1024]),
                (kv_hbm.at[:, :, 2048:3072], kv_ref.at[:, :, 2048:3072]),
                (qrow_hbm, qrow),
                (norms_hbm, norms_ref),
                (sums_hbm, sums_ref),
            )
        )
    ]
    for load in loads:
        load.start()
    spans_and_bounds(seg_ref, first, spans_ref, bounds_ref)
    perm = permutation(False)
    for load in loads:
        load.wait()

    def outside(low, high, step, carry):
        carry = lax.fori_loop(low, jnp.minimum(high, 4), step, carry)
        return lax.fori_loop(jnp.maximum(low, 8), high, step, carry)

    def build(chunk, tops):
        lanes = pl.ds(pl.multiple_of(chunk * CHUNK, CHUNK), CHUNK)
        build_values(spans_ref, first - 1024 + chunk * CHUNK, kv_ref, lanes, kx, vrow, lanes)
        return tuple(
            jnp.maximum(tops[head], squares(kv_ref[0, pl.ds(head * HEAD_DIM, HEAD_DIM), lanes]))
            for head in range(2)
        )

    tops = outside(bounds_ref[0, 0], bounds_ref[3, 1], build, (norms_ref[2], norms_ref[3]))
    small = jnp.max(norms_ref[0]) * jnp.max(tops[0]) <= SAFE * SAFE
    small = small & (jnp.max(norms_ref[1]) * jnp.max(tops[1]) <= SAFE * SAFE)

    def write(head, rows, sums, top_row):
        out = sums.T
        total_row = out[80:81, :]
        o_ref[pl.ds(head * HEAD_DIM, HEAD_DIM), rows] = (out[:80] * (1.0 / total_row)).astype(BF16)
        log_ref[head : head + 1, rows] = top_row + jnp.log(total_row) * LOG2E

    def plain_step(tile, carry):
        rows = pl.ds(pl.multiple_of(tile * 256, 256), 256)

        def step(chunk, sums):
            lanes = pl.ds(pl.multiple_of(chunk * CHUNK, CHUNK), CHUNK)
            return forward_step(rows, [lanes], qrow, kx, vrow, sums)

        start = (sums_ref[0, rows, :], sums_ref[1, rows, :])
        sums = outside(bounds_ref[tile, 0], bounds_ref[tile, 1], step, start)
        for head in range(2):
            write(head, rows, sums[head], 0.0)
        return carry

    lane = lax.broadcasted_iota(jnp.int32, (256, 128), 1)

    def shifted_step(tile, carry):
        low, high = bounds_ref[tile, 0], bounds_ref[tile, 1]
        rows = pl.ds(pl.multiple_of(tile * 256, 256), 256)

        def score_step(chunk, tops):
            lanes = pl.ds(pl.multiple_of(chunk * CHUNK, CHUNK), CHUNK)
            found = []
            for head in range(2):
                part = dot_nn(qrow[head, rows, :], kx[head, :, lanes])
                found.append(jnp.maximum(tops[head], jnp.maximum(part[:, :128], part[:, 128:])))
            return tuple(found)

        start = jnp.full((256, 128), BIG, F32)
        tops = lax.fori_loop(low, high, score_step, (start, start))
        for head in range(2):
            shift = -jnp.max(tops[head], axis=1, keepdims=True)
            part_one = shift.astype(BF16).astype(F32)
            part_two = (shift - part_one).astype(BF16).astype(F32)
            part_three = shift - part_one - part_two
            moved = jnp.where(lane == 112, part_one, qrow[head, rows, :].astype(F32))
            moved = jnp.where(lane == 113, part_two, moved)
            qrow[head, rows, :] = jnp.where(lane == 114, part_three, moved).astype(BF16)

        def step(chunk, sums):
            lanes = pl.ds(pl.multiple_of(chunk * CHUNK, CHUNK), CHUNK)
            return forward_step(rows, [lanes], qrow, kx, vrow, sums)

        start = jnp.zeros((256, 128), F32)
        sums = lax.fori_loop(low, high, step, (start, start))
        for head in range(2):
            write(head, rows, sums[head], jnp.max(tops[head].T, axis=0, keepdims=True))
        return carry

    @pl.when(small)
    def _():
        lax.fori_loop(0, 4, plain_step, 0)

    @pl.when(jnp.logical_not(small))
    def _():
        middle = pltpu.make_async_copy(
            kv_hbm.at[:, :, 1024:2048], kv_ref.at[:, :, 1024:2048], sems.at[5]
        )
        middle.start()
        middle.wait()
        for chunk in range(4, 8):
            lanes = pl.ds(chunk * CHUNK, CHUNK)
            build_values(spans_ref, first - 1024 + chunk * CHUNK, kv_ref, lanes, kx, vrow, lanes)
        lax.fori_loop(0, 4, shifted_step, 0)

    keep_o = pltpu.make_async_copy(o_ref, o_hbm, sems.at[6])
    keep_log = pltpu.make_async_copy(log_ref, log_hbm, sems.at[7])
    keep_o.start()
    keep_log.start()
    for half in range(2):
        moved = dot_nn(o_ref[:, half * 512 : half * 512 + 512], perm).astype(BF16)
        for part in range(4):
            op_ref[half, part] = moved[:, part * 128 : part * 128 + 128]
    keep_op = pltpu.make_async_copy(op_ref, op_hbm, sems.at[8])
    keep_op.start()
    keep_o.wait()
    keep_log.wait()
    keep_op.wait()


def build_keys(spans_ref, position, kv_ref, lanes, kx, vx, krow, into):
    ones = jnp.where(lax.broadcasted_iota(jnp.int32, (16, CHUNK), 0) < 3, 1.0, 0.0).astype(BF16)
    hot = jnp.where(membership(spans_ref, position, CHUNK), 1.0, 0.0).astype(BF16)
    for head in range(2):
        feats = pl.ds(head * HEAD_DIM, HEAD_DIM)
        keys = jnp.concatenate([kv_ref[0, feats, lanes], hot, ones], axis=0)
        kx[head, :, into] = keys
        krow[head, into, :] = keys.T
        vx[head, :, into] = jnp.concatenate(
            [kv_ref[1, feats, lanes], ones, jnp.zeros((32, CHUNK), BF16)], axis=0
        )


def backward_step(rows, chunks, q_ref, g_ref, qrow, grow, kx, vx, krow, dk_acc, dv_acc, sums):
    pairs = [(head, lanes) for lanes in chunks for head in range(2)]
    feats = [pl.ds(head * HEAD_DIM, HEAD_DIM) for head in range(2)]
    probs = [jnp.exp2(dot_nn(qrow[head, rows, :], kx[head, :, lanes])) for head, lanes in pairs]
    shifted = [dot_nn(grow[head, rows, :], vx[head, :, lanes]) for head, lanes in pairs]
    dscores = [(prob * part).astype(BF16) for prob, part in zip(probs, shifted)]
    weights = [prob.astype(BF16) for prob in probs]
    dk = [dot_nn(q_ref[feats[head], rows], part) for (head, _), part in zip(pairs, dscores)]
    dv = [dot_nn(g_ref[feats[head], rows], part) for (head, _), part in zip(pairs, weights)]
    sums = list(sums)
    for (head, lanes), part in zip(pairs, dscores):
        sums[head] = sums[head] + dot_nn(part, krow[head, lanes, :])
    for (head, lanes), dk_part, dv_part in zip(pairs, dk, dv):
        dk_acc[head, :, lanes] += dk_part
        dv_acc[head, :, lanes] += dv_part
    return tuple(sums)


def backward_body(
    seg_ref, sizes_ref, receiver_ref, q_hbm, kv_hbm, o_hbm, log_hbm, gp_hbm,
    dq_hbm, dkv_hbm, starts_hbm, here_hbm, qrow_hbm, grow_hbm, gnat_hbm, spans_hbm,
    dq_ref, dkv_ref, starts_ref, here_ref, qrow, grow, gnat, spans_ref, bounds_ref, q_ref, kv_ref, o_ref, log_ref, gp_ref, kx, vx, krow, dk_acc, dv_acc, sems,
):
    seq = lax.axis_index("seq")
    first = (seq // 2) * 1024
    load_kv = pltpu.make_async_copy(kv_hbm.at[:, :, 0:1024], kv_ref.at[:, :, 0:1024], sems.at[0])
    load_kv_after = pltpu.make_async_copy(
        kv_hbm.at[:, :, 2048:3072], kv_ref.at[:, :, 2048:3072], sems.at[13]
    )
    load_o = pltpu.make_async_copy(o_hbm, o_ref, sems.at[1])
    load_q = pltpu.make_async_copy(q_hbm, q_ref, sems.at[2])
    load_o.start()
    load_q.start()
    load_log = pltpu.make_async_copy(log_hbm, log_ref, sems.at[3])
    load_log.start()
    load_gp = pltpu.make_async_copy(gp_hbm, gp_ref, sems.at[4])
    load_gp.start()
    load_kv.start()
    load_kv_after.start()
    spans_and_bounds(seg_ref, first, spans_ref, bounds_ref)
    start = jnp.int32(0)
    my_start, my_size = jnp.int32(0), jnp.int32(0)
    for batch in range(32):
        size, receiver = sizes_ref[batch], receiver_ref[batch]
        starts_ref[pl.ds(pl.multiple_of(receiver * 16, 16), 16), :] = jnp.full((16, 128), start)
        my_start = jnp.where(receiver == seq, start, my_start)
        my_size = jnp.where(receiver == seq, size, my_size)
        start = start + size
    here_ref[0:8, :] = jnp.full((8, 512), my_start)
    here_ref[8:16, :] = jnp.full((8, 512), my_size)
    back = permutation(True)
    load_gp.wait()
    for half in range(2):
        joined = jnp.concatenate([gp_ref[half, part] for part in range(4)], axis=1)
        gnat[:, half * 512 : half * 512 + 512] = dot_nn(joined, back).astype(BF16)
    load_kv.wait()
    load_kv_after.wait()
    load_o.wait()
    load_q.wait()
    load_log.wait()
    for head in range(2):
        feats = pl.ds(head * HEAD_DIM, HEAD_DIM)
        for block in range(4):
            lanes = pl.ds(block * 256, 256)
            inside = membership(spans_ref, first + block * 256, 256)
            joined = jnp.concatenate(
                [
                    q_ref[feats, lanes],
                    jnp.where(inside, 0.0, BIG).astype(BF16),
                    three_parts(-log_ref[head : head + 1, lanes]),
                ],
                axis=0,
            )
            qrow[head, lanes, :] = joined.T
            grads = gnat[feats, lanes]
            delta = jnp.sum(
                grads.astype(F32) * o_ref[feats, lanes].astype(F32), axis=0, keepdims=True
            )
            joined = jnp.concatenate(
                [grads, three_parts(-delta), jnp.zeros((32, 256), BF16)], axis=0
            )
            grow[head, lanes, :] = joined.T

    keeps = [
        pltpu.make_async_copy(source, target, sems.at[5 + index])
        for index, (source, target) in enumerate(
            (
                (starts_ref, starts_hbm), (here_ref, here_hbm), (spans_ref, spans_hbm),
                (gnat, gnat_hbm), (qrow, qrow_hbm), (grow, grow_hbm),
            )
        )
    ]
    for keep in keeps:
        keep.start()

    def outside(low, high, step, carry):
        carry = lax.fori_loop(low, jnp.minimum(high, 4), step, carry)
        return lax.fori_loop(jnp.maximum(low, 8), high, step, carry)

    def place_of(chunk):
        return pl.ds(pl.multiple_of(jnp.where(chunk < 4, chunk, chunk - 4) * CHUNK, CHUNK), CHUNK)

    def build(chunk, carry):
        lanes = pl.ds(pl.multiple_of(chunk * CHUNK, CHUNK), CHUNK)
        build_keys(
            spans_ref, first - 1024 + chunk * CHUNK, kv_ref, lanes, kx, vx, krow, place_of(chunk)
        )
        return carry

    outside(bounds_ref[0, 0], bounds_ref[3, 1], build, 0)
    dk_acc[...] = jnp.zeros_like(dk_acc)
    dv_acc[...] = jnp.zeros_like(dv_acc)

    def tile_step(tile, carry):
        rows = pl.ds(pl.multiple_of(tile * 256, 256), 256)

        def step(chunk, sums):
            return backward_step(
                rows, [place_of(chunk)], q_ref, gnat, qrow, grow, kx, vx, krow, dk_acc, dv_acc, sums
            )

        start = jnp.zeros((256, 128), F32)
        sums = outside(bounds_ref[tile, 0], bounds_ref[tile, 1], step, (start, start))
        for head in range(2):
            dq_ref[head, rows, :] = sums[head]
        return carry

    lax.fori_loop(0, 4, tile_step, 0)
    keeps.append(pltpu.make_async_copy(dq_ref, dq_hbm, sems.at[12]))
    keeps[-1].start()
    for head in range(2):
        feats = pl.ds(head * HEAD_DIM, HEAD_DIM)
        dkv_ref[0, feats, :] = (dk_acc[head] * LN2).astype(BF16)
        dkv_ref[1, feats, :] = dv_acc[head].astype(BF16)
    keeps.append(pltpu.make_async_copy(dkv_ref, dkv_hbm, sems.at[11]))
    keeps[-1].start()
    for keep in keeps:
        keep.wait()


def middle_body(
    op_ref, w_hbm, w_out_hbm, tokens_hbm, mgrad_hbm, gain_hbm,
    gp_ref, gl_hbm, glt_hbm, own_ref, table_ref,
    w_ref, tokens_ref, mgrad_ref, gain_ref, gl_ref, glt_ref, att, gat, packed, send, recv,
):
    section, chip, core = place()
    copies = Copies(send, recv)
    peers = row_peers(section, chip, core) + core_peers(section, chip, core)
    greet(peers)
    columns = pl.ds(pl.multiple_of(section * 1280, 128), 1280)
    load_gain = copies.start(gain_hbm, gain_ref, None)
    load_mgrad = copies.start(mgrad_hbm.at[:, columns], mgrad_ref, None)
    load_tokens = copies.start(tokens_hbm, tokens_ref, None)
    loads = []
    for step in range(4):
        w_rows = pl.ds(pl.multiple_of((section + step) % 4 * 320, 16), 320)
        source = w_hbm.at[w_rows, :] if step else w_out_hbm
        loads.append(copies.start(source, w_ref.at[w_rows, :], None))
    greeted(peers)
    rows = pl.ds(pl.multiple_of((section * 2 + core) * PAIR, 16), PAIR)
    waits = []
    for step in (2, 1, 3, 0):
        for turn in range(2):
            to_section, to_core = (section + step) % 4, (core + turn) % 2
            device = dev(chip, to_core, to_section) if step or turn else None
            waits.append(copies.start(op_ref.at[to_core, to_section], att.at[rows, :], device))
    late = [copies.start(op_ref.at[1 - core], own_ref, dev(chip, 1 - core, section))]
    row = lax.broadcasted_iota(jnp.int32, (128, 512), 0)
    column = lax.broadcasted_iota(jnp.int32, (128, 512), 1)
    chosen = jnp.where(column == 4 * row + section, 1.0, 0.0).astype(BF16)
    load_tokens.wait()
    load_gain.wait()
    load_mgrad.wait()
    values = dot_nn(chosen, tokens_ref[...])
    gain = gain_ref[...].reshape(1, 1280).astype(F32)
    scaled = mgrad_ref[...].astype(F32) * gain
    scaled_mean = jnp.mean(scaled, axis=1, keepdims=True)
    row = lax.broadcasted_iota(jnp.int32, (128, 128), 0)
    column = lax.broadcasted_iota(jnp.int32, (128, 128), 1)
    order = jnp.where(column == 16 * (row % 8) + row // 8, 1.0, 0.0).astype(BF16)
    wait_all(loads)
    wait_all(waits)
    layer = values + dot_nn(att[...].T, w_ref[...])
    centered = layer - jnp.mean(layer, axis=1, keepdims=True)
    inv = lax.rsqrt(jnp.mean(centered * centered, axis=1, keepdims=True) + EPS)
    unit = centered * inv
    grad_layer = inv * (
        scaled - scaled_mean - unit * jnp.mean(scaled * unit, axis=1, keepdims=True)
    )
    grad_layer = grad_layer.astype(BF16)
    gat[...] = dot_nt(w_ref[...], grad_layer).astype(BF16)
    for step in (2, 1, 3, 0):
        for turn in range(2):
            to_section, to_core = (section + step) % 4, (core + turn) % 2
            device = dev(chip, to_core, to_section) if step or turn else None
            rows = pl.ds(pl.multiple_of((to_section * 2 + to_core) * PAIR, 16), PAIR)
            late.append(copies.start(gat.at[rows, :], gp_ref.at[core, section], device))
    moved = dot_nn(order, (unit * gain).astype(BF16))
    for chip_to in range(16):
        eight = moved[chip_to * 8 : chip_to * 8 + 8]
        packed[chip_to] = jnp.concatenate([eight[:, :640], eight[:, 640:]], axis=0).astype(BF16)
    for step in range(16):
        to_chip = (chip + step) % 16
        device = dev(to_chip, core, section) if step else None
        late.append(copies.start(packed.at[to_chip], table_ref.at[chip], device))
    gl_ref[...] = grad_layer
    glt_ref[...] = grad_layer.T
    late.append(copies.start(gl_ref, gl_hbm, None))
    late.append(copies.start(glt_ref, glt_hbm, None))
    wait_all(late)


def tail_body(
    dkv_ref, starts_hbm, live_hbm, dq_hbm, qrow_hbm, grow_hbm, gnat_hbm, spans_hbm, q_hbm, kv_hbm,
    glt_hbm, op_hbm, own_hbm, table_hbm, gl_hbm, tokens_hbm, gain_hbm, w_hbm, normed_t_hbm,
    delivered_hbm, gx_all, weights_ref,
    starts_ref, live_ref, qrow, grow, gnat, spans_ref, gain_ref, delivered_ref,
    table_ref, gl_ref, tokens_ref, w_ref, normed_t_ref,
    q_ref, kv_ref, kx, vx, krow, dk_acc, dv_acc, dq_acc, own_out, mate_in,
    dkv_in, dj, rows_ref, gn, relay_in, gn_in, gx_own, att, glt,
    parcels, arrived, p_mine, p_away, p_in,
    summed, stage_in, subtotal, late_in, total, send, recv,
):
    section, chip, core = place()
    y, z = chip // 4, chip % 4
    ahead, behind, far = (section + 1) % 4, (section + 3) % 4, (section + 2) % 4
    ahead_dev, behind_dev = dev(chip, core, ahead), dev(chip, core, behind)
    copies = Copies(send, recv)
    mate = dev(chip, 1 - core, section)
    peers = plane_peers(section, chip, core) + section_peers(section, chip, core)
    greet(peers)
    early = [
        copies.start(source, target, None)
        for source, target in (
            (spans_hbm, spans_ref), (kv_hbm.at[:, :, 1024:2048], kv_ref), (q_hbm, q_ref),
            (qrow_hbm, qrow), (grow_hbm, grow), (gnat_hbm, gnat), (dq_hbm, dq_acc),
        )
    ]
    greeted(peers)
    back, mates = [], []
    for half in range(2):
        waits = []
        for step, base, slot in ((-1, 0, 0), (1, 1024, 1)):
            for target in (core, 1 - core):
                lanes = pl.ds(pl.multiple_of(base + target * 512 + half * 256, 256), 256)
                device = dev(around(chip, step), target, section)
                waits.append(
                    copies.start(dkv_ref.at[:, :, lanes], dkv_in.at[half, slot, core], device)
                )
        back.append(waits)

    def glt_part(owner, start, count):
        lanes = pl.ds(pl.multiple_of(owner * 128, 128), 128)
        return glt.at[start : start + count, lanes]

    mine = glt_part(section, 0, 1280)
    glt_ahead = copies.start(glt_hbm, mine, ahead_dev)
    glt_behind = copies.start(glt_hbm, mine, behind_dev)
    gathered = [copies.start(glt_hbm, mine, None)]
    load_table = [
        copies.start(table_hbm, table_ref, None), copies.start(starts_hbm, starts_ref, None)
    ]
    load_w = copies.start(w_hbm, w_ref, None)
    loads = [
        copies.start(source, target, None)
        for source, target in (
            (normed_t_hbm, normed_t_ref), (tokens_hbm, tokens_ref), (gl_hbm, gl_ref),
            (gain_hbm, gain_ref), (live_hbm, live_ref),
        )
    ]
    for near, of_core in ((True, core), (False, 1 - core)):
        rows = pl.ds(pl.multiple_of(of_core * PAIR, 16), PAIR)
        for part in range(4):
            source = op_hbm.at[core, part] if near else own_hbm.at[part]
            loads.append(copies.start(source, att.at[rows, part * 128 : part * 128 + 128], None))

    wait_all(early)
    for chunk in range(4):
        lanes = pl.ds(chunk * CHUNK, CHUNK)
        build_keys(
            spans_ref, chip * 1024 + chunk * CHUNK, kv_ref, lanes, kx, vx, krow, lanes
        )
    dk_acc[...] = jnp.zeros_like(dk_acc)
    dv_acc[...] = jnp.zeros_like(dv_acc)

    def own_step(tile, group):
        rows = pl.ds(pl.multiple_of(tile * 256, 256), 256)
        chunks = [pl.ds((group + 2 * which) * CHUNK, CHUNK) for which in range(2)]
        sums = backward_step(
            rows, chunks, q_ref, gnat, qrow, grow, kx, vx, krow, dk_acc, dv_acc,
            (dq_acc[0, rows, :], dq_acc[1, rows, :]),
        )
        for head in range(2):
            dq_acc[head, rows, :] = sums[head]

    def finish_own(half):
        for of_core in range(2):
            lanes = pl.ds(of_core * 512 + half * 256, 256)
            for head in range(2):
                feats = pl.ds(head * HEAD_DIM, HEAD_DIM)
                part = dq_acc[head, lanes, :].T[:80] * FACTOR
                own_out[half, of_core, 0, feats, :] = part.astype(BF16)
                own_out[half, of_core, 1, feats, :] = (dk_acc[head, :, lanes] * LN2).astype(BF16)
                own_out[half, of_core, 2, feats, :] = dv_acc[head, :, lanes].astype(BF16)
        mates.append(copies.start(own_out.at[half, 1 - core], mate_in.at[half], mate))

    def first_step(tile, carry):
        own_step(tile, 0)
        return carry

    def even_step(index, carry):
        own_step(index * 2, 1)
        return carry

    def odd_step(index, carry):
        own_step(index * 2 + 1, 1)
        return carry

    lax.fori_loop(0, 4, first_step, 0)
    lax.fori_loop(0, 2, even_step, 0)
    finish_own(0)
    glt_ahead.wait()
    there = glt_part(behind, 0, 640)
    gathered.append(copies.start(there, there, ahead_dev))
    glt_behind.wait()
    there = glt_part(ahead, 640, 640)
    gathered.append(copies.start(there, there, behind_dev))
    lax.fori_loop(0, 2, odd_step, 0)
    finish_own(1)

    row = lax.broadcasted_iota(jnp.int32, (256, 256), 0)
    column = lax.broadcasted_iota(jnp.int32, (256, 256), 1)
    by_part = jnp.where(column == 4 * (row % 64) + row // 64, 1.0, 0.0).astype(BF16)
    load_w.wait()

    def collect(half, kinds):
        lanes = pl.ds(half * 256, 256)
        for near, head in ((True, core), (False, 1 - core)):
            for which in kinds:
                grad = own_out[half, core, which] if near else mate_in[half, which]
                if which:
                    grad = grad.astype(F32) + dkv_in[half, 0, head, which - 1].astype(F32)
                    grad = (grad + dkv_in[half, 1, head, which - 1].astype(F32)).astype(BF16)
                dj[pl.ds(pl.multiple_of(320 * which + head * PAIR, 16), PAIR), lanes] = grad

    sums = []

    def send_first(half):
        rows_ref[...] = dot_nt(by_part, dj[:, half * 256 : half * 256 + 256]).astype(BF16)
        grad = dot_nn(rows_ref[...], w_ref[...].reshape(960, 1280))
        gn[half] = grad.astype(BF16).reshape(4, 64, 1280)
        relays = [
            copies.start(gn.at[half, far, 0:32], relay_in.at[half, 0], behind_dev),
            copies.start(gn.at[half, far, 32:64], relay_in.at[half, 1], ahead_dev),
        ]
        sums.append([
            copies.start(gn.at[half, behind, 32:64], gn_in.at[half, 0, 32:64], behind_dev),
            copies.start(gn.at[half, ahead, 0:32], gn_in.at[half, 1, 0:32], ahead_dev),
        ])
        return relays

    def send_second(half, relays):
        relays[0].wait()
        grad = gn[half, behind, 0:32].astype(F32) + relay_in[half, 0].astype(F32)
        gn[half, behind, 0:32] = grad.astype(BF16)
        source = gn.at[half, behind, 0:32]
        sums[half].append(copies.start(source, gn_in.at[half, 0, 0:32], behind_dev))
        relays[1].wait()
        grad = gn[half, ahead, 32:64].astype(F32) + relay_in[half, 1].astype(F32)
        gn[half, ahead, 32:64] = grad.astype(BF16)
        source = gn.at[half, ahead, 32:64]
        sums[half].append(copies.start(source, gn_in.at[half, 1, 32:64], ahead_dev))

    def products(index, core_of, group):
        rows = pl.ds(index * 320, 320)
        if group == 0 and core_of == 1:
            return dot_nt(glt[rows, :], att[...])
        which = 0 if group == 0 else 1 + core_of
        return dot_nt(normed_t_ref[rows, :], dj[320 * which : 320 * which + 320, :])

    def send_products(group):
        pairs = []
        for index in range(4):
            for core_of in range(2):
                @pl.when(core != core_of)
                def _():
                    part = products(index, core_of, group)
                    p_away[group, index] = part.astype(BF16).reshape(4, 80, 320)

            pairs.append(copies.start(p_away.at[group, index], p_in.at[group, index], mate))
        for index in range(4):
            for core_of in range(2):
                @pl.when(core == core_of)
                def _():
                    p_mine[index] = products(index, core_of, group).reshape(4, 80, 320)

        return pairs

    def first_stage(group, pairs):
        for index in range(4):
            pairs[index].wait()
            grad = p_mine[index] + p_in[group, index].astype(F32)
            summed[group, index] = grad.astype(BF16)
        waits = []
        for step in (2, 1, 3):
            to_z, to_y = (z + step) % 4, (y + step) % 4
            if group == 0:
                source, device = summed.at[group, to_y], dev(to_y * 4 + z, core, section)
            else:
                source, device = summed.at[group, :, to_z], dev(y * 4 + to_z, core, section)
            waits.append(copies.start(source, stage_in.at[group, step - 1], device))
        return waits

    def second_stage(group, waits):
        wait_all(waits)
        for index in range(4):
            grad = (summed[group, y, index] if group == 0 else summed[group, index, z]).astype(F32)
            for step in range(3):
                grad = grad + stage_in[group, step, index].astype(F32)
            subtotal[group, index] = grad.astype(BF16)
        waits = []
        for step in (2, 1, 3):
            to_z, to_y = (z + step) % 4, (y + step) % 4
            place_to = to_z if group == 0 else to_y
            device = dev(y * 4 + to_z if group == 0 else to_y * 4 + z, core, section)
            waits.append(
                copies.start(subtotal.at[group, place_to], late_in.at[group, step - 1], device)
            )
        return waits

    def last_stage(group, waits):
        wait_all(waits)
        grad = subtotal[group, z if group == 0 else y].astype(F32)
        for step in range(3):
            grad = grad + late_in[group, step].astype(F32)
        total[group] = grad
        found = []
        for target, device in ((1 - core, mate), (core, None)):
            rows = pl.ds(pl.multiple_of(target * 40, 8), 40)
            found.append(
                copies.start(total.at[group, rows, :], weights_ref.at[core, group], device)
            )
        return found

    gathers, forwards = [], []

    def finish_norm(half):
        row = lax.broadcasted_iota(jnp.int32, (64, 256), 0)
        column = lax.broadcasted_iota(jnp.int32, (64, 256), 1)
        chosen = jnp.where(column == 4 * row + section, 1.0, 0.0).astype(BF16)
        values = dot_nn(chosen, tokens_ref[half * 256 : half * 256 + 256, :])
        centered = values - jnp.mean(values, axis=1, keepdims=True)
        inv = lax.rsqrt(jnp.mean(centered * centered, axis=1, keepdims=True) + EPS)
        unit = centered * inv
        wait_all(sums[half])
        grad = gn[half, section].astype(F32) + gn_in[half, 0].astype(F32)
        grad = grad + gn_in[half, 1].astype(F32)
        scaled = grad * gain_ref[...].reshape(1, 1280).astype(F32)
        grad = inv * (
            scaled
            - jnp.mean(scaled, axis=1, keepdims=True)
            - unit * jnp.mean(scaled * unit, axis=1, keepdims=True)
        )
        grad = grad + gl_ref[half * 64 : half * 64 + 64, :].astype(F32)
        gx_own[half] = grad.astype(BF16)
        target = gx_all.at[half, section]
        gathers.append([copies.start(gx_own.at[half], target, ahead_dev)])
        gathers[half].append(copies.start(gx_own.at[half], target, behind_dev))
        forwards.append(copies.start(gx_own.at[half], target, None))

    def forward(half):
        gathers[half][0].wait()
        there = gx_all.at[half, behind, 0:32]
        forwards.append(copies.start(there, there, ahead_dev))
        gathers[half][1].wait()
        there = gx_all.at[half, ahead, 32:64]
        forwards.append(copies.start(there, there, behind_dev))

    wait_all(back[0])
    mates[0].wait()
    collect(0, (0, 1, 2))
    relays_a = send_first(0)

    wait_all(load_table)
    begin = starts_ref[:, 0:1]
    block, offset = begin // 128, begin % 128
    first = 8 * ((block + 1 - core) // 2)
    first = first + jnp.where(block % 2 == core, (offset - chip + 15) // 16, 0)
    out_row = lax.broadcasted_iota(jnp.int32, (512, 256), 0)
    in_row = lax.broadcasted_iota(jnp.int32, (512, 256), 1)
    wanted = first + out_row % 8
    wanted = (wanted // 8) * 16 + wanted % 8 + 8 * ((out_row // 8) % 2)
    hot = jnp.where(in_row == wanted, 1.0, 0.0).astype(BF16)
    table = table_ref[...].reshape(256, 640)
    parcels[...] = dot_nn(hot, table).astype(BF16).reshape(32, 16, 640)

    wait_all(loads)
    wait_all(gathered)
    mates[1].wait()
    collect(1, (0,))
    pairs = send_products(0)
    wait_all(back[1])
    collect(1, (1, 2))
    relays_b = send_first(1)
    deliveries = []
    for step in range(16):
        for turn in range(2):
            to_chip, to_core = (chip + step) % 16, (core + turn) % 2
            device = dev(to_chip, to_core, section) if step or turn else None
            deliveries.append(
                copies.start(parcels.at[to_chip * 2 + to_core], arrived.at[chip * 2 + core], device)
            )
    send_second(0, relays_a)
    stage_y = first_stage(0, pairs)
    pairs = send_products(1)
    stage_z = first_stage(1, pairs)
    send_second(1, relays_b)
    finish_norm(0)
    finish_norm(1)
    forward(0)
    later_z = second_stage(0, stage_y)
    forward(1)

    lane = lax.broadcasted_iota(jnp.int32, (1, 512), 1)
    from_chip, from_core, side, number = lane // 32, (lane // 16) % 2, (lane // 8) % 2, lane % 8
    begin, live = live_ref[0:1, :], live_ref[8:9, :]
    block, offset = begin // 128, begin % 128
    spot = 8 * ((block + 1 - from_core) // 2) + number
    spot = spot + jnp.where(block % 2 == from_core, (offset - from_chip + 15) // 16, 0)
    slot = (2 * (spot // 8) + from_core) * 128 + 16 * (spot % 8) + from_chip - begin
    out_row = lax.broadcasted_iota(jnp.int32, (256, 512), 0)
    taken = (out_row == slot) & (out_row < live)
    wait_all(deliveries)
    rows = arrived[...].reshape(512, 640)
    for which in range(2):
        hot = jnp.where(taken & (side == which), 1.0, 0.0).astype(BF16)
        delivered_ref[:, which * 640 : which * 640 + 640] = dot_nn(hot, rows).astype(BF16)
    lasts = [copies.start(delivered_ref, delivered_hbm, None)]

    later_y = second_stage(1, stage_z)
    lasts += last_stage(0, later_z)
    lasts += last_stage(1, later_y)
    wait_all(lasts)
    wait_all(forwards)


def results_body(
    gx_hbm, both_hbm, arrived_hbm, gx_out, w_qkv_out, w_out_out, delivered_out,
    gx_in, gx_ref, both_ref, delivered_ref, sems,
):
    loads = [
        pltpu.make_async_copy(source, target, sems.at[index])
        for index, (source, target) in enumerate(
            (
                (gx_hbm.at[0], gx_in.at[0]), (gx_hbm.at[1], gx_in.at[1]),
                (both_hbm, both_ref), (arrived_hbm, delivered_ref),
            )
        )
    ]
    for load in loads:
        load.start()
    row = lax.broadcasted_iota(jnp.int32, (256, 256), 0)
    column = lax.broadcasted_iota(jnp.int32, (256, 256), 1)
    natural = jnp.where(row == 4 * (column % 64) + column // 64, 1.0, 0.0).astype(BF16)
    stores = []

    def store(source, target):
        stores.append(pltpu.make_async_copy(source, target, sems.at[4 + len(stores)]))
        stores[-1].start()

    for half in range(2):
        loads[half].wait()
        rows = gx_in[half].reshape(256, 1280)
        gx_ref[half] = dot_nn(natural, rows).astype(BF16)
        store(gx_ref.at[half], gx_out.at[half * 256 : half * 256 + 256, :])
    loads[2].wait()
    store(both_ref.at[0], w_qkv_out.at[0:2])
    store(both_ref.at[1, 1], w_qkv_out.at[2])
    store(both_ref.at[1, 0], w_out_out)
    loads[3].wait()
    store(delivered_ref, delivered_out)
    for copy in stores:
        copy.wait()


def halo_peers(section, chip, core):
    found = [dev(chip, 1 - core, section)]
    for step in (1, -1):
        for other in (core, 1 - core):
            found.append(dev(around(chip, step), other, section))
    return found


def row_peers(section, chip, core):
    found = []
    for step in range(4):
        for turn in range(2):
            if step or turn:
                found.append(dev(chip, (core + turn) % 2, (section + step) % 4))
    return found


def section_peers(section, chip, core):
    return [dev(chip, core, (section + step) % 4) for step in range(1, 4)]


def core_peers(section, chip, core):
    return [dev((chip + step) % 16, core, section) for step in range(1, 16)]


def plane_peers(section, chip, core):
    found = [dev(chip, 1 - core, section)]
    for step in range(1, 16):
        for turn in range(2):
            found.append(dev((chip + step) % 16, (core + turn) % 2, section))
    return found


def local(
    tokens, norm_gain, w_qkv, w_out, merge_gain, seg_blocks, mb_sizes, mb_receiver, merged_grad
):
    w_rows = w_qkv.transpose(0, 2, 1)
    q, kv, normed_t, w_full, q_rows, sums, norms = call(
        project_body,
        [
            (HBM, shape((PAIR, 1024))),
            (HBM, shape((2, PAIR, 3072))),
            (HBM, shape((1280, 512))),
            (HBM, shape((1280, 1280))),
            (HBM, shape((2, 1024, 128))),
            (HBM, shape((2, 1024, 128), F32)),
            (HBM, shape((4, 8, 128), F32)),
        ],
        [(SMEM, seg_blocks), (HBM, tokens), (HBM, norm_gain), (HBM, w_rows), (HBM, w_out)],
        [
            pltpu.VMEM((512, 1280), BF16),
            pltpu.VMEM((1280,), BF16),
            pltpu.VMEM((3, 320, 1280), BF16),
            pltpu.VMEM((1280, 512), BF16),
            pltpu.VMEM((3, 320, 512), BF16),
            pltpu.VMEM((PAIR, 1024), BF16),
            pltpu.VMEM((2, PAIR, 1024), BF16),
            pltpu.VMEM((2, 32, 128), jnp.int32),
            pltpu.VMEM((2, 1024, 128), BF16),
            pltpu.VMEM((2, 128, 1024), BF16),
            pltpu.VMEM((2, 1024, 128), BF16),
            pltpu.VMEM((2, 1024, 128), F32),
            pltpu.VMEM((4, 8, 128), F32),
        ],
        copies=40,
        number=1,
        limit=62,
    )
    o, op, log_total = call(
        forward_body,
        [
            (HBM, shape((PAIR, 1024))),
            (HBM, shape((2, 4, PAIR, 128))),
            (HBM, shape((2, 1024), F32)),
        ],
        [(SMEM, seg_blocks), (HBM, kv), (HBM, q_rows), (HBM, sums), (HBM, norms)],
        [
            pltpu.VMEM((2, 32, 128), jnp.int32),
            pltpu.SMEM((4, 2), jnp.int32),
            pltpu.VMEM((PAIR, 1024), BF16),
            pltpu.VMEM((2, PAIR, 3072), BF16),
            pltpu.VMEM((2, 1024, 128), BF16),
            pltpu.VMEM((2, 128, 3072), BF16),
            pltpu.VMEM((2, 3072, 128), BF16),
            pltpu.VMEM((2, 1024, 128), F32),
            pltpu.VMEM((4, 8, 128), F32),
            pltpu.VMEM((2, 4, PAIR, 128), BF16),
            pltpu.VMEM((2, 1024), F32),
        ],
        copies=9,
        limit=62,
    )
    gp, grad_layer, glt, att_own, table = call(
        middle_body,
        [
            (HBM, shape((2, 4, PAIR, 128))),
            (HBM, shape((128, 1280))),
            (HBM, shape((1280, 128))),
            (HBM, shape((4, PAIR, 128))),
            (HBM, shape((16, 16, 640))),
        ],
        [(HBM, op), (HBM, w_full), (HBM, w_out), (HBM, tokens), (HBM, merged_grad), (HBM, merge_gain)],
        [
            pltpu.VMEM((1280, 1280), BF16),
            pltpu.VMEM((512, 1280), BF16),
            pltpu.VMEM((128, 1280), BF16),
            pltpu.VMEM((1280,), BF16),
            pltpu.VMEM((128, 1280), BF16),
            pltpu.VMEM((1280, 128), BF16),
            pltpu.VMEM((1280, 128), BF16),
            pltpu.VMEM((1280, 128), BF16),
            pltpu.VMEM((16, 16, 640), BF16),
        ],
        copies=44,
        number=2,
        limit=62,
    )
    dq, dkv, start_rows, here, qrow, grow, gnat, spans = call(
        backward_body,
        [
            (HBM, shape((2, 1024, 128), F32)),
            (HBM, shape((2, PAIR, 2048))),
            (HBM, shape((512, 128), jnp.int32)),
            (HBM, shape((16, 512), jnp.int32)),
            (HBM, shape((2, 1024, 128))),
            (HBM, shape((2, 1024, 128))),
            (HBM, shape((PAIR, 1024))),
            (HBM, shape((2, 32, 128), jnp.int32)),
        ],
        [
            (SMEM, seg_blocks), (SMEM, mb_sizes), (SMEM, mb_receiver),
            (HBM, q), (HBM, kv), (HBM, o), (HBM, log_total), (HBM, gp),
        ],
        [
            pltpu.VMEM((2, 1024, 128), F32),
            pltpu.VMEM((2, PAIR, 2048), BF16),
            pltpu.VMEM((512, 128), jnp.int32),
            pltpu.VMEM((16, 512), jnp.int32),
            pltpu.VMEM((2, 1024, 128), BF16),
            pltpu.VMEM((2, 1024, 128), BF16),
            pltpu.VMEM((PAIR, 1024), BF16),
            pltpu.VMEM((2, 32, 128), jnp.int32),
            pltpu.SMEM((4, 2), jnp.int32),
            pltpu.VMEM((PAIR, 1024), BF16),
            pltpu.VMEM((2, PAIR, 3072), BF16),
            pltpu.VMEM((PAIR, 1024), BF16),
            pltpu.VMEM((2, 1024), F32),
            pltpu.VMEM((2, 4, PAIR, 128), BF16),
            pltpu.VMEM((2, 128, 2048), BF16),
            pltpu.VMEM((2, 128, 2048), BF16),
            pltpu.VMEM((2, 2048, 128), BF16),
            pltpu.VMEM((2, HEAD_DIM, 2048), F32),
            pltpu.VMEM((2, HEAD_DIM, 2048), F32),
        ],
        copies=14,
        limit=62,
    )
    arrived, gx_all, weights = call(
        tail_body,
        [
            (HBM, shape((256, 1280))),
            (HBM, shape((2, 4, 64, 1280))),
            (HBM, shape((2, 2, 40, 320), F32)),
        ],
        [
            (HBM, dkv), (HBM, start_rows), (HBM, here), (HBM, dq), (HBM, qrow), (HBM, grow),
            (HBM, gnat), (HBM, spans), (HBM, q), (HBM, kv), (HBM, glt), (HBM, op), (HBM, att_own),
            (HBM, table), (HBM, grad_layer), (HBM, tokens), (HBM, norm_gain), (HBM, w_rows),
            (HBM, normed_t),
        ],
        [
            pltpu.VMEM((512, 128), jnp.int32),
            pltpu.VMEM((16, 512), jnp.int32),
            pltpu.VMEM((2, 1024, 128), BF16),
            pltpu.VMEM((2, 1024, 128), BF16),
            pltpu.VMEM((PAIR, 1024), BF16),
            pltpu.VMEM((2, 32, 128), jnp.int32),
            pltpu.VMEM((1280,), BF16),
            pltpu.VMEM((256, 1280), BF16),
            pltpu.VMEM((16, 16, 640), BF16),
            pltpu.VMEM((128, 1280), BF16),
            pltpu.VMEM((512, 1280), BF16),
            pltpu.VMEM((3, 320, 1280), BF16),
            pltpu.VMEM((1280, 512), BF16),
            pltpu.VMEM((PAIR, 1024), BF16),
            pltpu.VMEM((2, PAIR, 1024), BF16),
            pltpu.VMEM((2, 128, 1024), BF16),
            pltpu.VMEM((2, 128, 1024), BF16),
            pltpu.VMEM((2, 1024, 128), BF16),
            pltpu.VMEM((2, HEAD_DIM, 1024), F32),
            pltpu.VMEM((2, HEAD_DIM, 1024), F32),
            pltpu.VMEM((2, 1024, 128), F32),
            pltpu.VMEM((2, 2, 3, PAIR, 256), BF16),
            pltpu.VMEM((2, 3, PAIR, 256), BF16),
            pltpu.VMEM((2, 2, 2, 2, PAIR, 256), BF16),
            pltpu.VMEM((960, 512), BF16),
            pltpu.VMEM((256, 960), BF16),
            pltpu.VMEM((2, 4, 64, 1280), BF16),
            pltpu.VMEM((2, 2, 32, 1280), BF16),
            pltpu.VMEM((2, 2, 64, 1280), BF16),
            pltpu.VMEM((2, 64, 1280), BF16),
            pltpu.VMEM((320, 512), BF16),
            pltpu.VMEM((1280, 512), BF16),
            pltpu.VMEM((32, 16, 640), BF16),
            pltpu.VMEM((32, 16, 640), BF16),
            pltpu.VMEM((4, 4, 80, 320), F32),
            pltpu.VMEM((2, 4, 4, 80, 320), BF16),
            pltpu.VMEM((2, 4, 4, 80, 320), BF16),
            pltpu.VMEM((2, 4, 4, 80, 320), BF16),
            pltpu.VMEM((2, 3, 4, 80, 320), BF16),
            pltpu.VMEM((2, 4, 80, 320), BF16),
            pltpu.VMEM((2, 3, 80, 320), BF16),
            pltpu.VMEM((2, 80, 320), F32),
        ],
        copies=124,
        number=3,
        limit=62,
    )
    grad_x, grad_w_qkv, grad_w_out, delivered = call(
        results_body,
        [
            (HBM, shape((512, 1280))),
            (HBM, shape((3, 40, 320), F32)),
            (HBM, shape((40, 320), F32)),
            (HBM, shape((256, 1280))),
        ],
        [(HBM, gx_all), (HBM, weights), (HBM, arrived)],
        [
            pltpu.VMEM((2, 4, 64, 1280), BF16),
            pltpu.VMEM((2, 256, 1280), BF16),
            pltpu.VMEM((2, 2, 40, 320), F32),
            pltpu.VMEM((256, 1280), BF16),
        ],
        copies=10,
        limit=62,
    )
    return (delivered, grad_x, grad_w_qkv, grad_w_out.T)


def solution(mesh):
    placed = (
        P("seq", None),
        P(),
        P(None, None, "section"),
        P("section", None),
        P(),
        P(),
        P(),
        P(),
        P("seq", None),
    )
    return jax.shard_map(
        local,
        mesh=mesh,
        in_specs=placed,
        out_specs=(
            P("seq", "section"),
            P("seq", None),
            P(None, "seq", "section"),
            P("section", "seq"),
        ),
        check_vma=False,
    )
```

```python
import math

import jax
import jax.numpy as jnp
from jax import lax
from jax.experimental import pallas as pl
from jax.experimental.pallas import tpu as pltpu
from jax.sharding import PartitionSpec as P

HEADS = 16
EPS = 1e-06
HEAD_DIM = 80
PAIR = 160
BIG = -1e30
CHUNK = 256
SAFE = 60.0
BF16 = jnp.bfloat16
F32 = jnp.float32
MESH = pl.DeviceIdType.MESH
FACTOR = HEAD_DIM ** -0.5
LOG2E = 1.0 / math.log(2.0)
SCALE = FACTOR * LOG2E


def dot_nn(left, right):
    return lax.dot_general(left, right, (((1,), (0,)), ((), ())), preferred_element_type=F32)


def dot_nt(left, right):
    return lax.dot_general(left, right, (((1,), (1,)), ((), ())), preferred_element_type=F32)


def place():
    section = lax.axis_index("section")
    seq = lax.axis_index("seq")
    return section, seq // 2, seq % 2


def shape(dims, dtype=BF16):
    return jax.ShapeDtypeStruct(dims, dtype)


class Copies:
    def __init__(self, send_sems, recv_sems):
        self.send_sems, self.recv_sems, self.used = send_sems, recv_sems, 0

    def start(self, source, target, device):
        index = self.used
        self.used = index + 1
        if device is None:
            copy = pltpu.make_async_copy(source, target, self.recv_sems.at[index])
        else:
            copy = pltpu.make_async_remote_copy(
                src_ref=source,
                dst_ref=target,
                send_sem=self.send_sems.at[index],
                recv_sem=self.recv_sems.at[index],
                device_id=device,
                device_id_type=MESH,
            )
        copy.start()
        return copy


def wait_all(copies):
    for copy in copies:
        copy.wait()


def greet(peers):
    barrier = pltpu.get_barrier_semaphore()
    for peer in peers:
        pl.semaphore_signal(barrier, inc=1, device_id=peer, device_id_type=MESH)


def greeted(peers):
    pl.semaphore_wait(pltpu.get_barrier_semaphore(), len(peers))


VMEM = pl.BlockSpec(memory_space=pltpu.VMEM)
SMEM = pl.BlockSpec(memory_space=pltpu.SMEM)
HBM = pl.BlockSpec(memory_space=pltpu.HBM)


def call(body, outs, ins, scratch=(), copies=0, number=None, limit=14):
    more = {} if number is None else {"collective_id": number, "has_side_effects": True}
    semaphores = [pltpu.SemaphoreType.DMA((copies,))] * (0 if not copies else 1 if number is None else 2)
    return pl.pallas_call(
        body,
        out_shape=[array for _, array in outs],
        in_specs=[place for place, _ in ins],
        out_specs=[place for place, _ in outs],
        scratch_shapes=list(scratch) + semaphores,
        compiler_params=pltpu.CompilerParams(vmem_limit_bytes=limit << 20, **more),
    )(*[array for _, array in ins])


def dev(chip, core, section):
    return (chip * 2 + core, section)


def around(chip, step):
    return (chip + step + 16) % 16


def project_body(
    seg_ref, tokens_hbm, gain_hbm, w_hbm, w_out_hbm,
    q_hbm, kv_hbm, normed_t_hbm, w_full, qrow_hbm, sums_hbm, norms_hbm,
    tokens_ref, gain_ref, w_ref, normed_t_ref, out_ref,
    q_ref, kv_ref, spans_ref, qrow, kx, vrow, sums_ref, norms_ref, send, recv,
):
    section, chip, core = place()
    copies = Copies(send, recv)
    peers = halo_peers(section, chip, core) + section_peers(section, chip, core)[::2]
    greet(peers)
    load_gain = copies.start(gain_hbm, gain_ref, None)
    load_tokens = []
    for tile in range(4):
        rows = pl.ds(tile * 128, 128)
        load_tokens.append(copies.start(tokens_hbm.at[rows, :], tokens_ref.at[rows, :], None))
    load_w = {which: copies.start(w_hbm.at[which], w_ref.at[which], None) for which in (1, 2, 0)}
    greeted(peers)
    mate = dev(chip, 1 - core, section)
    ahead, behind = (section + 1) % 4, (section + 3) % 4
    ahead_dev, behind_dev = dev(chip, core, ahead), dev(chip, core, behind)

    def w_rows(owner, start, count):
        return w_full.at[pl.ds(pl.multiple_of(owner * 320 + core * PAIR + start, 16), count), :]

    def mine(start):
        return w_out_hbm.at[pl.ds(pl.multiple_of(core * PAIR + start, 16), 80), :]

    to_ahead = copies.start(mine(0), w_rows(section, 0, 80), ahead_dev)
    to_behind = copies.start(mine(80), w_rows(section, 80, 80), behind_dev)
    rest_ahead = copies.start(mine(80), w_rows(section, 80, 80), ahead_dev)
    rest_behind = copies.start(mine(0), w_rows(section, 0, 80), behind_dev)
    waits, inner = [], []
    load_gain.wait()
    gain = gain_ref[...].reshape(1, 1280).astype(F32)
    for tile in range(4):
        rows = pl.ds(tile * 128, 128)
        load_tokens[tile].wait()
        values = tokens_ref[rows, :].astype(F32)
        centered = values - jnp.mean(values, axis=1, keepdims=True)
        inv = lax.rsqrt(jnp.mean(centered * centered, axis=1, keepdims=True) + EPS)
        normed_t_ref[:, rows] = (centered * inv * gain).astype(BF16).T
    own = pl.ds(pl.multiple_of(core * PAIR, 16), PAIR)
    other = pl.ds(pl.multiple_of((1 - core) * PAIR, 16), PAIR)
    for which in (1, 2, 0):
        load_w[which].wait()
        out = dot_nn(w_ref[which], normed_t_ref[...])
        out_ref[which] = out.astype(BF16)
        mine = pl.ds(pl.multiple_of(core * 512, 512), 512)
        target = q_ref.at[:, mine]
        if which:
            for step, base in ((1, 0), (-1, 2048)):
                lanes = pl.ds(pl.multiple_of(base + core * 512, 512), 512)
                for rows, to_core in ((own, core), (other, 1 - core)):
                    device = dev(around(chip, step), to_core, section)
                    waits.append(
                        copies.start(out_ref.at[which, rows, :], kv_hbm.at[which - 1, :, lanes], device)
                    )
            target = kv_ref.at[which - 1, :, mine]
        inner.append(copies.start(out_ref.at[which, other, :], target, mate))
        inner.append(copies.start(out_ref.at[which, own, :], target, None))
    waits.append(copies.start(normed_t_ref, normed_t_hbm, None))
    image_spans(seg_ref, spans_ref)
    wait_all(inner)
    waits.append(copies.start(q_ref, q_hbm, None))
    waits.append(copies.start(kv_ref, kv_hbm.at[:, :, 1024:2048], None))
    first = chip * 1024
    for block in range(4):
        lanes = pl.ds(block * 256, 256)
        build_queries(spans_ref, first + block * 256, q_ref, lanes, qrow)
        build_values(spans_ref, first + block * 256, kv_ref, lanes, kx, vrow, lanes)
    for head in range(2):
        feats = pl.ds(head * HEAD_DIM, HEAD_DIM)
        for which, values in enumerate((q_ref[feats, :], kv_ref[0, feats, :])):
            norms_ref[which * 2 + head, :, :] = squares(values)

    def tile_step(tile, carry):
        rows = pl.ds(pl.multiple_of(tile * 256, 256), 256)
        sums = (jnp.zeros((256, 128), F32),) * 2
        for chunk in range(0, 4, 2):
            lanes = [pl.ds((chunk + which) * CHUNK, CHUNK) for which in range(2)]
            sums = forward_step(rows, lanes, qrow, kx, vrow, sums)
        for head in range(2):
            sums_ref[head, rows, :] = sums[head]
        return carry

    lax.fori_loop(0, 2, tile_step, 0)
    to_ahead.wait()
    relay = [copies.start(w_rows(behind, 0, 80), w_rows(behind, 0, 80), ahead_dev)]
    to_behind.wait()
    relay.append(copies.start(w_rows(ahead, 80, 80), w_rows(ahead, 80, 80), behind_dev))
    lax.fori_loop(2, 4, tile_step, 0)
    waits.append(copies.start(qrow, qrow_hbm, None))
    waits.append(copies.start(sums_ref, sums_hbm, None))
    waits.append(copies.start(norms_ref, norms_hbm, None))
    rest_ahead.wait()
    waits.append(copies.start(w_rows(behind, 0, PAIR), w_rows(behind, 0, PAIR), mate))
    rest_behind.wait()
    waits.append(copies.start(w_rows(ahead, 0, PAIR), w_rows(ahead, 0, PAIR), mate))
    far = (section + 2) % 4
    for copy, start in zip(relay, (0, 80)):
        copy.wait()
        waits.append(copies.start(w_rows(far, start, 80), w_rows(far, start, 80), mate))
    wait_all(waits)


def image_spans(seg_ref, spans_ref):
    row = lax.broadcasted_iota(jnp.int32, (32, 128), 0)
    begins, ends = jnp.zeros((32, 128), jnp.int32), jnp.zeros((32, 128), jnp.int32)
    end = jnp.int32(0)
    for image in range(32):
        begin = end
        end = begin + 64 * seg_ref[image]
        begins = jnp.where(row == image, begin, begins)
        ends = jnp.where(row == image, end, ends)
    spans_ref[0] = begins
    spans_ref[1] = ends


def squares(values):
    values = values.astype(F32)
    total = jnp.sum(values * values, axis=0, keepdims=True)
    blocks = [total[:, start : start + 128] for start in range(0, total.shape[1], 128)]
    top = blocks[0]
    for block in blocks[1:]:
        top = jnp.maximum(top, block)
    return jnp.broadcast_to(top, (8, 128))


def build_queries(spans_ref, position, q_ref, lanes, qrow):
    inside = membership(spans_ref, position, 256)
    for head in range(2):
        joined = jnp.concatenate(
            [
                q_ref[pl.ds(head * HEAD_DIM, HEAD_DIM), lanes],
                jnp.where(inside, 0.0, BIG).astype(BF16),
                jnp.zeros((16, 256), BF16),
            ],
            axis=0,
        )
        qrow[head, lanes, :] = joined.T


def build_values(spans_ref, position, kv_ref, lanes, kx, vrow, into):
    ones = jnp.where(lax.broadcasted_iota(jnp.int32, (16, CHUNK), 0) < 3, 1.0, 0.0).astype(BF16)
    hot = jnp.where(membership(spans_ref, position, CHUNK), 1.0, 0.0).astype(BF16)
    for head in range(2):
        feats = pl.ds(head * HEAD_DIM, HEAD_DIM)
        kx[head, :, into] = jnp.concatenate([kv_ref[0, feats, lanes], hot, ones], axis=0)
        joined = jnp.concatenate(
            [kv_ref[1, feats, lanes], ones, jnp.zeros((32, CHUNK), BF16)], axis=0
        )
        vrow[head, into, :] = joined.T


def forward_step(rows, chunks, qrow, kx, vrow, sums):
    pairs = [(head, lanes) for lanes in chunks for head in range(2)]
    probs = [
        jnp.exp2(dot_nn(qrow[head, rows, :], kx[head, :, lanes]) * SCALE).astype(BF16)
        for head, lanes in pairs
    ]
    sums = list(sums)
    for (head, lanes), part in zip(pairs, probs):
        sums[head] = sums[head] + dot_nn(part, vrow[head, lanes, :])
    return tuple(sums)


def spans_and_bounds(seg_ref, first, spans_ref, bounds_ref):
    row = lax.broadcasted_iota(jnp.int32, (32, 128), 0)
    begins, ends = jnp.zeros((32, 128), jnp.int32), jnp.zeros((32, 128), jnp.int32)
    end = jnp.int32(0)
    low = [jnp.int32(0)] * 4
    high = [jnp.int32(16384)] * 4
    for image in range(32):
        begin = end
        end = begin + 64 * seg_ref[image]
        begins = jnp.where(row == image, begin, begins)
        ends = jnp.where(row == image, end, ends)
        for tile in range(4):
            start = first + 256 * tile
            low[tile] = jnp.where(begin <= start, begin, low[tile])
            high[tile] = jnp.where((begin < start + 256) & (end >= start + 256), end, high[tile])
    spans_ref[0] = begins
    spans_ref[1] = ends
    for tile in range(4):
        bounds_ref[tile, 0] = (low[tile] - (first - 1024)) // CHUNK
        bounds_ref[tile, 1] = (high[tile] - (first - 1024) + CHUNK - 1) // CHUNK


def membership(spans_ref, first, count):
    spots = first + lax.broadcasted_iota(jnp.int32, (32, count), 1)
    return (spots >= spans_ref[0, :, 0:1]) & (spots < spans_ref[1, :, 0:1])


def three_parts(row):
    high = row.astype(BF16)
    rest = row - high.astype(F32)
    middle = rest.astype(BF16)
    low = (rest - middle.astype(F32)).astype(BF16)
    return jnp.concatenate([high, middle, low, jnp.zeros((13, row.shape[1]), BF16)], axis=0)


def permutation(transposed):
    moved = lax.broadcasted_iota(jnp.int32, (512, 1) if transposed else (1, 512), 0 if transposed else 1)
    natural = lax.broadcasted_iota(jnp.int32, (512, 512), 1 if transposed else 0)
    return jnp.where(natural == 4 * (moved % 128) + moved // 128, 1.0, 0.0).astype(BF16)


def forward_body(
    seg_ref, kv_hbm, qrow_hbm, sums_hbm, norms_hbm, o_hbm, op_hbm, log_hbm,
    spans_ref, bounds_ref, o_ref, kv_ref, qrow, kx, vrow, sums_ref, norms_ref, op_ref, log_ref, sems,
):
    first = (lax.axis_index("seq") // 2) * 1024
    loads = [
        pltpu.make_async_copy(source, target, sems.at[index])
        for index, (source, target) in enumerate(
            (
                (kv_hbm.at[:, :, 0:1024], kv_ref.at[:, :, 0:1024]),
                (kv_hbm.at[:, :, 2048:3072], kv_ref.at[:, :, 2048:3072]),
                (qrow_hbm, qrow),
                (norms_hbm, norms_ref),
                (sums_hbm, sums_ref),
            )
        )
    ]
    for load in loads:
        load.start()
    spans_and_bounds(seg_ref, first, spans_ref, bounds_ref)
    perm = permutation(False)
    for load in loads:
        load.wait()

    def outside(low, high, step, carry):
        carry = lax.fori_loop(low, jnp.minimum(high, 4), step, carry)
        return lax.fori_loop(jnp.maximum(low, 8), high, step, carry)

    def build(chunk, tops):
        lanes = pl.ds(pl.multiple_of(chunk * CHUNK, CHUNK), CHUNK)
        build_values(spans_ref, first - 1024 + chunk * CHUNK, kv_ref, lanes, kx, vrow, lanes)
        return tuple(
            jnp.maximum(tops[head], squares(kv_ref[0, pl.ds(head * HEAD_DIM, HEAD_DIM), lanes]))
            for head in range(2)
        )

    tops = outside(bounds_ref[0, 0], bounds_ref[3, 1], build, (norms_ref[2], norms_ref[3]))
    limit = (SAFE / SCALE) ** 2
    small = jnp.max(norms_ref[0]) * jnp.max(tops[0]) <= limit
    small = small & (jnp.max(norms_ref[1]) * jnp.max(tops[1]) <= limit)

    def write(head, rows, sums, top_row):
        out = sums.T
        total_row = out[80:81, :]
        o_ref[pl.ds(head * HEAD_DIM, HEAD_DIM), rows] = (out[:80] * (1.0 / total_row)).astype(BF16)
        log_ref[head : head + 1, rows] = top_row + jnp.log(total_row) * (LOG2E / SCALE)

    def plain_step(tile, carry):
        rows = pl.ds(pl.multiple_of(tile * 256, 256), 256)

        def step(chunk, sums):
            lanes = pl.ds(pl.multiple_of(chunk * CHUNK, CHUNK), CHUNK)
            return forward_step(rows, [lanes], qrow, kx, vrow, sums)

        start = (sums_ref[0, rows, :], sums_ref[1, rows, :])
        sums = outside(bounds_ref[tile, 0], bounds_ref[tile, 1], step, start)
        for head in range(2):
            write(head, rows, sums[head], 0.0)
        return carry

    lane = lax.broadcasted_iota(jnp.int32, (256, 128), 1)

    def shifted_step(tile, carry):
        low, high = bounds_ref[tile, 0], bounds_ref[tile, 1]
        rows = pl.ds(pl.multiple_of(tile * 256, 256), 256)

        def score_step(chunk, tops):
            lanes = pl.ds(pl.multiple_of(chunk * CHUNK, CHUNK), CHUNK)
            found = []
            for head in range(2):
                part = dot_nn(qrow[head, rows, :], kx[head, :, lanes])
                found.append(jnp.maximum(tops[head], jnp.maximum(part[:, :128], part[:, 128:])))
            return tuple(found)

        start = jnp.full((256, 128), BIG, F32)
        tops = lax.fori_loop(low, high, score_step, (start, start))
        for head in range(2):
            shift = -jnp.max(tops[head], axis=1, keepdims=True)
            part_one = shift.astype(BF16).astype(F32)
            part_two = (shift - part_one).astype(BF16).astype(F32)
            part_three = shift - part_one - part_two
            moved = jnp.where(lane == 112, part_one, qrow[head, rows, :].astype(F32))
            moved = jnp.where(lane == 113, part_two, moved)
            qrow[head, rows, :] = jnp.where(lane == 114, part_three, moved).astype(BF16)

        def step(chunk, sums):
            lanes = pl.ds(pl.multiple_of(chunk * CHUNK, CHUNK), CHUNK)
            return forward_step(rows, [lanes], qrow, kx, vrow, sums)

        start = jnp.zeros((256, 128), F32)
        sums = lax.fori_loop(low, high, step, (start, start))
        for head in range(2):
            write(head, rows, sums[head], jnp.max(tops[head].T, axis=0, keepdims=True))
        return carry

    @pl.when(small)
    def _():
        lax.fori_loop(0, 4, plain_step, 0)

    @pl.when(jnp.logical_not(small))
    def _():
        middle = pltpu.make_async_copy(
            kv_hbm.at[:, :, 1024:2048], kv_ref.at[:, :, 1024:2048], sems.at[5]
        )
        middle.start()
        middle.wait()
        for chunk in range(4, 8):
            lanes = pl.ds(chunk * CHUNK, CHUNK)
            build_values(spans_ref, first - 1024 + chunk * CHUNK, kv_ref, lanes, kx, vrow, lanes)
        lax.fori_loop(0, 4, shifted_step, 0)

    keep_o = pltpu.make_async_copy(o_ref, o_hbm, sems.at[6])
    keep_log = pltpu.make_async_copy(log_ref, log_hbm, sems.at[7])
    keep_o.start()
    keep_log.start()
    for half in range(2):
        moved = dot_nn(o_ref[:, half * 512 : half * 512 + 512], perm).astype(BF16)
        for part in range(4):
            op_ref[half, part] = moved[:, part * 128 : part * 128 + 128]
    keep_op = pltpu.make_async_copy(op_ref, op_hbm, sems.at[8])
    keep_op.start()
    keep_o.wait()
    keep_log.wait()
    keep_op.wait()


def build_keys(spans_ref, position, kv_ref, lanes, kx, vx, krow, into):
    ones = jnp.where(lax.broadcasted_iota(jnp.int32, (16, CHUNK), 0) < 3, 1.0, 0.0).astype(BF16)
    hot = jnp.where(membership(spans_ref, position, CHUNK), 1.0, 0.0).astype(BF16)
    for head in range(2):
        feats = pl.ds(head * HEAD_DIM, HEAD_DIM)
        keys = jnp.concatenate([kv_ref[0, feats, lanes], hot, ones], axis=0)
        kx[head, :, into] = keys
        krow[head, into, :] = keys.T
        vx[head, :, into] = jnp.concatenate(
            [kv_ref[1, feats, lanes], ones, jnp.zeros((32, CHUNK), BF16)], axis=0
        )


def backward_step(rows, chunks, q_ref, g_ref, qrow, grow, kx, vx, krow, dk_acc, dv_acc, sums):
    pairs = [(head, lanes) for lanes in chunks for head in range(2)]
    feats = [pl.ds(head * HEAD_DIM, HEAD_DIM) for head in range(2)]
    probs = [
        jnp.exp2(dot_nn(qrow[head, rows, :], kx[head, :, lanes]) * SCALE) for head, lanes in pairs
    ]
    shifted = [dot_nn(grow[head, rows, :], vx[head, :, lanes]) for head, lanes in pairs]
    dscores = [(prob * part).astype(BF16) for prob, part in zip(probs, shifted)]
    weights = [prob.astype(BF16) for prob in probs]
    dk = [dot_nn(q_ref[feats[head], rows], part) for (head, _), part in zip(pairs, dscores)]
    dv = [dot_nn(g_ref[feats[head], rows], part) for (head, _), part in zip(pairs, weights)]
    sums = list(sums)
    for (head, lanes), part in zip(pairs, dscores):
        sums[head] = sums[head] + dot_nn(part, krow[head, lanes, :])
    for (head, lanes), dk_part, dv_part in zip(pairs, dk, dv):
        dk_acc[head, :, lanes] += dk_part
        dv_acc[head, :, lanes] += dv_part
    return tuple(sums)


def backward_body(
    seg_ref, sizes_ref, receiver_ref, q_hbm, kv_hbm, o_hbm, log_hbm, gp_hbm,
    dq_hbm, dkv_hbm, starts_hbm, here_hbm, qrow_hbm, grow_hbm, gnat_hbm, spans_hbm,
    dq_ref, dkv_ref, starts_ref, here_ref, qrow, grow, gnat, spans_ref, bounds_ref, q_ref, kv_ref, o_ref, log_ref, gp_ref, kx, vx, krow, dk_acc, dv_acc, sems,
):
    seq = lax.axis_index("seq")
    first = (seq // 2) * 1024
    load_kv = pltpu.make_async_copy(kv_hbm.at[:, :, 0:1024], kv_ref.at[:, :, 0:1024], sems.at[0])
    load_kv_after = pltpu.make_async_copy(
        kv_hbm.at[:, :, 2048:3072], kv_ref.at[:, :, 2048:3072], sems.at[13]
    )
    load_o = pltpu.make_async_copy(o_hbm, o_ref, sems.at[1])
    load_q = pltpu.make_async_copy(q_hbm, q_ref, sems.at[2])
    load_o.start()
    load_q.start()
    load_log = pltpu.make_async_copy(log_hbm, log_ref, sems.at[3])
    load_log.start()
    load_gp = pltpu.make_async_copy(gp_hbm, gp_ref, sems.at[4])
    load_gp.start()
    load_kv.start()
    load_kv_after.start()
    spans_and_bounds(seg_ref, first, spans_ref, bounds_ref)
    start = jnp.int32(0)
    my_start, my_size = jnp.int32(0), jnp.int32(0)
    for batch in range(32):
        size, receiver = sizes_ref[batch], receiver_ref[batch]
        starts_ref[pl.ds(pl.multiple_of(receiver * 16, 16), 16), :] = jnp.full((16, 128), start)
        my_start = jnp.where(receiver == seq, start, my_start)
        my_size = jnp.where(receiver == seq, size, my_size)
        start = start + size
    here_ref[0:8, :] = jnp.full((8, 512), my_start)
    here_ref[8:16, :] = jnp.full((8, 512), my_size)
    back = permutation(True)
    load_gp.wait()
    for half in range(2):
        joined = jnp.concatenate([gp_ref[half, part] for part in range(4)], axis=1)
        gnat[:, half * 512 : half * 512 + 512] = dot_nn(joined, back).astype(BF16)
    load_kv.wait()
    load_kv_after.wait()
    load_o.wait()
    load_q.wait()
    load_log.wait()
    for head in range(2):
        feats = pl.ds(head * HEAD_DIM, HEAD_DIM)
        for block in range(4):
            lanes = pl.ds(block * 256, 256)
            inside = membership(spans_ref, first + block * 256, 256)
            joined = jnp.concatenate(
                [
                    q_ref[feats, lanes],
                    jnp.where(inside, 0.0, BIG).astype(BF16),
                    three_parts(-log_ref[head : head + 1, lanes]),
                ],
                axis=0,
            )
            qrow[head, lanes, :] = joined.T
            grads = gnat[feats, lanes]
            delta = jnp.sum(
                grads.astype(F32) * o_ref[feats, lanes].astype(F32), axis=0, keepdims=True
            )
            joined = jnp.concatenate(
                [grads, three_parts(-delta), jnp.zeros((32, 256), BF16)], axis=0
            )
            grow[head, lanes, :] = joined.T

    keeps = [
        pltpu.make_async_copy(source, target, sems.at[5 + index])
        for index, (source, target) in enumerate(
            (
                (starts_ref, starts_hbm), (here_ref, here_hbm), (spans_ref, spans_hbm),
                (gnat, gnat_hbm), (qrow, qrow_hbm), (grow, grow_hbm),
            )
        )
    ]
    for keep in keeps:
        keep.start()

    def outside(low, high, step, carry):
        carry = lax.fori_loop(low, jnp.minimum(high, 4), step, carry)
        return lax.fori_loop(jnp.maximum(low, 8), high, step, carry)

    def place_of(chunk):
        return pl.ds(pl.multiple_of(jnp.where(chunk < 4, chunk, chunk - 4) * CHUNK, CHUNK), CHUNK)

    def build(chunk, carry):
        lanes = pl.ds(pl.multiple_of(chunk * CHUNK, CHUNK), CHUNK)
        build_keys(
            spans_ref, first - 1024 + chunk * CHUNK, kv_ref, lanes, kx, vx, krow, place_of(chunk)
        )
        return carry

    outside(bounds_ref[0, 0], bounds_ref[3, 1], build, 0)
    dk_acc[...] = jnp.zeros_like(dk_acc)
    dv_acc[...] = jnp.zeros_like(dv_acc)

    def tile_step(tile, carry):
        rows = pl.ds(pl.multiple_of(tile * 256, 256), 256)

        def step(chunk, sums):
            return backward_step(
                rows, [place_of(chunk)], q_ref, gnat, qrow, grow, kx, vx, krow, dk_acc, dv_acc, sums
            )

        start = jnp.zeros((256, 128), F32)
        sums = outside(bounds_ref[tile, 0], bounds_ref[tile, 1], step, (start, start))
        for head in range(2):
            dq_ref[head, rows, :] = sums[head]
        return carry

    lax.fori_loop(0, 4, tile_step, 0)
    keeps.append(pltpu.make_async_copy(dq_ref, dq_hbm, sems.at[12]))
    keeps[-1].start()
    for head in range(2):
        feats = pl.ds(head * HEAD_DIM, HEAD_DIM)
        dkv_ref[0, feats, :] = (dk_acc[head] * FACTOR).astype(BF16)
        dkv_ref[1, feats, :] = dv_acc[head].astype(BF16)
    keeps.append(pltpu.make_async_copy(dkv_ref, dkv_hbm, sems.at[11]))
    keeps[-1].start()
    for keep in keeps:
        keep.wait()


def middle_body(
    op_ref, w_hbm, w_out_hbm, tokens_hbm, mgrad_hbm, gain_hbm,
    gp_ref, gl_hbm, glt_hbm, own_ref, table_ref,
    w_ref, tokens_ref, mgrad_ref, gain_ref, gl_ref, glt_ref, att, gat, packed, send, recv,
):
    section, chip, core = place()
    copies = Copies(send, recv)
    peers = row_peers(section, chip, core) + core_peers(section, chip, core)
    greet(peers)
    columns = pl.ds(pl.multiple_of(section * 1280, 128), 1280)
    load_gain = copies.start(gain_hbm, gain_ref, None)
    load_mgrad = copies.start(mgrad_hbm.at[:, columns], mgrad_ref, None)
    load_tokens = copies.start(tokens_hbm, tokens_ref, None)
    loads = []
    for step in range(4):
        w_rows = pl.ds(pl.multiple_of((section + step) % 4 * 320, 16), 320)
        source = w_hbm.at[w_rows, :] if step else w_out_hbm
        loads.append(copies.start(source, w_ref.at[w_rows, :], None))
    greeted(peers)
    rows = pl.ds(pl.multiple_of((section * 2 + core) * PAIR, 16), PAIR)
    waits = []
    for step in (2, 1, 3, 0):
        for turn in range(2):
            to_section, to_core = (section + step) % 4, (core + turn) % 2
            device = dev(chip, to_core, to_section) if step or turn else None
            waits.append(copies.start(op_ref.at[to_core, to_section], att.at[rows, :], device))
    late = [copies.start(op_ref.at[1 - core], own_ref, dev(chip, 1 - core, section))]
    row = lax.broadcasted_iota(jnp.int32, (128, 512), 0)
    column = lax.broadcasted_iota(jnp.int32, (128, 512), 1)
    chosen = jnp.where(column == 4 * row + section, 1.0, 0.0).astype(BF16)
    load_tokens.wait()
    load_gain.wait()
    load_mgrad.wait()
    values = dot_nn(chosen, tokens_ref[...])
    gain = gain_ref[...].reshape(1, 1280).astype(F32)
    scaled = mgrad_ref[...].astype(F32) * gain
    scaled_mean = jnp.mean(scaled, axis=1, keepdims=True)
    row = lax.broadcasted_iota(jnp.int32, (128, 128), 0)
    column = lax.broadcasted_iota(jnp.int32, (128, 128), 1)
    order = jnp.where(column == 16 * (row % 8) + row // 8, 1.0, 0.0).astype(BF16)
    wait_all(loads)
    wait_all(waits)
    layer = values + dot_nn(att[...].T, w_ref[...])
    centered = layer - jnp.mean(layer, axis=1, keepdims=True)
    inv = lax.rsqrt(jnp.mean(centered * centered, axis=1, keepdims=True) + EPS)
    unit = centered * inv
    grad_layer = inv * (
        scaled - scaled_mean - unit * jnp.mean(scaled * unit, axis=1, keepdims=True)
    )
    grad_layer = grad_layer.astype(BF16)
    gat[...] = dot_nt(w_ref[...], grad_layer).astype(BF16)
    for step in (2, 1, 3, 0):
        for turn in range(2):
            to_section, to_core = (section + step) % 4, (core + turn) % 2
            device = dev(chip, to_core, to_section) if step or turn else None
            rows = pl.ds(pl.multiple_of((to_section * 2 + to_core) * PAIR, 16), PAIR)
            late.append(copies.start(gat.at[rows, :], gp_ref.at[core, section], device))
    moved = dot_nn(order, (unit * gain).astype(BF16))
    for chip_to in range(16):
        eight = moved[chip_to * 8 : chip_to * 8 + 8]
        packed[chip_to] = jnp.concatenate([eight[:, :640], eight[:, 640:]], axis=0).astype(BF16)
    for step in range(16):
        to_chip = (chip + step) % 16
        device = dev(to_chip, core, section) if step else None
        late.append(copies.start(packed.at[to_chip], table_ref.at[chip], device))
    gl_ref[...] = grad_layer
    glt_ref[...] = grad_layer.T
    late.append(copies.start(gl_ref, gl_hbm, None))
    late.append(copies.start(glt_ref, glt_hbm, None))
    wait_all(late)


def tail_body(
    dkv_ref, starts_hbm, live_hbm, dq_hbm, qrow_hbm, grow_hbm, gnat_hbm, spans_hbm, q_hbm, kv_hbm,
    glt_hbm, op_hbm, own_hbm, table_hbm, gl_hbm, tokens_hbm, gain_hbm, w_hbm, normed_t_hbm,
    delivered_hbm, gx_all, weights_ref,
    starts_ref, live_ref, qrow, grow, gnat, spans_ref, gain_ref, delivered_ref,
    table_ref, gl_ref, tokens_ref, w_ref, normed_t_ref,
    q_ref, kv_ref, kx, vx, krow, dk_acc, dv_acc, dq_acc, own_out, mate_in,
    dkv_in, dj, rows_ref, gn, relay_in, gn_in, gx_own, att, glt,
    parcels, arrived, p_mine, p_away, p_in,
    summed, stage_in, subtotal, late_in, total, send, recv,
):
    section, chip, core = place()
    y, z = chip // 4, chip % 4
    ahead, behind, far = (section + 1) % 4, (section + 3) % 4, (section + 2) % 4
    ahead_dev, behind_dev = dev(chip, core, ahead), dev(chip, core, behind)
    copies = Copies(send, recv)
    mate = dev(chip, 1 - core, section)
    peers = plane_peers(section, chip, core) + section_peers(section, chip, core)
    greet(peers)
    early = [
        copies.start(source, target, None)
        for source, target in (
            (spans_hbm, spans_ref), (kv_hbm.at[:, :, 1024:2048], kv_ref), (q_hbm, q_ref),
            (qrow_hbm, qrow), (grow_hbm, grow), (gnat_hbm, gnat), (dq_hbm, dq_acc),
        )
    ]
    greeted(peers)
    back, mates = [], []
    for half in range(2):
        waits = []
        for step, base, slot in ((-1, 0, 0), (1, 1024, 1)):
            for target in (core, 1 - core):
                lanes = pl.ds(pl.multiple_of(base + target * 512 + half * 256, 256), 256)
                device = dev(around(chip, step), target, section)
                waits.append(
                    copies.start(dkv_ref.at[:, :, lanes], dkv_in.at[half, slot, core], device)
                )
        back.append(waits)

    def glt_part(owner, start, count):
        lanes = pl.ds(pl.multiple_of(owner * 128, 128), 128)
        return glt.at[start : start + count, lanes]

    mine = glt_part(section, 0, 1280)
    glt_ahead = copies.start(glt_hbm, mine, ahead_dev)
    glt_behind = copies.start(glt_hbm, mine, behind_dev)
    gathered = [copies.start(glt_hbm, mine, None)]
    load_table = [
        copies.start(table_hbm, table_ref, None), copies.start(starts_hbm, starts_ref, None)
    ]
    load_w = copies.start(w_hbm, w_ref, None)
    loads = [
        copies.start(source, target, None)
        for source, target in (
            (normed_t_hbm, normed_t_ref), (tokens_hbm, tokens_ref), (gl_hbm, gl_ref),
            (gain_hbm, gain_ref), (live_hbm, live_ref),
        )
    ]
    for near, of_core in ((True, core), (False, 1 - core)):
        rows = pl.ds(pl.multiple_of(of_core * PAIR, 16), PAIR)
        for part in range(4):
            source = op_hbm.at[core, part] if near else own_hbm.at[part]
            loads.append(copies.start(source, att.at[rows, part * 128 : part * 128 + 128], None))

    wait_all(early)
    for chunk in range(4):
        lanes = pl.ds(chunk * CHUNK, CHUNK)
        build_keys(
            spans_ref, chip * 1024 + chunk * CHUNK, kv_ref, lanes, kx, vx, krow, lanes
        )
    dk_acc[...] = jnp.zeros_like(dk_acc)
    dv_acc[...] = jnp.zeros_like(dv_acc)

    def own_step(tile, group):
        rows = pl.ds(pl.multiple_of(tile * 256, 256), 256)
        chunks = [pl.ds((group + 2 * which) * CHUNK, CHUNK) for which in range(2)]
        sums = backward_step(
            rows, chunks, q_ref, gnat, qrow, grow, kx, vx, krow, dk_acc, dv_acc,
            (dq_acc[0, rows, :], dq_acc[1, rows, :]),
        )
        for head in range(2):
            dq_acc[head, rows, :] = sums[head]

    def finish_own(half):
        for of_core in range(2):
            lanes = pl.ds(of_core * 512 + half * 256, 256)
            for head in range(2):
                feats = pl.ds(head * HEAD_DIM, HEAD_DIM)
                part = dq_acc[head, lanes, :].T[:80] * FACTOR
                own_out[half, of_core, 0, feats, :] = part.astype(BF16)
                own_out[half, of_core, 1, feats, :] = (dk_acc[head, :, lanes] * FACTOR).astype(BF16)
                own_out[half, of_core, 2, feats, :] = dv_acc[head, :, lanes].astype(BF16)
        mates.append(copies.start(own_out.at[half, 1 - core], mate_in.at[half], mate))

    def first_step(tile, carry):
        own_step(tile, 0)
        return carry

    def even_step(index, carry):
        own_step(index * 2, 1)
        return carry

    def odd_step(index, carry):
        own_step(index * 2 + 1, 1)
        return carry

    lax.fori_loop(0, 4, first_step, 0)
    lax.fori_loop(0, 2, even_step, 0)
    finish_own(0)
    glt_ahead.wait()
    there = glt_part(behind, 0, 640)
    gathered.append(copies.start(there, there, ahead_dev))
    glt_behind.wait()
    there = glt_part(ahead, 640, 640)
    gathered.append(copies.start(there, there, behind_dev))
    lax.fori_loop(0, 2, odd_step, 0)
    finish_own(1)

    row = lax.broadcasted_iota(jnp.int32, (256, 256), 0)
    column = lax.broadcasted_iota(jnp.int32, (256, 256), 1)
    by_part = jnp.where(column == 4 * (row % 64) + row // 64, 1.0, 0.0).astype(BF16)
    load_w.wait()

    def collect(half, kinds):
        lanes = pl.ds(half * 256, 256)
        for near, head in ((True, core), (False, 1 - core)):
            for which in kinds:
                grad = own_out[half, core, which] if near else mate_in[half, which]
                if which:
                    grad = grad.astype(F32) + dkv_in[half, 0, head, which - 1].astype(F32)
                    grad = (grad + dkv_in[half, 1, head, which - 1].astype(F32)).astype(BF16)
                dj[pl.ds(pl.multiple_of(320 * which + head * PAIR, 16), PAIR), lanes] = grad

    sums = []

    def send_first(half):
        rows_ref[...] = dot_nt(by_part, dj[:, half * 256 : half * 256 + 256]).astype(BF16)
        grad = dot_nn(rows_ref[...], w_ref[...].reshape(960, 1280))
        gn[half] = grad.astype(BF16).reshape(4, 64, 1280)
        relays = [
            copies.start(gn.at[half, far, 0:32], relay_in.at[half, 0], behind_dev),
            copies.start(gn.at[half, far, 32:64], relay_in.at[half, 1], ahead_dev),
        ]
        sums.append([
            copies.start(gn.at[half, behind, 32:64], gn_in.at[half, 0, 32:64], behind_dev),
            copies.start(gn.at[half, ahead, 0:32], gn_in.at[half, 1, 0:32], ahead_dev),
        ])
        return relays

    def send_second(half, relays):
        relays[0].wait()
        grad = gn[half, behind, 0:32].astype(F32) + relay_in[half, 0].astype(F32)
        gn[half, behind, 0:32] = grad.astype(BF16)
        source = gn.at[half, behind, 0:32]
        sums[half].append(copies.start(source, gn_in.at[half, 0, 0:32], behind_dev))
        relays[1].wait()
        grad = gn[half, ahead, 32:64].astype(F32) + relay_in[half, 1].astype(F32)
        gn[half, ahead, 32:64] = grad.astype(BF16)
        source = gn.at[half, ahead, 32:64]
        sums[half].append(copies.start(source, gn_in.at[half, 1, 32:64], ahead_dev))

    def products(index, core_of, group):
        rows = pl.ds(index * 320, 320)
        if group == 0 and core_of == 1:
            return dot_nt(glt[rows, :], att[...])
        which = 0 if group == 0 else 1 + core_of
        return dot_nt(normed_t_ref[rows, :], dj[320 * which : 320 * which + 320, :])

    def send_products(group):
        pairs = []
        for index in range(4):
            for core_of in range(2):
                @pl.when(core != core_of)
                def _():
                    part = products(index, core_of, group)
                    p_away[group, index] = part.astype(BF16).reshape(4, 80, 320)

            pairs.append(copies.start(p_away.at[group, index], p_in.at[group, index], mate))
        for index in range(4):
            for core_of in range(2):
                @pl.when(core == core_of)
                def _():
                    p_mine[index] = products(index, core_of, group).reshape(4, 80, 320)

        return pairs

    def first_stage(group, pairs):
        for index in range(4):
            pairs[index].wait()
            grad = p_mine[index] + p_in[group, index].astype(F32)
            summed[group, index] = grad.astype(BF16)
        waits = []
        for step in (2, 1, 3):
            to_z, to_y = (z + step) % 4, (y + step) % 4
            if group == 0:
                source, device = summed.at[group, to_y], dev(to_y * 4 + z, core, section)
            else:
                source, device = summed.at[group, :, to_z], dev(y * 4 + to_z, core, section)
            waits.append(copies.start(source, stage_in.at[group, step - 1], device))
        return waits

    def second_stage(group, waits):
        wait_all(waits)
        for index in range(4):
            grad = (summed[group, y, index] if group == 0 else summed[group, index, z]).astype(F32)
            for step in range(3):
                grad = grad + stage_in[group, step, index].astype(F32)
            subtotal[group, index] = grad.astype(BF16)
        waits = []
        for step in (2, 1, 3):
            to_z, to_y = (z + step) % 4, (y + step) % 4
            place_to = to_z if group == 0 else to_y
            device = dev(y * 4 + to_z if group == 0 else to_y * 4 + z, core, section)
            waits.append(
                copies.start(subtotal.at[group, place_to], late_in.at[group, step - 1], device)
            )
        return waits

    def last_stage(group, waits):
        wait_all(waits)
        grad = subtotal[group, z if group == 0 else y].astype(F32)
        for step in range(3):
            grad = grad + late_in[group, step].astype(F32)
        total[group] = grad
        found = []
        for target, device in ((1 - core, mate), (core, None)):
            rows = pl.ds(pl.multiple_of(target * 40, 8), 40)
            found.append(
                copies.start(total.at[group, rows, :], weights_ref.at[core, group], device)
            )
        return found

    gathers, forwards = [], []

    def finish_norm(half):
        row = lax.broadcasted_iota(jnp.int32, (64, 256), 0)
        column = lax.broadcasted_iota(jnp.int32, (64, 256), 1)
        chosen = jnp.where(column == 4 * row + section, 1.0, 0.0).astype(BF16)
        values = dot_nn(chosen, tokens_ref[half * 256 : half * 256 + 256, :])
        centered = values - jnp.mean(values, axis=1, keepdims=True)
        inv = lax.rsqrt(jnp.mean(centered * centered, axis=1, keepdims=True) + EPS)
        unit = centered * inv
        wait_all(sums[half])
        grad = gn[half, section].astype(F32) + gn_in[half, 0].astype(F32)
        grad = grad + gn_in[half, 1].astype(F32)
        scaled = grad * gain_ref[...].reshape(1, 1280).astype(F32)
        grad = inv * (
            scaled
            - jnp.mean(scaled, axis=1, keepdims=True)
            - unit * jnp.mean(scaled * unit, axis=1, keepdims=True)
        )
        grad = grad + gl_ref[half * 64 : half * 64 + 64, :].astype(F32)
        gx_own[half] = grad.astype(BF16)
        target = gx_all.at[half, section]
        gathers.append([copies.start(gx_own.at[half], target, ahead_dev)])
        gathers[half].append(copies.start(gx_own.at[half], target, behind_dev))
        forwards.append(copies.start(gx_own.at[half], target, None))

    def forward(half):
        gathers[half][0].wait()
        there = gx_all.at[half, behind, 0:32]
        forwards.append(copies.start(there, there, ahead_dev))
        gathers[half][1].wait()
        there = gx_all.at[half, ahead, 32:64]
        forwards.append(copies.start(there, there, behind_dev))

    wait_all(back[0])
    mates[0].wait()
    collect(0, (0, 1, 2))
    relays_a = send_first(0)

    wait_all(load_table)
    begin = starts_ref[:, 0:1]
    block, offset = begin // 128, begin % 128
    first = 8 * ((block + 1 - core) // 2)
    first = first + jnp.where(block % 2 == core, (offset - chip + 15) // 16, 0)
    out_row = lax.broadcasted_iota(jnp.int32, (512, 256), 0)
    in_row = lax.broadcasted_iota(jnp.int32, (512, 256), 1)
    wanted = first + out_row % 8
    wanted = (wanted // 8) * 16 + wanted % 8 + 8 * ((out_row // 8) % 2)
    hot = jnp.where(in_row == wanted, 1.0, 0.0).astype(BF16)
    table = table_ref[...].reshape(256, 640)
    parcels[...] = dot_nn(hot, table).astype(BF16).reshape(32, 16, 640)

    wait_all(loads)
    wait_all(gathered)
    mates[1].wait()
    collect(1, (0,))
    pairs = send_products(0)
    wait_all(back[1])
    collect(1, (1, 2))
    relays_b = send_first(1)
    deliveries = []
    for step in range(16):
        for turn in range(2):
            to_chip, to_core = (chip + step) % 16, (core + turn) % 2
            device = dev(to_chip, to_core, section) if step or turn else None
            deliveries.append(
                copies.start(parcels.at[to_chip * 2 + to_core], arrived.at[chip * 2 + core], device)
            )
    send_second(0, relays_a)
    stage_y = first_stage(0, pairs)
    pairs = send_products(1)
    stage_z = first_stage(1, pairs)
    send_second(1, relays_b)
    finish_norm(0)
    finish_norm(1)
    forward(0)
    later_z = second_stage(0, stage_y)
    forward(1)

    lane = lax.broadcasted_iota(jnp.int32, (1, 512), 1)
    from_chip, from_core, side, number = lane // 32, (lane // 16) % 2, (lane // 8) % 2, lane % 8
    begin, live = live_ref[0:1, :], live_ref[8:9, :]
    block, offset = begin // 128, begin % 128
    spot = 8 * ((block + 1 - from_core) // 2) + number
    spot = spot + jnp.where(block % 2 == from_core, (offset - from_chip + 15) // 16, 0)
    slot = (2 * (spot // 8) + from_core) * 128 + 16 * (spot % 8) + from_chip - begin
    out_row = lax.broadcasted_iota(jnp.int32, (256, 512), 0)
    taken = (out_row == slot) & (out_row < live)
    wait_all(deliveries)
    rows = arrived[...].reshape(512, 640)
    for which in range(2):
        hot = jnp.where(taken & (side == which), 1.0, 0.0).astype(BF16)
        delivered_ref[:, which * 640 : which * 640 + 640] = dot_nn(hot, rows).astype(BF16)
    lasts = [copies.start(delivered_ref, delivered_hbm, None)]

    later_y = second_stage(1, stage_z)
    lasts += last_stage(0, later_z)
    lasts += last_stage(1, later_y)
    wait_all(lasts)
    wait_all(forwards)


def results_body(
    gx_hbm, both_hbm, arrived_hbm, gx_out, w_qkv_out, w_out_out, delivered_out,
    gx_in, gx_ref, both_ref, delivered_ref, sems,
):
    loads = [
        pltpu.make_async_copy(source, target, sems.at[index])
        for index, (source, target) in enumerate(
            (
                (gx_hbm.at[0], gx_in.at[0]), (gx_hbm.at[1], gx_in.at[1]),
                (both_hbm, both_ref), (arrived_hbm, delivered_ref),
            )
        )
    ]
    for load in loads:
        load.start()
    row = lax.broadcasted_iota(jnp.int32, (256, 256), 0)
    column = lax.broadcasted_iota(jnp.int32, (256, 256), 1)
    natural = jnp.where(row == 4 * (column % 64) + column // 64, 1.0, 0.0).astype(BF16)
    stores = []

    def store(source, target):
        stores.append(pltpu.make_async_copy(source, target, sems.at[4 + len(stores)]))
        stores[-1].start()

    for half in range(2):
        loads[half].wait()
        rows = gx_in[half].reshape(256, 1280)
        gx_ref[half] = dot_nn(natural, rows).astype(BF16)
        store(gx_ref.at[half], gx_out.at[half * 256 : half * 256 + 256, :])
    loads[2].wait()
    store(both_ref.at[0], w_qkv_out.at[0:2])
    store(both_ref.at[1, 1], w_qkv_out.at[2])
    store(both_ref.at[1, 0], w_out_out)
    loads[3].wait()
    store(delivered_ref, delivered_out)
    for copy in stores:
        copy.wait()


def halo_peers(section, chip, core):
    found = [dev(chip, 1 - core, section)]
    for step in (1, -1):
        for other in (core, 1 - core):
            found.append(dev(around(chip, step), other, section))
    return found


def row_peers(section, chip, core):
    found = []
    for step in range(4):
        for turn in range(2):
            if step or turn:
                found.append(dev(chip, (core + turn) % 2, (section + step) % 4))
    return found


def section_peers(section, chip, core):
    return [dev(chip, core, (section + step) % 4) for step in range(1, 4)]


def core_peers(section, chip, core):
    return [dev((chip + step) % 16, core, section) for step in range(1, 16)]


def plane_peers(section, chip, core):
    found = [dev(chip, 1 - core, section)]
    for step in range(1, 16):
        for turn in range(2):
            found.append(dev((chip + step) % 16, (core + turn) % 2, section))
    return found


def local(
    tokens, norm_gain, w_qkv, w_out, merge_gain, seg_blocks, mb_sizes, mb_receiver, merged_grad
):
    w_rows = w_qkv.transpose(0, 2, 1)
    q, kv, normed_t, w_full, q_rows, sums, norms = call(
        project_body,
        [
            (HBM, shape((PAIR, 1024))),
            (HBM, shape((2, PAIR, 3072))),
            (HBM, shape((1280, 512))),
            (HBM, shape((1280, 1280))),
            (HBM, shape((2, 1024, 128))),
            (HBM, shape((2, 1024, 128), F32)),
            (HBM, shape((4, 8, 128), F32)),
        ],
        [(SMEM, seg_blocks), (HBM, tokens), (HBM, norm_gain), (HBM, w_rows), (HBM, w_out)],
        [
            pltpu.VMEM((512, 1280), BF16),
            pltpu.VMEM((1280,), BF16),
            pltpu.VMEM((3, 320, 1280), BF16),
            pltpu.VMEM((1280, 512), BF16),
            pltpu.VMEM((3, 320, 512), BF16),
            pltpu.VMEM((PAIR, 1024), BF16),
            pltpu.VMEM((2, PAIR, 1024), BF16),
            pltpu.VMEM((2, 32, 128), jnp.int32),
            pltpu.VMEM((2, 1024, 128), BF16),
            pltpu.VMEM((2, 128, 1024), BF16),
            pltpu.VMEM((2, 1024, 128), BF16),
            pltpu.VMEM((2, 1024, 128), F32),
            pltpu.VMEM((4, 8, 128), F32),
        ],
        copies=40,
        number=1,
        limit=62,
    )
    o, op, log_total = call(
        forward_body,
        [
            (HBM, shape((PAIR, 1024))),
            (HBM, shape((2, 4, PAIR, 128))),
            (HBM, shape((2, 1024), F32)),
        ],
        [(SMEM, seg_blocks), (HBM, kv), (HBM, q_rows), (HBM, sums), (HBM, norms)],
        [
            pltpu.VMEM((2, 32, 128), jnp.int32),
            pltpu.SMEM((4, 2), jnp.int32),
            pltpu.VMEM((PAIR, 1024), BF16),
            pltpu.VMEM((2, PAIR, 3072), BF16),
            pltpu.VMEM((2, 1024, 128), BF16),
            pltpu.VMEM((2, 128, 3072), BF16),
            pltpu.VMEM((2, 3072, 128), BF16),
            pltpu.VMEM((2, 1024, 128), F32),
            pltpu.VMEM((4, 8, 128), F32),
            pltpu.VMEM((2, 4, PAIR, 128), BF16),
            pltpu.VMEM((2, 1024), F32),
        ],
        copies=9,
        limit=62,
    )
    gp, grad_layer, glt, att_own, table = call(
        middle_body,
        [
            (HBM, shape((2, 4, PAIR, 128))),
            (HBM, shape((128, 1280))),
            (HBM, shape((1280, 128))),
            (HBM, shape((4, PAIR, 128))),
            (HBM, shape((16, 16, 640))),
        ],
        [(HBM, op), (HBM, w_full), (HBM, w_out), (HBM, tokens), (HBM, merged_grad), (HBM, merge_gain)],
        [
            pltpu.VMEM((1280, 1280), BF16),
            pltpu.VMEM((512, 1280), BF16),
            pltpu.VMEM((128, 1280), BF16),
            pltpu.VMEM((1280,), BF16),
            pltpu.VMEM((128, 1280), BF16),
            pltpu.VMEM((1280, 128), BF16),
            pltpu.VMEM((1280, 128), BF16),
            pltpu.VMEM((1280, 128), BF16),
            pltpu.VMEM((16, 16, 640), BF16),
        ],
        copies=44,
        number=2,
        limit=62,
    )
    dq, dkv, start_rows, here, qrow, grow, gnat, spans = call(
        backward_body,
        [
            (HBM, shape((2, 1024, 128), F32)),
            (HBM, shape((2, PAIR, 2048))),
            (HBM, shape((512, 128), jnp.int32)),
            (HBM, shape((16, 512), jnp.int32)),
            (HBM, shape((2, 1024, 128))),
            (HBM, shape((2, 1024, 128))),
            (HBM, shape((PAIR, 1024))),
            (HBM, shape((2, 32, 128), jnp.int32)),
        ],
        [
            (SMEM, seg_blocks), (SMEM, mb_sizes), (SMEM, mb_receiver),
            (HBM, q), (HBM, kv), (HBM, o), (HBM, log_total), (HBM, gp),
        ],
        [
            pltpu.VMEM((2, 1024, 128), F32),
            pltpu.VMEM((2, PAIR, 2048), BF16),
            pltpu.VMEM((512, 128), jnp.int32),
            pltpu.VMEM((16, 512), jnp.int32),
            pltpu.VMEM((2, 1024, 128), BF16),
            pltpu.VMEM((2, 1024, 128), BF16),
            pltpu.VMEM((PAIR, 1024), BF16),
            pltpu.VMEM((2, 32, 128), jnp.int32),
            pltpu.SMEM((4, 2), jnp.int32),
            pltpu.VMEM((PAIR, 1024), BF16),
            pltpu.VMEM((2, PAIR, 3072), BF16),
            pltpu.VMEM((PAIR, 1024), BF16),
            pltpu.VMEM((2, 1024), F32),
            pltpu.VMEM((2, 4, PAIR, 128), BF16),
            pltpu.VMEM((2, 128, 2048), BF16),
            pltpu.VMEM((2, 128, 2048), BF16),
            pltpu.VMEM((2, 2048, 128), BF16),
            pltpu.VMEM((2, HEAD_DIM, 2048), F32),
            pltpu.VMEM((2, HEAD_DIM, 2048), F32),
        ],
        copies=14,
        limit=62,
    )
    arrived, gx_all, weights = call(
        tail_body,
        [
            (HBM, shape((256, 1280))),
            (HBM, shape((2, 4, 64, 1280))),
            (HBM, shape((2, 2, 40, 320), F32)),
        ],
        [
            (HBM, dkv), (HBM, start_rows), (HBM, here), (HBM, dq), (HBM, qrow), (HBM, grow),
            (HBM, gnat), (HBM, spans), (HBM, q), (HBM, kv), (HBM, glt), (HBM, op), (HBM, att_own),
            (HBM, table), (HBM, grad_layer), (HBM, tokens), (HBM, norm_gain), (HBM, w_rows),
            (HBM, normed_t),
        ],
        [
            pltpu.VMEM((512, 128), jnp.int32),
            pltpu.VMEM((16, 512), jnp.int32),
            pltpu.VMEM((2, 1024, 128), BF16),
            pltpu.VMEM((2, 1024, 128), BF16),
            pltpu.VMEM((PAIR, 1024), BF16),
            pltpu.VMEM((2, 32, 128), jnp.int32),
            pltpu.VMEM((1280,), BF16),
            pltpu.VMEM((256, 1280), BF16),
            pltpu.VMEM((16, 16, 640), BF16),
            pltpu.VMEM((128, 1280), BF16),
            pltpu.VMEM((512, 1280), BF16),
            pltpu.VMEM((3, 320, 1280), BF16),
            pltpu.VMEM((1280, 512), BF16),
            pltpu.VMEM((PAIR, 1024), BF16),
            pltpu.VMEM((2, PAIR, 1024), BF16),
            pltpu.VMEM((2, 128, 1024), BF16),
            pltpu.VMEM((2, 128, 1024), BF16),
            pltpu.VMEM((2, 1024, 128), BF16),
            pltpu.VMEM((2, HEAD_DIM, 1024), F32),
            pltpu.VMEM((2, HEAD_DIM, 1024), F32),
            pltpu.VMEM((2, 1024, 128), F32),
            pltpu.VMEM((2, 2, 3, PAIR, 256), BF16),
            pltpu.VMEM((2, 3, PAIR, 256), BF16),
            pltpu.VMEM((2, 2, 2, 2, PAIR, 256), BF16),
            pltpu.VMEM((960, 512), BF16),
            pltpu.VMEM((256, 960), BF16),
            pltpu.VMEM((2, 4, 64, 1280), BF16),
            pltpu.VMEM((2, 2, 32, 1280), BF16),
            pltpu.VMEM((2, 2, 64, 1280), BF16),
            pltpu.VMEM((2, 64, 1280), BF16),
            pltpu.VMEM((320, 512), BF16),
            pltpu.VMEM((1280, 512), BF16),
            pltpu.VMEM((32, 16, 640), BF16),
            pltpu.VMEM((32, 16, 640), BF16),
            pltpu.VMEM((4, 4, 80, 320), F32),
            pltpu.VMEM((2, 4, 4, 80, 320), BF16),
            pltpu.VMEM((2, 4, 4, 80, 320), BF16),
            pltpu.VMEM((2, 4, 4, 80, 320), BF16),
            pltpu.VMEM((2, 3, 4, 80, 320), BF16),
            pltpu.VMEM((2, 4, 80, 320), BF16),
            pltpu.VMEM((2, 3, 80, 320), BF16),
            pltpu.VMEM((2, 80, 320), F32),
        ],
        copies=124,
        number=3,
        limit=62,
    )
    grad_x, grad_w_qkv, grad_w_out, delivered = call(
        results_body,
        [
            (HBM, shape((512, 1280))),
            (HBM, shape((3, 40, 320), F32)),
            (HBM, shape((40, 320), F32)),
            (HBM, shape((256, 1280))),
        ],
        [(HBM, gx_all), (HBM, weights), (HBM, arrived)],
        [
            pltpu.VMEM((2, 4, 64, 1280), BF16),
            pltpu.VMEM((2, 256, 1280), BF16),
            pltpu.VMEM((2, 2, 40, 320), F32),
            pltpu.VMEM((256, 1280), BF16),
        ],
        copies=10,
        limit=62,
    )
    return (delivered, grad_x, grad_w_qkv, grad_w_out.T)


def solution(mesh):
    placed = (
        P("seq", None),
        P(),
        P(None, None, "section"),
        P("section", None),
        P(),
        P(),
        P(),
        P(),
        P("seq", None),
    )
    return jax.shard_map(
        local,
        mesh=mesh,
        in_specs=placed,
        out_specs=(
            P("seq", "section"),
            P("seq", None),
            P(None, "seq", "section"),
            P("section", "seq"),
        ),
        check_vma=False,
    )
```

```python
import math

import jax
import jax.numpy as jnp
from jax import lax
from jax.experimental import pallas as pl
from jax.experimental.pallas import tpu as pltpu
from jax.sharding import PartitionSpec as P

HEADS = 16
EPS = 1e-06
HEAD_DIM = 80
PAIR = 160
BIG = -1e30
CHUNK = 256
SAFE = 60.0
BF16 = jnp.bfloat16
F32 = jnp.float32
MESH = pl.DeviceIdType.MESH
FACTOR = HEAD_DIM ** -0.5
LOG2E = 1.0 / math.log(2.0)
LN2 = math.log(2.0)


def dot_nn(left, right):
    return lax.dot_general(left, right, (((1,), (0,)), ((), ())), preferred_element_type=F32)


def dot_nt(left, right):
    return lax.dot_general(left, right, (((1,), (1,)), ((), ())), preferred_element_type=F32)


def place():
    section = lax.axis_index("section")
    seq = lax.axis_index("seq")
    return section, seq // 2, seq % 2


def shape(dims, dtype=BF16):
    return jax.ShapeDtypeStruct(dims, dtype)


class Copies:
    def __init__(self, send_sems, recv_sems):
        self.send_sems, self.recv_sems, self.used = send_sems, recv_sems, 0

    def start(self, source, target, device):
        index = self.used
        self.used = index + 1
        if device is None:
            copy = pltpu.make_async_copy(source, target, self.recv_sems.at[index])
        else:
            copy = pltpu.make_async_remote_copy(
                src_ref=source,
                dst_ref=target,
                send_sem=self.send_sems.at[index],
                recv_sem=self.recv_sems.at[index],
                device_id=device,
                device_id_type=MESH,
            )
        copy.start()
        return copy


def wait_all(copies):
    for copy in copies:
        copy.wait()


def greet(peers):
    barrier = pltpu.get_barrier_semaphore()
    for peer in peers:
        pl.semaphore_signal(barrier, inc=1, device_id=peer, device_id_type=MESH)


def greeted(peers):
    pl.semaphore_wait(pltpu.get_barrier_semaphore(), len(peers))


VMEM = pl.BlockSpec(memory_space=pltpu.VMEM)
SMEM = pl.BlockSpec(memory_space=pltpu.SMEM)
HBM = pl.BlockSpec(memory_space=pltpu.HBM)


def call(body, outs, ins, scratch=(), copies=0, number=None, limit=14):
    more = {} if number is None else {"collective_id": number, "has_side_effects": True}
    semaphores = [pltpu.SemaphoreType.DMA((copies,))] * (0 if not copies else 1 if number is None else 2)
    return pl.pallas_call(
        body,
        out_shape=[array for _, array in outs],
        in_specs=[place for place, _ in ins],
        out_specs=[place for place, _ in outs],
        scratch_shapes=list(scratch) + semaphores,
        compiler_params=pltpu.CompilerParams(vmem_limit_bytes=limit << 20, **more),
    )(*[array for _, array in ins])


def dev(chip, core, section):
    return (chip * 2 + core, section)


def around(chip, step):
    return (chip + step + 16) % 16


def project_body(
    seg_ref, tokens_hbm, gain_hbm, w_hbm, w_out_hbm,
    q_hbm, kv_hbm, normed_t_hbm, w_full, qrow_hbm, sums_hbm, norms_hbm,
    tokens_ref, gain_ref, w_ref, normed_t_ref, out_ref,
    q_ref, kv_ref, spans_ref, qrow, kx, vrow, sums_ref, norms_ref, send, recv,
):
    section, chip, core = place()
    copies = Copies(send, recv)
    peers = halo_peers(section, chip, core) + section_peers(section, chip, core)[::2]
    greet(peers)
    load_gain = copies.start(gain_hbm, gain_ref, None)
    load_tokens = []
    for tile in range(4):
        rows = pl.ds(tile * 128, 128)
        load_tokens.append(copies.start(tokens_hbm.at[rows, :], tokens_ref.at[rows, :], None))
    load_w = {which: copies.start(w_hbm.at[which], w_ref.at[which], None) for which in (1, 2, 0)}
    greeted(peers)
    mate = dev(chip, 1 - core, section)
    ahead, behind = (section + 1) % 4, (section + 3) % 4
    ahead_dev, behind_dev = dev(chip, core, ahead), dev(chip, core, behind)

    def w_rows(owner, start, count):
        return w_full.at[pl.ds(pl.multiple_of(owner * 320 + core * PAIR + start, 16), count), :]

    def mine(start):
        return w_out_hbm.at[pl.ds(pl.multiple_of(core * PAIR + start, 16), 80), :]

    to_ahead = copies.start(mine(0), w_rows(section, 0, 80), ahead_dev)
    to_behind = copies.start(mine(80), w_rows(section, 80, 80), behind_dev)
    rest_ahead = copies.start(mine(80), w_rows(section, 80, 80), ahead_dev)
    rest_behind = copies.start(mine(0), w_rows(section, 0, 80), behind_dev)
    waits, inner = [], []
    load_gain.wait()
    gain = gain_ref[...].reshape(1, 1280).astype(F32)
    for tile in range(4):
        rows = pl.ds(tile * 128, 128)
        load_tokens[tile].wait()
        values = tokens_ref[rows, :].astype(F32)
        centered = values - jnp.mean(values, axis=1, keepdims=True)
        inv = lax.rsqrt(jnp.mean(centered * centered, axis=1, keepdims=True) + EPS)
        normed_t_ref[:, rows] = (centered * inv * gain).astype(BF16).T
    own = pl.ds(pl.multiple_of(core * PAIR, 16), PAIR)
    other = pl.ds(pl.multiple_of((1 - core) * PAIR, 16), PAIR)
    for which in (1, 2, 0):
        load_w[which].wait()
        out = dot_nn(w_ref[which], normed_t_ref[...])
        if which == 0:
            out = out * (FACTOR * LOG2E)
        out_ref[which] = out.astype(BF16)
        mine = pl.ds(pl.multiple_of(core * 512, 512), 512)
        target = q_ref.at[:, mine]
        if which:
            for step, base in ((1, 0), (-1, 2048)):
                lanes = pl.ds(pl.multiple_of(base + core * 512, 512), 512)
                for rows, to_core in ((own, core), (other, 1 - core)):
                    device = dev(around(chip, step), to_core, section)
                    waits.append(
                        copies.start(out_ref.at[which, rows, :], kv_hbm.at[which - 1, :, lanes], device)
                    )
            target = kv_ref.at[which - 1, :, mine]
        inner.append(copies.start(out_ref.at[which, other, :], target, mate))
        inner.append(copies.start(out_ref.at[which, own, :], target, None))
    waits.append(copies.start(normed_t_ref, normed_t_hbm, None))
    image_spans(seg_ref, spans_ref)
    wait_all(inner)
    waits.append(copies.start(q_ref, q_hbm, None))
    waits.append(copies.start(kv_ref, kv_hbm.at[:, :, 1024:2048], None))
    first = chip * 1024
    for block in range(4):
        lanes = pl.ds(block * 256, 256)
        build_queries(spans_ref, first + block * 256, q_ref, lanes, qrow)
        build_values(spans_ref, first + block * 256, kv_ref, lanes, kx, vrow, lanes)
    for head in range(2):
        feats = pl.ds(head * HEAD_DIM, HEAD_DIM)
        for which, values in enumerate((q_ref[feats, :], kv_ref[0, feats, :])):
            norms_ref[which * 2 + head, :, :] = squares(values)

    def tile_step(tile, carry):
        rows = pl.ds(pl.multiple_of(tile * 256, 256), 256)
        sums = (jnp.zeros((256, 128), F32),) * 2
        for chunk in range(0, 4, 2):
            lanes = [pl.ds((chunk + which) * CHUNK, CHUNK) for which in range(2)]
            sums = forward_step(rows, lanes, qrow, kx, vrow, sums)
        for head in range(2):
            sums_ref[head, rows, :] = sums[head]
        return carry

    lax.fori_loop(0, 2, tile_step, 0)
    to_ahead.wait()
    relay = [copies.start(w_rows(behind, 0, 80), w_rows(behind, 0, 80), ahead_dev)]
    to_behind.wait()
    relay.append(copies.start(w_rows(ahead, 80, 80), w_rows(ahead, 80, 80), behind_dev))
    lax.fori_loop(2, 4, tile_step, 0)
    waits.append(copies.start(qrow, qrow_hbm, None))
    waits.append(copies.start(sums_ref, sums_hbm, None))
    waits.append(copies.start(norms_ref, norms_hbm, None))
    rest_ahead.wait()
    waits.append(copies.start(w_rows(behind, 0, PAIR), w_rows(behind, 0, PAIR), mate))
    rest_behind.wait()
    waits.append(copies.start(w_rows(ahead, 0, PAIR), w_rows(ahead, 0, PAIR), mate))
    far = (section + 2) % 4
    for copy, start in zip(relay, (0, 80)):
        copy.wait()
        waits.append(copies.start(w_rows(far, start, 80), w_rows(far, start, 80), mate))
    wait_all(waits)


def image_spans(seg_ref, spans_ref):
    row = lax.broadcasted_iota(jnp.int32, (32, 128), 0)
    begins, ends = jnp.zeros((32, 128), jnp.int32), jnp.zeros((32, 128), jnp.int32)
    end = jnp.int32(0)
    for image in range(32):
        begin = end
        end = begin + 64 * seg_ref[image]
        begins = jnp.where(row == image, begin, begins)
        ends = jnp.where(row == image, end, ends)
    spans_ref[0] = begins
    spans_ref[1] = ends


def squares(values):
    values = values.astype(F32)
    total = jnp.sum(values * values, axis=0, keepdims=True)
    blocks = [total[:, start : start + 128] for start in range(0, total.shape[1], 128)]
    top = blocks[0]
    for block in blocks[1:]:
        top = jnp.maximum(top, block)
    return jnp.broadcast_to(top, (8, 128))


def build_queries(spans_ref, position, q_ref, lanes, qrow):
    inside = membership(spans_ref, position, 256)
    for head in range(2):
        joined = jnp.concatenate(
            [
                q_ref[pl.ds(head * HEAD_DIM, HEAD_DIM), lanes],
                jnp.where(inside, 0.0, BIG).astype(BF16),
                jnp.zeros((16, 256), BF16),
            ],
            axis=0,
        )
        qrow[head, lanes, :] = joined.T


def build_values(spans_ref, position, kv_ref, lanes, kx, vrow, into):
    ones = jnp.where(lax.broadcasted_iota(jnp.int32, (16, CHUNK), 0) < 3, 1.0, 0.0).astype(BF16)
    hot = jnp.where(membership(spans_ref, position, CHUNK), 1.0, 0.0).astype(BF16)
    for head in range(2):
        feats = pl.ds(head * HEAD_DIM, HEAD_DIM)
        kx[head, :, into] = jnp.concatenate([kv_ref[0, feats, lanes], hot, ones], axis=0)
        joined = jnp.concatenate(
            [kv_ref[1, feats, lanes], ones, jnp.zeros((32, CHUNK), BF16)], axis=0
        )
        vrow[head, into, :] = joined.T


def forward_step(rows, chunks, qrow, kx, vrow, sums):
    pairs = [(head, lanes) for lanes in chunks for head in range(2)]
    probs = [
        jnp.exp2(dot_nn(qrow[head, rows, :], kx[head, :, lanes])).astype(BF16)
        for head, lanes in pairs
    ]
    sums = list(sums)
    for (head, lanes), part in zip(pairs, probs):
        sums[head] = sums[head] + dot_nn(part, vrow[head, lanes, :])
    return tuple(sums)


def spans_and_bounds(seg_ref, first, spans_ref, bounds_ref):
    row = lax.broadcasted_iota(jnp.int32, (32, 128), 0)
    begins, ends = jnp.zeros((32, 128), jnp.int32), jnp.zeros((32, 128), jnp.int32)
    end = jnp.int32(0)
    low = [jnp.int32(0)] * 4
    high = [jnp.int32(16384)] * 4
    for image in range(32):
        begin = end
        end = begin + 64 * seg_ref[image]
        begins = jnp.where(row == image, begin, begins)
        ends = jnp.where(row == image, end, ends)
        for tile in range(4):
            start = first + 256 * tile
            low[tile] = jnp.where(begin <= start, begin, low[tile])
            high[tile] = jnp.where((begin < start + 256) & (end >= start + 256), end, high[tile])
    spans_ref[0] = begins
    spans_ref[1] = ends
    for tile in range(4):
        bounds_ref[tile, 0] = (low[tile] - (first - 1024)) // CHUNK
        bounds_ref[tile, 1] = (high[tile] - (first - 1024) + CHUNK - 1) // CHUNK


def membership(spans_ref, first, count):
    spots = first + lax.broadcasted_iota(jnp.int32, (32, count), 1)
    return (spots >= spans_ref[0, :, 0:1]) & (spots < spans_ref[1, :, 0:1])


def three_parts(row):
    high = row.astype(BF16)
    rest = row - high.astype(F32)
    middle = rest.astype(BF16)
    low = (rest - middle.astype(F32)).astype(BF16)
    return jnp.concatenate([high, middle, low, jnp.zeros((13, row.shape[1]), BF16)], axis=0)


def permutation(transposed):
    moved = lax.broadcasted_iota(jnp.int32, (512, 1) if transposed else (1, 512), 0 if transposed else 1)
    natural = lax.broadcasted_iota(jnp.int32, (512, 512), 1 if transposed else 0)
    return jnp.where(natural == 4 * (moved % 128) + moved // 128, 1.0, 0.0).astype(BF16)


def forward_body(
    seg_ref, kv_hbm, qrow_hbm, sums_hbm, norms_hbm, o_hbm, op_hbm, log_hbm,
    spans_ref, bounds_ref, o_ref, kv_ref, qrow, kx, vrow, sums_ref, norms_ref, op_ref, log_ref, sems,
):
    first = (lax.axis_index("seq") // 2) * 1024
    loads = [
        pltpu.make_async_copy(source, target, sems.at[index])
        for index, (source, target) in enumerate(
            (
                (kv_hbm.at[:, :, 0:1024], kv_ref.at[:, :, 0:1024]),
                (kv_hbm.at[:, :, 2048:3072], kv_ref.at[:, :, 2048:3072]),
                (qrow_hbm, qrow),
                (norms_hbm, norms_ref),
                (sums_hbm, sums_ref),
            )
        )
    ]
    for load in loads:
        load.start()
    spans_and_bounds(seg_ref, first, spans_ref, bounds_ref)
    perm = permutation(False)
    for load in loads:
        load.wait()

    def outside(low, high, step, carry):
        carry = lax.fori_loop(low, jnp.minimum(high, 4), step, carry)
        return lax.fori_loop(jnp.maximum(low, 8), high, step, carry)

    def build(chunk, tops):
        lanes = pl.ds(pl.multiple_of(chunk * CHUNK, CHUNK), CHUNK)
        build_values(spans_ref, first - 1024 + chunk * CHUNK, kv_ref, lanes, kx, vrow, lanes)
        return tuple(
            jnp.maximum(tops[head], squares(kv_ref[0, pl.ds(head * HEAD_DIM, HEAD_DIM), lanes]))
            for head in range(2)
        )

    tops = outside(bounds_ref[0, 0], bounds_ref[3, 1], build, (norms_ref[2], norms_ref[3]))
    small = jnp.max(norms_ref[0]) * jnp.max(tops[0]) <= SAFE * SAFE
    small = small & (jnp.max(norms_ref[1]) * jnp.max(tops[1]) <= SAFE * SAFE)

    def write(head, rows, sums, top_row):
        out = sums.T
        total_row = out[80:81, :]
        o_ref[pl.ds(head * HEAD_DIM, HEAD_DIM), rows] = (out[:80] * (1.0 / total_row)).astype(BF16)
        log_ref[head : head + 1, rows] = top_row + jnp.log(total_row) * LOG2E

    def plain_step(tile, carry):
        rows = pl.ds(pl.multiple_of(tile * 256, 256), 256)

        def step(chunk, sums):
            lanes = pl.ds(pl.multiple_of(chunk * CHUNK, CHUNK), CHUNK)
            return forward_step(rows, [lanes], qrow, kx, vrow, sums)

        start = (sums_ref[0, rows, :], sums_ref[1, rows, :])
        sums = outside(bounds_ref[tile, 0], bounds_ref[tile, 1], step, start)
        for head in range(2):
            write(head, rows, sums[head], 0.0)
        return carry

    lane = lax.broadcasted_iota(jnp.int32, (256, 128), 1)

    def shifted_step(tile, carry):
        low, high = bounds_ref[tile, 0], bounds_ref[tile, 1]
        rows = pl.ds(pl.multiple_of(tile * 256, 256), 256)

        def score_step(chunk, tops):
            lanes = pl.ds(pl.multiple_of(chunk * CHUNK, CHUNK), CHUNK)
            found = []
            for head in range(2):
                part = dot_nn(qrow[head, rows, :], kx[head, :, lanes])
                found.append(jnp.maximum(tops[head], jnp.maximum(part[:, :128], part[:, 128:])))
            return tuple(found)

        start = jnp.full((256, 128), BIG, F32)
        tops = lax.fori_loop(low, high, score_step, (start, start))
        for head in range(2):
            shift = -jnp.max(tops[head], axis=1, keepdims=True)
            part_one = shift.astype(BF16).astype(F32)
            part_two = (shift - part_one).astype(BF16).astype(F32)
            part_three = shift - part_one - part_two
            moved = jnp.where(lane == 112, part_one, qrow[head, rows, :].astype(F32))
            moved = jnp.where(lane == 113, part_two, moved)
            qrow[head, rows, :] = jnp.where(lane == 114, part_three, moved).astype(BF16)

        def step(chunk, sums):
            lanes = pl.ds(pl.multiple_of(chunk * CHUNK, CHUNK), CHUNK)
            return forward_step(rows, [lanes], qrow, kx, vrow, sums)

        start = jnp.zeros((256, 128), F32)
        sums = lax.fori_loop(low, high, step, (start, start))
        for head in range(2):
            write(head, rows, sums[head], jnp.max(tops[head].T, axis=0, keepdims=True))
        return carry

    @pl.when(small)
    def _():
        lax.fori_loop(0, 4, plain_step, 0)

    @pl.when(jnp.logical_not(small))
    def _():
        middle = pltpu.make_async_copy(
            kv_hbm.at[:, :, 1024:2048], kv_ref.at[:, :, 1024:2048], sems.at[5]
        )
        middle.start()
        middle.wait()
        for chunk in range(4, 8):
            lanes = pl.ds(chunk * CHUNK, CHUNK)
            build_values(spans_ref, first - 1024 + chunk * CHUNK, kv_ref, lanes, kx, vrow, lanes)
        lax.fori_loop(0, 4, shifted_step, 0)

    keep_o = pltpu.make_async_copy(o_ref, o_hbm, sems.at[6])
    keep_log = pltpu.make_async_copy(log_ref, log_hbm, sems.at[7])
    keep_o.start()
    keep_log.start()
    for half in range(2):
        moved = dot_nn(o_ref[:, half * 512 : half * 512 + 512], perm).astype(BF16)
        for part in range(4):
            op_ref[half, part] = moved[:, part * 128 : part * 128 + 128]
    keep_op = pltpu.make_async_copy(op_ref, op_hbm, sems.at[8])
    keep_op.start()
    keep_o.wait()
    keep_log.wait()
    keep_op.wait()


def build_keys(spans_ref, position, kv_ref, lanes, kx, vx, krow, into):
    ones = jnp.where(lax.broadcasted_iota(jnp.int32, (16, CHUNK), 0) < 3, 1.0, 0.0).astype(BF16)
    hot = jnp.where(membership(spans_ref, position, CHUNK), 1.0, 0.0).astype(BF16)
    for head in range(2):
        feats = pl.ds(head * HEAD_DIM, HEAD_DIM)
        keys = jnp.concatenate([kv_ref[0, feats, lanes], hot, ones], axis=0)
        kx[head, :, into] = keys
        krow[head, into, :] = keys.T
        vx[head, :, into] = jnp.concatenate(
            [kv_ref[1, feats, lanes], ones, jnp.zeros((32, CHUNK), BF16)], axis=0
        )


def backward_step(rows, chunks, q_ref, g_ref, qrow, grow, kx, vx, krow, dk_acc, dv_acc, sums):
    pairs = [(head, lanes) for lanes in chunks for head in range(2)]
    feats = [pl.ds(head * HEAD_DIM, HEAD_DIM) for head in range(2)]
    probs = [jnp.exp2(dot_nn(qrow[head, rows, :], kx[head, :, lanes])) for head, lanes in pairs]
    shifted = [dot_nn(grow[head, rows, :], vx[head, :, lanes]) for head, lanes in pairs]
    dscores = [(prob * part).astype(BF16) for prob, part in zip(probs, shifted)]
    weights = [prob.astype(BF16) for prob in probs]
    dk = [dot_nn(q_ref[feats[head], rows], part) for (head, _), part in zip(pairs, dscores)]
    dv = [dot_nn(g_ref[feats[head], rows], part) for (head, _), part in zip(pairs, weights)]
    sums = list(sums)
    for (head, lanes), part in zip(pairs, dscores):
        sums[head] = sums[head] + dot_nn(part, krow[head, lanes, :])
    for (head, lanes), dk_part, dv_part in zip(pairs, dk, dv):
        dk_acc[head, :, lanes] += dk_part
        dv_acc[head, :, lanes] += dv_part
    return tuple(sums)


def backward_body(
    seg_ref, sizes_ref, receiver_ref, q_hbm, kv_hbm, o_hbm, log_hbm, gp_hbm,
    dq_hbm, dkv_hbm, starts_hbm, here_hbm, qrow_hbm, grow_hbm, gnat_hbm, spans_hbm,
    dq_ref, dkv_ref, starts_ref, here_ref, qrow, grow, gnat, spans_ref, bounds_ref, q_ref, kv_ref, o_ref, log_ref, gp_ref, kx, vx, krow, dk_acc, dv_acc, sems,
):
    seq = lax.axis_index("seq")
    first = (seq // 2) * 1024
    load_kv = pltpu.make_async_copy(kv_hbm.at[:, :, 0:1024], kv_ref.at[:, :, 0:1024], sems.at[0])
    load_kv_after = pltpu.make_async_copy(
        kv_hbm.at[:, :, 2048:3072], kv_ref.at[:, :, 2048:3072], sems.at[13]
    )
    load_o = pltpu.make_async_copy(o_hbm, o_ref, sems.at[1])
    load_q = pltpu.make_async_copy(q_hbm, q_ref, sems.at[2])
    load_o.start()
    load_q.start()
    load_log = pltpu.make_async_copy(log_hbm, log_ref, sems.at[3])
    load_log.start()
    load_gp = pltpu.make_async_copy(gp_hbm, gp_ref, sems.at[4])
    load_gp.start()
    load_kv.start()
    load_kv_after.start()
    spans_and_bounds(seg_ref, first, spans_ref, bounds_ref)
    start = jnp.int32(0)
    my_start, my_size = jnp.int32(0), jnp.int32(0)
    for batch in range(32):
        size, receiver = sizes_ref[batch], receiver_ref[batch]
        starts_ref[pl.ds(pl.multiple_of(receiver * 16, 16), 16), :] = jnp.full((16, 128), start)
        my_start = jnp.where(receiver == seq, start, my_start)
        my_size = jnp.where(receiver == seq, size, my_size)
        start = start + size
    here_ref[0:8, :] = jnp.full((8, 512), my_start)
    here_ref[8:16, :] = jnp.full((8, 512), my_size)
    back = permutation(True)
    load_gp.wait()
    for half in range(2):
        joined = jnp.concatenate([gp_ref[half, part] for part in range(4)], axis=1)
        gnat[:, half * 512 : half * 512 + 512] = dot_nn(joined, back).astype(BF16)
    load_kv.wait()
    load_kv_after.wait()
    load_o.wait()
    load_q.wait()
    load_log.wait()
    for head in range(2):
        feats = pl.ds(head * HEAD_DIM, HEAD_DIM)
        for block in range(4):
            lanes = pl.ds(block * 256, 256)
            inside = membership(spans_ref, first + block * 256, 256)
            joined = jnp.concatenate(
                [
                    q_ref[feats, lanes],
                    jnp.where(inside, 0.0, BIG).astype(BF16),
                    three_parts(-log_ref[head : head + 1, lanes]),
                ],
                axis=0,
            )
            qrow[head, lanes, :] = joined.T
            grads = gnat[feats, lanes]
            delta = jnp.sum(
                grads.astype(F32) * o_ref[feats, lanes].astype(F32), axis=0, keepdims=True
            )
            joined = jnp.concatenate(
                [grads, three_parts(-delta), jnp.zeros((32, 256), BF16)], axis=0
            )
            grow[head, lanes, :] = joined.T

    keeps = [
        pltpu.make_async_copy(source, target, sems.at[5 + index])
        for index, (source, target) in enumerate(
            (
                (starts_ref, starts_hbm), (here_ref, here_hbm), (spans_ref, spans_hbm),
                (gnat, gnat_hbm), (qrow, qrow_hbm), (grow, grow_hbm),
            )
        )
    ]
    for keep in keeps:
        keep.start()

    def outside(low, high, step, carry):
        carry = lax.fori_loop(low, jnp.minimum(high, 4), step, carry)
        return lax.fori_loop(jnp.maximum(low, 8), high, step, carry)

    def place_of(chunk):
        return pl.ds(pl.multiple_of(jnp.where(chunk < 4, chunk, chunk - 4) * CHUNK, CHUNK), CHUNK)

    def build(chunk, carry):
        lanes = pl.ds(pl.multiple_of(chunk * CHUNK, CHUNK), CHUNK)
        build_keys(
            spans_ref, first - 1024 + chunk * CHUNK, kv_ref, lanes, kx, vx, krow, place_of(chunk)
        )
        return carry

    outside(bounds_ref[0, 0], bounds_ref[3, 1], build, 0)
    dk_acc[...] = jnp.zeros_like(dk_acc)
    dv_acc[...] = jnp.zeros_like(dv_acc)

    def tile_step(tile, carry):
        rows = pl.ds(pl.multiple_of(tile * 256, 256), 256)

        def step(chunk, sums):
            return backward_step(
                rows, [place_of(chunk)], q_ref, gnat, qrow, grow, kx, vx, krow, dk_acc, dv_acc, sums
            )

        start = jnp.zeros((256, 128), F32)
        sums = outside(bounds_ref[tile, 0], bounds_ref[tile, 1], step, (start, start))
        for head in range(2):
            dq_ref[head, rows, :] = sums[head]
        return carry

    lax.fori_loop(0, 4, tile_step, 0)
    keeps.append(pltpu.make_async_copy(dq_ref, dq_hbm, sems.at[12]))
    keeps[-1].start()
    for head in range(2):
        feats = pl.ds(head * HEAD_DIM, HEAD_DIM)
        dkv_ref[0, feats, :] = (dk_acc[head] * LN2).astype(BF16)
        dkv_ref[1, feats, :] = dv_acc[head].astype(BF16)
    keeps.append(pltpu.make_async_copy(dkv_ref, dkv_hbm, sems.at[11]))
    keeps[-1].start()
    for keep in keeps:
        keep.wait()


def middle_body(
    op_ref, w_hbm, w_out_hbm, tokens_hbm, mgrad_hbm, gain_hbm,
    gp_ref, gl_hbm, glt_hbm, own_ref, table_ref,
    w_ref, tokens_ref, mgrad_ref, gain_ref, gl_ref, glt_ref, att, gat, packed, send, recv,
):
    section, chip, core = place()
    copies = Copies(send, recv)
    peers = row_peers(section, chip, core) + core_peers(section, chip, core)
    greet(peers)
    columns = pl.ds(pl.multiple_of(section * 1280, 128), 1280)
    load_gain = copies.start(gain_hbm, gain_ref, None)
    load_mgrad = copies.start(mgrad_hbm.at[:, columns], mgrad_ref, None)
    load_tokens = copies.start(tokens_hbm, tokens_ref, None)
    loads = []
    for step in range(4):
        w_rows = pl.ds(pl.multiple_of((section + step) % 4 * 320, 16), 320)
        source = w_hbm.at[w_rows, :] if step else w_out_hbm
        loads.append(copies.start(source, w_ref.at[w_rows, :], None))
    greeted(peers)
    rows = pl.ds(pl.multiple_of((section * 2 + core) * PAIR, 16), PAIR)
    waits = []
    for step in (2, 1, 3, 0):
        for turn in range(2):
            to_section, to_core = (section + step) % 4, (core + turn) % 2
            device = dev(chip, to_core, to_section) if step or turn else None
            waits.append(copies.start(op_ref.at[to_core, to_section], att.at[rows, :], device))
    late = [copies.start(op_ref.at[1 - core], own_ref, dev(chip, 1 - core, section))]
    row = lax.broadcasted_iota(jnp.int32, (128, 512), 0)
    column = lax.broadcasted_iota(jnp.int32, (128, 512), 1)
    chosen = jnp.where(column == 4 * row + section, 1.0, 0.0).astype(BF16)
    load_tokens.wait()
    load_gain.wait()
    load_mgrad.wait()
    values = dot_nn(chosen, tokens_ref[...])
    gain = gain_ref[...].reshape(1, 1280).astype(F32)
    scaled = mgrad_ref[...].astype(F32) * gain
    scaled_mean = jnp.mean(scaled, axis=1, keepdims=True)
    row = lax.broadcasted_iota(jnp.int32, (128, 128), 0)
    column = lax.broadcasted_iota(jnp.int32, (128, 128), 1)
    order = jnp.where(column == 16 * (row % 8) + row // 8, 1.0, 0.0).astype(BF16)
    wait_all(loads)
    wait_all(waits)
    layer = values + dot_nn(att[...].T, w_ref[...])
    centered = layer - jnp.mean(layer, axis=1, keepdims=True)
    inv = lax.rsqrt(jnp.mean(centered * centered, axis=1, keepdims=True) + EPS)
    unit = centered * inv
    grad_layer = inv * (
        scaled - scaled_mean - unit * jnp.mean(scaled * unit, axis=1, keepdims=True)
    )
    grad_layer = grad_layer.astype(BF16)
    gat[...] = dot_nt(w_ref[...], grad_layer).astype(BF16)
    for step in (2, 1, 3, 0):
        for turn in range(2):
            to_section, to_core = (section + step) % 4, (core + turn) % 2
            device = dev(chip, to_core, to_section) if step or turn else None
            rows = pl.ds(pl.multiple_of((to_section * 2 + to_core) * PAIR, 16), PAIR)
            late.append(copies.start(gat.at[rows, :], gp_ref.at[core, section], device))
    moved = dot_nn(order, (unit * gain).astype(BF16))
    for chip_to in range(16):
        eight = moved[chip_to * 8 : chip_to * 8 + 8]
        packed[chip_to] = jnp.concatenate([eight[:, :640], eight[:, 640:]], axis=0).astype(BF16)
    for step in range(16):
        to_chip = (chip + step) % 16
        device = dev(to_chip, core, section) if step else None
        late.append(copies.start(packed.at[to_chip], table_ref.at[chip], device))
    gl_ref[...] = grad_layer
    glt_ref[...] = grad_layer.T
    late.append(copies.start(gl_ref, gl_hbm, None))
    late.append(copies.start(glt_ref, glt_hbm, None))
    wait_all(late)


def tail_body(
    dkv_ref, starts_hbm, live_hbm, dq_hbm, qrow_hbm, grow_hbm, gnat_hbm, spans_hbm, q_hbm, kv_hbm,
    glt_hbm, op_hbm, own_hbm, table_hbm, gl_hbm, tokens_hbm, gain_hbm, w_hbm, normed_t_hbm,
    delivered_hbm, gx_all, weights_ref,
    starts_ref, live_ref, qrow, grow, gnat, spans_ref, gain_ref, delivered_ref,
    table_ref, gl_ref, tokens_ref, w_ref, normed_t_ref,
    q_ref, kv_ref, kx, vx, krow, dk_acc, dv_acc, dq_acc, own_out, mate_in,
    dkv_in, dj, rows_ref, gn, relay_in, gn_in, gx_own, att, glt,
    parcels, arrived, p_mine, p_away, p_in,
    summed, stage_in, subtotal, late_in, total, send, recv,
):
    section, chip, core = place()
    y, z = chip // 4, chip % 4
    ahead, behind, far = (section + 1) % 4, (section + 3) % 4, (section + 2) % 4
    ahead_dev, behind_dev = dev(chip, core, ahead), dev(chip, core, behind)
    copies = Copies(send, recv)
    mate = dev(chip, 1 - core, section)
    peers = plane_peers(section, chip, core) + section_peers(section, chip, core)
    greet(peers)
    early = [
        copies.start(source, target, None)
        for source, target in (
            (spans_hbm, spans_ref), (kv_hbm.at[:, :, 1024:2048], kv_ref), (q_hbm, q_ref),
            (qrow_hbm, qrow), (grow_hbm, grow), (gnat_hbm, gnat), (dq_hbm, dq_acc),
        )
    ]
    greeted(peers)
    back, mates = [], []
    for half in range(2):
        waits = []
        for step, base, slot in ((-1, 0, 0), (1, 1024, 1)):
            for target in (core, 1 - core):
                lanes = pl.ds(pl.multiple_of(base + target * 512 + half * 256, 256), 256)
                device = dev(around(chip, step), target, section)
                waits.append(
                    copies.start(dkv_ref.at[:, :, lanes], dkv_in.at[half, slot, core], device)
                )
        back.append(waits)

    def glt_part(owner, start, count):
        lanes = pl.ds(pl.multiple_of(owner * 128, 128), 128)
        return glt.at[start : start + count, lanes]

    mine = glt_part(section, 0, 1280)
    glt_ahead = copies.start(glt_hbm, mine, ahead_dev)
    glt_behind = copies.start(glt_hbm, mine, behind_dev)
    gathered = [copies.start(glt_hbm, mine, None)]
    load_table = [
        copies.start(table_hbm, table_ref, None), copies.start(starts_hbm, starts_ref, None)
    ]
    load_w = copies.start(w_hbm, w_ref, None)
    loads = [
        copies.start(source, target, None)
        for source, target in (
            (normed_t_hbm, normed_t_ref), (tokens_hbm, tokens_ref), (gl_hbm, gl_ref),
            (gain_hbm, gain_ref), (live_hbm, live_ref),
        )
    ]
    for near, of_core in ((True, core), (False, 1 - core)):
        rows = pl.ds(pl.multiple_of(of_core * PAIR, 16), PAIR)
        for part in range(4):
            source = op_hbm.at[core, part] if near else own_hbm.at[part]
            loads.append(copies.start(source, att.at[rows, part * 128 : part * 128 + 128], None))

    wait_all(early)
    for chunk in range(4):
        lanes = pl.ds(chunk * CHUNK, CHUNK)
        build_keys(
            spans_ref, chip * 1024 + chunk * CHUNK, kv_ref, lanes, kx, vx, krow, lanes
        )
    dk_acc[...] = jnp.zeros_like(dk_acc)
    dv_acc[...] = jnp.zeros_like(dv_acc)

    def own_step(tile, group):
        rows = pl.ds(pl.multiple_of(tile * 256, 256), 256)
        chunks = [pl.ds((group + 2 * which) * CHUNK, CHUNK) for which in range(2)]
        sums = backward_step(
            rows, chunks, q_ref, gnat, qrow, grow, kx, vx, krow, dk_acc, dv_acc,
            (dq_acc[0, rows, :], dq_acc[1, rows, :]),
        )
        for head in range(2):
            dq_acc[head, rows, :] = sums[head]

    def finish_own(half):
        for of_core in range(2):
            lanes = pl.ds(of_core * 512 + half * 256, 256)
            for head in range(2):
                feats = pl.ds(head * HEAD_DIM, HEAD_DIM)
                part = dq_acc[head, lanes, :].T[:80] * FACTOR
                own_out[half, of_core, 0, feats, :] = part.astype(BF16)
                own_out[half, of_core, 1, feats, :] = (dk_acc[head, :, lanes] * LN2).astype(BF16)
                own_out[half, of_core, 2, feats, :] = dv_acc[head, :, lanes].astype(BF16)
        mates.append(copies.start(own_out.at[half, 1 - core], mate_in.at[half], mate))

    def first_step(tile, carry):
        own_step(tile, 0)
        return carry

    def even_step(index, carry):
        own_step(index * 2, 1)
        return carry

    def odd_step(index, carry):
        own_step(index * 2 + 1, 1)
        return carry

    lax.fori_loop(0, 4, first_step, 0)
    lax.fori_loop(0, 2, even_step, 0)
    finish_own(0)
    glt_ahead.wait()
    there = glt_part(behind, 0, 640)
    gathered.append(copies.start(there, there, ahead_dev))
    glt_behind.wait()
    there = glt_part(ahead, 640, 640)
    gathered.append(copies.start(there, there, behind_dev))
    lax.fori_loop(0, 2, odd_step, 0)
    finish_own(1)

    row = lax.broadcasted_iota(jnp.int32, (256, 256), 0)
    column = lax.broadcasted_iota(jnp.int32, (256, 256), 1)
    by_part = jnp.where(column == 4 * (row % 64) + row // 64, 1.0, 0.0).astype(BF16)
    load_w.wait()

    def collect(half, kinds):
        lanes = pl.ds(half * 256, 256)
        for near, head in ((True, core), (False, 1 - core)):
            for which in kinds:
                grad = own_out[half, core, which] if near else mate_in[half, which]
                if which:
                    grad = grad.astype(F32) + dkv_in[half, 0, head, which - 1].astype(F32)
                    grad = (grad + dkv_in[half, 1, head, which - 1].astype(F32)).astype(BF16)
                dj[pl.ds(pl.multiple_of(320 * which + head * PAIR, 16), PAIR), lanes] = grad

    sums = []

    def send_first(half):
        rows_ref[...] = dot_nt(by_part, dj[:, half * 256 : half * 256 + 256]).astype(BF16)
        grad = dot_nn(rows_ref[...], w_ref[...].reshape(960, 1280))
        gn[half] = grad.astype(BF16).reshape(4, 64, 1280)
        relays = [
            copies.start(gn.at[half, far, 0:32], relay_in.at[half, 0], behind_dev),
            copies.start(gn.at[half, far, 32:64], relay_in.at[half, 1], ahead_dev),
        ]
        sums.append([
            copies.start(gn.at[half, behind, 32:64], gn_in.at[half, 0, 32:64], behind_dev),
            copies.start(gn.at[half, ahead, 0:32], gn_in.at[half, 1, 0:32], ahead_dev),
        ])
        return relays

    def send_second(half, relays):
        relays[0].wait()
        grad = gn[half, behind, 0:32].astype(F32) + relay_in[half, 0].astype(F32)
        gn[half, behind, 0:32] = grad.astype(BF16)
        source = gn.at[half, behind, 0:32]
        sums[half].append(copies.start(source, gn_in.at[half, 0, 0:32], behind_dev))
        relays[1].wait()
        grad = gn[half, ahead, 32:64].astype(F32) + relay_in[half, 1].astype(F32)
        gn[half, ahead, 32:64] = grad.astype(BF16)
        source = gn.at[half, ahead, 32:64]
        sums[half].append(copies.start(source, gn_in.at[half, 1, 32:64], ahead_dev))

    def products(index, core_of, group):
        rows = pl.ds(index * 320, 320)
        if group == 0 and core_of == 1:
            return dot_nt(glt[rows, :], att[...])
        which = 0 if group == 0 else 1 + core_of
        return dot_nt(normed_t_ref[rows, :], dj[320 * which : 320 * which + 320, :])

    def send_products(group):
        pairs = []
        for index in range(4):
            for core_of in range(2):
                @pl.when(core != core_of)
                def _():
                    part = products(index, core_of, group)
                    p_away[group, index] = part.astype(BF16).reshape(4, 80, 320)

            pairs.append(copies.start(p_away.at[group, index], p_in.at[group, index], mate))
        for index in range(4):
            for core_of in range(2):
                @pl.when(core == core_of)
                def _():
                    p_mine[index] = products(index, core_of, group).reshape(4, 80, 320)

        return pairs

    def first_stage(group, pairs):
        for index in range(4):
            pairs[index].wait()
            grad = p_mine[index] + p_in[group, index].astype(F32)
            summed[group, index] = grad.astype(BF16)
        waits = []
        for step in (2, 1, 3):
            to_z, to_y = (z + step) % 4, (y + step) % 4
            if group == 0:
                source, device = summed.at[group, to_y], dev(to_y * 4 + z, core, section)
            else:
                source, device = summed.at[group, :, to_z], dev(y * 4 + to_z, core, section)
            waits.append(copies.start(source, stage_in.at[group, step - 1], device))
        return waits

    def second_stage(group, waits):
        wait_all(waits)
        for index in range(4):
            grad = (summed[group, y, index] if group == 0 else summed[group, index, z]).astype(F32)
            for step in range(3):
                grad = grad + stage_in[group, step, index].astype(F32)
            subtotal[group, index] = grad.astype(BF16)
        waits = []
        for step in (2, 1, 3):
            to_z, to_y = (z + step) % 4, (y + step) % 4
            place_to = to_z if group == 0 else to_y
            device = dev(y * 4 + to_z if group == 0 else to_y * 4 + z, core, section)
            waits.append(
                copies.start(subtotal.at[group, place_to], late_in.at[group, step - 1], device)
            )
        return waits

    def last_stage(group, waits):
        wait_all(waits)
        grad = subtotal[group, z if group == 0 else y].astype(F32)
        for step in range(3):
            grad = grad + late_in[group, step].astype(F32)
        total[group] = grad
        found = []
        for target, device in ((1 - core, mate), (core, None)):
            rows = pl.ds(pl.multiple_of(target * 40, 8), 40)
            found.append(
                copies.start(total.at[group, rows, :], weights_ref.at[core, group], device)
            )
        return found

    gathers, forwards = [], []

    def finish_norm(half):
        row = lax.broadcasted_iota(jnp.int32, (64, 256), 0)
        column = lax.broadcasted_iota(jnp.int32, (64, 256), 1)
        chosen = jnp.where(column == 4 * row + section, 1.0, 0.0).astype(BF16)
        values = dot_nn(chosen, tokens_ref[half * 256 : half * 256 + 256, :])
        centered = values - jnp.mean(values, axis=1, keepdims=True)
        inv = lax.rsqrt(jnp.mean(centered * centered, axis=1, keepdims=True) + EPS)
        unit = centered * inv
        wait_all(sums[half])
        grad = gn[half, section].astype(F32) + gn_in[half, 0].astype(F32)
        grad = grad + gn_in[half, 1].astype(F32)
        scaled = grad * gain_ref[...].reshape(1, 1280).astype(F32)
        grad = inv * (
            scaled
            - jnp.mean(scaled, axis=1, keepdims=True)
            - unit * jnp.mean(scaled * unit, axis=1, keepdims=True)
        )
        grad = grad + gl_ref[half * 64 : half * 64 + 64, :].astype(F32)
        gx_own[half] = grad.astype(BF16)
        target = gx_all.at[half, section]
        gathers.append([copies.start(gx_own.at[half], target, ahead_dev)])
        gathers[half].append(copies.start(gx_own.at[half], target, behind_dev))
        forwards.append(copies.start(gx_own.at[half], target, None))

    def forward(half):
        gathers[half][0].wait()
        there = gx_all.at[half, behind, 0:32]
        forwards.append(copies.start(there, there, ahead_dev))
        gathers[half][1].wait()
        there = gx_all.at[half, ahead, 32:64]
        forwards.append(copies.start(there, there, behind_dev))

    wait_all(back[0])
    mates[0].wait()
    collect(0, (0, 1, 2))
    relays_a = send_first(0)

    wait_all(load_table)
    begin = starts_ref[:, 0:1]
    block, offset = begin // 128, begin % 128
    first = 8 * ((block + 1 - core) // 2)
    first = first + jnp.where(block % 2 == core, (offset - chip + 15) // 16, 0)
    out_row = lax.broadcasted_iota(jnp.int32, (512, 256), 0)
    in_row = lax.broadcasted_iota(jnp.int32, (512, 256), 1)
    wanted = first + out_row % 8
    wanted = (wanted // 8) * 16 + wanted % 8 + 8 * ((out_row // 8) % 2)
    hot = jnp.where(in_row == wanted, 1.0, 0.0).astype(BF16)
    table = table_ref[...].reshape(256, 640)
    parcels[...] = dot_nn(hot, table).astype(BF16).reshape(32, 16, 640)

    wait_all(loads)
    wait_all(gathered)
    mates[1].wait()
    collect(1, (0,))
    pairs = send_products(0)
    wait_all(back[1])
    collect(1, (1, 2))
    relays_b = send_first(1)
    deliveries = []
    for step in range(16):
        for turn in range(2):
            to_chip, to_core = (chip + step) % 16, (core + turn) % 2
            device = dev(to_chip, to_core, section) if step or turn else None
            deliveries.append(
                copies.start(parcels.at[to_chip * 2 + to_core], arrived.at[chip * 2 + core], device)
            )
    send_second(0, relays_a)
    stage_y = first_stage(0, pairs)
    pairs = send_products(1)
    stage_z = first_stage(1, pairs)
    send_second(1, relays_b)
    finish_norm(0)
    finish_norm(1)
    forward(0)
    later_z = second_stage(0, stage_y)
    forward(1)

    lane = lax.broadcasted_iota(jnp.int32, (1, 512), 1)
    from_chip, from_core, side, number = lane // 32, (lane // 16) % 2, (lane // 8) % 2, lane % 8
    begin, live = live_ref[0:1, :], live_ref[8:9, :]
    block, offset = begin // 128, begin % 128
    spot = 8 * ((block + 1 - from_core) // 2) + number
    spot = spot + jnp.where(block % 2 == from_core, (offset - from_chip + 15) // 16, 0)
    slot = (2 * (spot // 8) + from_core) * 128 + 16 * (spot % 8) + from_chip - begin
    out_row = lax.broadcasted_iota(jnp.int32, (256, 512), 0)
    taken = (out_row == slot) & (out_row < live)
    wait_all(deliveries)
    rows = arrived[...].reshape(512, 640)
    for which in range(2):
        hot = jnp.where(taken & (side == which), 1.0, 0.0).astype(BF16)
        delivered_ref[:, which * 640 : which * 640 + 640] = dot_nn(hot, rows).astype(BF16)
    lasts = [copies.start(delivered_ref, delivered_hbm, None)]

    later_y = second_stage(1, stage_z)
    lasts += last_stage(0, later_z)
    lasts += last_stage(1, later_y)
    wait_all(lasts)
    wait_all(forwards)


def results_body(
    gx_hbm, both_hbm, arrived_hbm, gx_out, w_qkv_out, w_out_out, delivered_out,
    gx_in, gx_ref, both_ref, delivered_ref, sems,
):
    loads = [
        pltpu.make_async_copy(source, target, sems.at[index])
        for index, (source, target) in enumerate(
            (
                (gx_hbm.at[0], gx_in.at[0]), (gx_hbm.at[1], gx_in.at[1]),
                (both_hbm, both_ref), (arrived_hbm, delivered_ref),
            )
        )
    ]
    for load in loads:
        load.start()
    row = lax.broadcasted_iota(jnp.int32, (256, 256), 0)
    column = lax.broadcasted_iota(jnp.int32, (256, 256), 1)
    natural = jnp.where(row == 4 * (column % 64) + column // 64, 1.0, 0.0).astype(BF16)
    stores = []

    def store(source, target):
        stores.append(pltpu.make_async_copy(source, target, sems.at[4 + len(stores)]))
        stores[-1].start()

    for half in range(2):
        loads[half].wait()
        rows = gx_in[half].reshape(256, 1280)
        gx_ref[half] = dot_nn(natural, rows).astype(BF16)
        store(gx_ref.at[half], gx_out.at[half * 256 : half * 256 + 256, :])
    loads[2].wait()
    store(both_ref.at[0], w_qkv_out.at[0:2])
    store(both_ref.at[1, 1], w_qkv_out.at[2])
    store(both_ref.at[1, 0], w_out_out)
    loads[3].wait()
    store(delivered_ref, delivered_out)
    for copy in stores:
        copy.wait()


def halo_peers(section, chip, core):
    found = [dev(chip, 1 - core, section)]
    for step in (1, -1):
        for other in (core, 1 - core):
            found.append(dev(around(chip, step), other, section))
    return found


def row_peers(section, chip, core):
    found = []
    for step in range(4):
        for turn in range(2):
            if step or turn:
                found.append(dev(chip, (core + turn) % 2, (section + step) % 4))
    return found


def section_peers(section, chip, core):
    return [dev(chip, core, (section + step) % 4) for step in range(1, 4)]


def core_peers(section, chip, core):
    return [dev((chip + step) % 16, core, section) for step in range(1, 16)]


def plane_peers(section, chip, core):
    found = [dev(chip, 1 - core, section)]
    for step in range(1, 16):
        for turn in range(2):
            found.append(dev((chip + step) % 16, (core + turn) % 2, section))
    return found


def local(
    tokens, norm_gain, w_qkv, w_out, merge_gain, seg_blocks, mb_sizes, mb_receiver, merged_grad
):
    w_rows = w_qkv.transpose(0, 2, 1)
    q, kv, normed_t, w_full, q_rows, sums, norms = call(
        project_body,
        [
            (HBM, shape((PAIR, 1024))),
            (HBM, shape((2, PAIR, 3072))),
            (HBM, shape((1280, 512))),
            (HBM, shape((1280, 1280))),
            (HBM, shape((2, 1024, 128))),
            (HBM, shape((2, 1024, 128), F32)),
            (HBM, shape((4, 8, 128), F32)),
        ],
        [(SMEM, seg_blocks), (HBM, tokens), (HBM, norm_gain), (HBM, w_rows), (HBM, w_out)],
        [
            pltpu.VMEM((512, 1280), BF16),
            pltpu.VMEM((1280,), BF16),
            pltpu.VMEM((3, 320, 1280), BF16),
            pltpu.VMEM((1280, 512), BF16),
            pltpu.VMEM((3, 320, 512), BF16),
            pltpu.VMEM((PAIR, 1024), BF16),
            pltpu.VMEM((2, PAIR, 1024), BF16),
            pltpu.VMEM((2, 32, 128), jnp.int32),
            pltpu.VMEM((2, 1024, 128), BF16),
            pltpu.VMEM((2, 128, 1024), BF16),
            pltpu.VMEM((2, 1024, 128), BF16),
            pltpu.VMEM((2, 1024, 128), F32),
            pltpu.VMEM((4, 8, 128), F32),
        ],
        copies=40,
        number=1,
        limit=62,
    )
    o, op, log_total = call(
        forward_body,
        [
            (HBM, shape((PAIR, 1024))),
            (HBM, shape((2, 4, PAIR, 128))),
            (HBM, shape((2, 1024), F32)),
        ],
        [(SMEM, seg_blocks), (HBM, kv), (HBM, q_rows), (HBM, sums), (HBM, norms)],
        [
            pltpu.VMEM((2, 32, 128), jnp.int32),
            pltpu.SMEM((4, 2), jnp.int32),
            pltpu.VMEM((PAIR, 1024), BF16),
            pltpu.VMEM((2, PAIR, 3072), BF16),
            pltpu.VMEM((2, 1024, 128), BF16),
            pltpu.VMEM((2, 128, 3072), BF16),
            pltpu.VMEM((2, 3072, 128), BF16),
            pltpu.VMEM((2, 1024, 128), F32),
            pltpu.VMEM((4, 8, 128), F32),
            pltpu.VMEM((2, 4, PAIR, 128), BF16),
            pltpu.VMEM((2, 1024), F32),
        ],
        copies=9,
        limit=62,
    )
    gp, grad_layer, glt, att_own, table = call(
        middle_body,
        [
            (HBM, shape((2, 4, PAIR, 128))),
            (HBM, shape((128, 1280))),
            (HBM, shape((1280, 128))),
            (HBM, shape((4, PAIR, 128))),
            (HBM, shape((16, 16, 640))),
        ],
        [(HBM, op), (HBM, w_full), (HBM, w_out), (HBM, tokens), (HBM, merged_grad), (HBM, merge_gain)],
        [
            pltpu.VMEM((1280, 1280), BF16),
            pltpu.VMEM((512, 1280), BF16),
            pltpu.VMEM((128, 1280), BF16),
            pltpu.VMEM((1280,), BF16),
            pltpu.VMEM((128, 1280), BF16),
            pltpu.VMEM((1280, 128), BF16),
            pltpu.VMEM((1280, 128), BF16),
            pltpu.VMEM((1280, 128), BF16),
            pltpu.VMEM((16, 16, 640), BF16),
        ],
        copies=44,
        number=2,
        limit=62,
    )
    dq, dkv, start_rows, here, qrow, grow, gnat, spans = call(
        backward_body,
        [
            (HBM, shape((2, 1024, 128), F32)),
            (HBM, shape((2, PAIR, 2048))),
            (HBM, shape((512, 128), jnp.int32)),
            (HBM, shape((16, 512), jnp.int32)),
            (HBM, shape((2, 1024, 128))),
            (HBM, shape((2, 1024, 128))),
            (HBM, shape((PAIR, 1024))),
            (HBM, shape((2, 32, 128), jnp.int32)),
        ],
        [
            (SMEM, seg_blocks), (SMEM, mb_sizes), (SMEM, mb_receiver),
            (HBM, q), (HBM, kv), (HBM, o), (HBM, log_total), (HBM, gp),
        ],
        [
            pltpu.VMEM((2, 1024, 128), F32),
            pltpu.VMEM((2, PAIR, 2048), BF16),
            pltpu.VMEM((512, 128), jnp.int32),
            pltpu.VMEM((16, 512), jnp.int32),
            pltpu.VMEM((2, 1024, 128), BF16),
            pltpu.VMEM((2, 1024, 128), BF16),
            pltpu.VMEM((PAIR, 1024), BF16),
            pltpu.VMEM((2, 32, 128), jnp.int32),
            pltpu.SMEM((4, 2), jnp.int32),
            pltpu.VMEM((PAIR, 1024), BF16),
            pltpu.VMEM((2, PAIR, 3072), BF16),
            pltpu.VMEM((PAIR, 1024), BF16),
            pltpu.VMEM((2, 1024), F32),
            pltpu.VMEM((2, 4, PAIR, 128), BF16),
            pltpu.VMEM((2, 128, 2048), BF16),
            pltpu.VMEM((2, 128, 2048), BF16),
            pltpu.VMEM((2, 2048, 128), BF16),
            pltpu.VMEM((2, HEAD_DIM, 2048), F32),
            pltpu.VMEM((2, HEAD_DIM, 2048), F32),
        ],
        copies=14,
        limit=62,
    )
    arrived, gx_all, weights = call(
        tail_body,
        [
            (HBM, shape((256, 1280))),
            (HBM, shape((2, 4, 64, 1280))),
            (HBM, shape((2, 2, 40, 320), F32)),
        ],
        [
            (HBM, dkv), (HBM, start_rows), (HBM, here), (HBM, dq), (HBM, qrow), (HBM, grow),
            (HBM, gnat), (HBM, spans), (HBM, q), (HBM, kv), (HBM, glt), (HBM, op), (HBM, att_own),
            (HBM, table), (HBM, grad_layer), (HBM, tokens), (HBM, norm_gain), (HBM, w_rows),
            (HBM, normed_t),
        ],
        [
            pltpu.VMEM((512, 128), jnp.int32),
            pltpu.VMEM((16, 512), jnp.int32),
            pltpu.VMEM((2, 1024, 128), BF16),
            pltpu.VMEM((2, 1024, 128), BF16),
            pltpu.VMEM((PAIR, 1024), BF16),
            pltpu.VMEM((2, 32, 128), jnp.int32),
            pltpu.VMEM((1280,), BF16),
            pltpu.VMEM((256, 1280), BF16),
            pltpu.VMEM((16, 16, 640), BF16),
            pltpu.VMEM((128, 1280), BF16),
            pltpu.VMEM((512, 1280), BF16),
            pltpu.VMEM((3, 320, 1280), BF16),
            pltpu.VMEM((1280, 512), BF16),
            pltpu.VMEM((PAIR, 1024), BF16),
            pltpu.VMEM((2, PAIR, 1024), BF16),
            pltpu.VMEM((2, 128, 1024), BF16),
            pltpu.VMEM((2, 128, 1024), BF16),
            pltpu.VMEM((2, 1024, 128), BF16),
            pltpu.VMEM((2, HEAD_DIM, 1024), F32),
            pltpu.VMEM((2, HEAD_DIM, 1024), F32),
            pltpu.VMEM((2, 1024, 128), F32),
            pltpu.VMEM((2, 2, 3, PAIR, 256), BF16),
            pltpu.VMEM((2, 3, PAIR, 256), BF16),
            pltpu.VMEM((2, 2, 2, 2, PAIR, 256), BF16),
            pltpu.VMEM((960, 512), BF16),
            pltpu.VMEM((256, 960), BF16),
            pltpu.VMEM((2, 4, 64, 1280), BF16),
            pltpu.VMEM((2, 2, 32, 1280), BF16),
            pltpu.VMEM((2, 2, 64, 1280), BF16),
            pltpu.VMEM((2, 64, 1280), BF16),
            pltpu.VMEM((320, 512), BF16),
            pltpu.VMEM((1280, 512), BF16),
            pltpu.VMEM((32, 16, 640), BF16),
            pltpu.VMEM((32, 16, 640), BF16),
            pltpu.VMEM((4, 4, 80, 320), F32),
            pltpu.VMEM((2, 4, 4, 80, 320), BF16),
            pltpu.VMEM((2, 4, 4, 80, 320), BF16),
            pltpu.VMEM((2, 4, 4, 80, 320), BF16),
            pltpu.VMEM((2, 3, 4, 80, 320), BF16),
            pltpu.VMEM((2, 4, 80, 320), BF16),
            pltpu.VMEM((2, 3, 80, 320), BF16),
            pltpu.VMEM((2, 80, 320), F32),
        ],
        copies=124,
        number=3,
        limit=62,
    )
    grad_x, grad_w_qkv, grad_w_out, delivered = call(
        results_body,
        [
            (HBM, shape((512, 1280))),
            (HBM, shape((3, 40, 320), F32)),
            (HBM, shape((40, 320), F32)),
            (HBM, shape((256, 1280))),
        ],
        [(HBM, gx_all), (HBM, weights), (HBM, arrived)],
        [
            pltpu.VMEM((2, 4, 64, 1280), BF16),
            pltpu.VMEM((2, 256, 1280), BF16),
            pltpu.VMEM((2, 2, 40, 320), F32),
            pltpu.VMEM((256, 1280), BF16),
        ],
        copies=10,
        limit=62,
    )
    return (delivered, grad_x, grad_w_qkv, grad_w_out.T)


def solution(mesh):
    placed = (
        P("seq", None),
        P(),
        P(None, None, "section"),
        P("section", None),
        P(),
        P(),
        P(),
        P(),
        P("seq", None),
    )
    return jax.shard_map(
        local,
        mesh=mesh,
        in_specs=placed,
        out_specs=(
            P("seq", "section"),
            P("seq", None),
            P(None, "seq", "section"),
            P("section", "seq"),
        ),
        check_vma=False,
    )
```
